256 devices in a mesh: attn: 8 (over z_lo, core), ffn: 16 (over x, y), rep: 2 (over z_hi).
Axes of the slice: x: 4, y: 4, z: 8 (z_hi: 2, z_lo: 4; z = z_hi * 4 + z_lo), core: 2. Of those that a mesh axis runs over, the one named last changes fastest.
Arguments:
- hidden_in: bfloat16 [3, 256, 7168], P(None, 'rep', 'attn'), parts along dimension 1, may hold values from -18 to 18
- queries: bfloat16 [3, 256, 16384], P(None, ('rep', 'attn', 'ffn')), parts along dimension 1, may hold values from -128 to 128
- key_cache: bfloat16 [768, 1024, 256], P(('rep', 'attn', 'ffn')), parts along dimension 0, may hold values from -6 to 6
- value_cache: bfloat16 [768, 1024, 256], P(('rep', 'attn', 'ffn')), parts along dimension 0, may hold values from -6 to 6
- lengths: int32 [3, 256], P(None, ('rep', 'attn', 'ffn')), parts along dimension 1, may hold values from 256 to 1024, as said below
- cache_slot: int32 [3, 256], P(None, ('rep', 'attn', 'ffn')), parts along dimension 1, may hold values from 0 to 2, as said below
- out_weight: bfloat16 [16384, 7168], P('ffn', 'attn'), may hold values from -0.046875 to 0.046875
- ffn_gain: bfloat16 [7168], P('attn'), may hold values from 0.099609375 to 1.8984375
- gate_weight: bfloat16 [7168, 18432], P('attn', 'ffn'), may hold values from -0.0625 to 0.0625
- up_weight: bfloat16 [7168, 18432], P('attn', 'ffn'), may hold values from -0.0625 to 0.0625
- down_weight: bfloat16 [18432, 7168], P('ffn', 'attn'), may hold values from -0.046875 to 0.046875
Outputs:
- hidden_out: bfloat16 [3, 256, 7168], P(None, ('rep', 'attn', 'ffn')), parts along dimension 1
The draws below stay inside these ranges and needn't reach their ends.
There are 2 independent parts, one for each index of `rep`. The reference program is written for one: setup_inputs(seed, part) draws one part's arguments, and reference() takes and returns one part's arrays. A program takes and returns all parts, laid end to end along the dimension named above; an argument that names none is the same for every part. Nothing has to cross between parts.
Inputs may be any that keep to these rules, and one draw needn't show every extreme that they name: Each request reads positions 0 to lengths - 1 of its slot; request 0 of every micro-batch has a full cache of 1024 positions. `cache_slot`: the requests of one device, over all micro-batches, occupy distinct slots of that device.
All inputs are finite; a program needn't handle non-finite values.
Results may differ from the reference program's by a relative error of at most 0.013.
Values may be sent and summed in bfloat16 or wider, within the bound.
No kernel may reach another device: no remote copies, remote signals or barrier semaphores. Data moves between devices by JAX's collectives and lax.ppermute only.
A program may use at most 64 MiB of HBM per device.

```python
import jax
import jax.numpy as jnp
from jax import lax

D = 7168
FF = 18432
HEADS = 64
HEAD_DIM = 256
CACHE_LEN = 1024
ROWS_DEV = 1
MICRO = 3
SLOTS_DEV = 3
ROWS = 128
SLOTS = 384


def slot_table(key):
    key = jax.random.fold_in(key, 21)
    owners = ROWS // ROWS_DEV
    key_list = jax.random.split(key, owners)
    permuted = jax.vmap(lambda single: jax.random.permutation(single, SLOTS_DEV))(key_list)
    permuted = permuted.reshape(owners, MICRO, ROWS_DEV).transpose(1, 0, 2).reshape(MICRO, ROWS)
    return permuted.astype(jnp.int32)


def cache_keys(key):
    key = jax.random.fold_in(key, 31)
    drawn = jnp.clip(jax.random.normal(key, (SLOTS, CACHE_LEN, HEAD_DIM), jnp.float32), -6.0, 6.0)
    drawn = drawn.at[:, 6, :].set(drawn[:, 6, :])
    return drawn


def draw_key_cache(key, part):
    drawn = cache_keys(key)
    return drawn.astype(jnp.bfloat16)


def draw_queries(key, part):
    key = jax.random.fold_in(key, 41)
    query_base = jnp.clip(2.5 * jax.random.normal(key, (MICRO, ROWS, HEADS * HEAD_DIM), jnp.float32), -15.0, 15.0)
    return query_base.astype(jnp.bfloat16)


def draw_hidden_in(key, part):
    key = jax.random.fold_in(key, 61)
    column = jnp.arange(D, dtype=jnp.float32) / (D - 1)
    rising = 1.0 + 2.0 * column
    base = jnp.clip(jax.random.normal(key, (MICRO, ROWS, D), jnp.float32), -6.0, 6.0)
    drawn = base * rising[None, None, :]
    return jnp.clip(drawn, -18.0, 18.0).astype(jnp.bfloat16)


def draw_lengths(key, part):
    key = jax.random.fold_in(key, 51)
    drawn_lengths = jax.random.randint(key, (MICRO, ROWS), CACHE_LEN // 4, CACHE_LEN + 1)
    return drawn_lengths.at[:, 0].set(CACHE_LEN).astype(jnp.int32)


def draw_cache_slot(key, part):
    return slot_table(key)


def level_of(key, dims, cuts, least, largest):
    loudness = 1.0
    for axis_at, shards_of in cuts:
        heights = jax.random.uniform(jax.random.fold_in(jax.random.fold_in(key, 6), axis_at), (shards_of,), jnp.float32, least / len(cuts), largest / len(cuts))
        loudness = loudness * jnp.repeat(jnp.exp(heights), dims[axis_at] // shards_of).reshape((-1,) + (1,) * (len(dims) - 1 - axis_at))
    return loudness


def noise(own_key, extent, width, reach, cuts=(), kind=jnp.bfloat16):
    level = level_of(own_key, extent, cuts, -0.22, 0.18) if cuts else 1.0
    result = jax.random.normal(own_key, extent, jnp.float32) * width * level
    return jnp.minimum(jnp.maximum(result, -reach), reach).astype(kind)


def setup_inputs(seed: int = 0, part: int = 0) -> dict:
    seeds = jax.random.split(jax.random.key(seed), 12)
    part_splits = jax.random.split(jax.random.fold_in(seeds[11], part), 12)
    hidden_in = draw_hidden_in(jax.random.fold_in(jax.random.fold_in(seeds[11], part), 71), part)
    queries = draw_queries(jax.random.fold_in(jax.random.fold_in(seeds[11], part), 71), part)
    key_cache = draw_key_cache(jax.random.fold_in(jax.random.fold_in(seeds[11], part), 71), part)
    value_cache = noise(part_splits[3], (SLOTS, CACHE_LEN, HEAD_DIM), 1.0, 6.0, ((0, 128),))
    lengths = draw_lengths(jax.random.fold_in(jax.random.fold_in(seeds[11], part), 71), part)
    cache_slot = draw_cache_slot(jax.random.fold_in(jax.random.fold_in(seeds[11], part), 71), part)
    out_weight = noise(seeds[6], (HEADS * HEAD_DIM, D), (HEADS * HEAD_DIM) ** -0.5, 0.046875, ((0, 16), (1, 8)))
    ffn_gain = jnp.clip(1.0 + 0.18 * jax.random.normal(seeds[7], (D,), jnp.float32), 0.099609375, 1.8984375).astype(jnp.bfloat16)
    gate_weight = noise(seeds[8], (D, FF), D ** -0.5, 0.0625, ((0, 8), (1, 16)))
    up_weight = noise(seeds[9], (D, FF), D ** -0.5, 0.0625, ((0, 8), (1, 16)))
    down_weight = noise(seeds[10], (FF, D), FF ** -0.5, 0.046875, ((0, 16), (1, 8)))
    return dict(hidden_in=hidden_in, queries=queries, key_cache=key_cache, value_cache=value_cache, lengths=lengths, cache_slot=cache_slot, out_weight=out_weight, ffn_gain=ffn_gain, gate_weight=gate_weight, up_weight=up_weight, down_weight=down_weight)


EPSILON = 1e-06
MASKED = -1e+30

def rms_normed(stream, gain_vector):
    widened = stream.astype(jnp.float32)
    mean_square = lax.optimization_barrier(jnp.mean(widened * widened, axis=-1, keepdims=True))
    return (widened * lax.rsqrt(mean_square + EPSILON) * gain_vector.astype(jnp.float32)).astype(jnp.bfloat16)

def attend_row(query_row, key_rows, value_rows, length):
    query_heads = query_row.reshape(HEADS, HEAD_DIM)
    scores = jnp.dot(query_heads, key_rows.T, preferred_element_type=jnp.float32) * HEAD_DIM ** (-0.5)
    positions = jnp.arange(CACHE_LEN, dtype=jnp.int32)
    in_cache = (positions < length)[None, :]
    scores = jnp.where(in_cache, scores, MASKED)
    highest = lax.optimization_barrier(jnp.max(scores, axis=1, keepdims=True))
    softened = jnp.where(in_cache, jnp.exp(scores - highest), 0.0)
    totals = lax.optimization_barrier(jnp.sum(softened, axis=1, keepdims=True))
    weighted = jnp.dot(softened.astype(jnp.bfloat16), value_rows, preferred_element_type=jnp.float32)
    return (weighted / totals).astype(jnp.bfloat16).reshape(HEADS * HEAD_DIM)

def reference(hidden_in, queries, key_cache, value_cache, lengths, cache_slot, out_weight, ffn_gain, gate_weight, up_weight, down_weight):
    owners = jnp.arange(ROWS, dtype=jnp.int32) // ROWS_DEV
    results = []
    for micro_step in range(MICRO):
        cache_index = (owners * SLOTS_DEV + cache_slot[micro_step].astype(jnp.int32)).astype(jnp.int32)

        def one_row(packed):
            query_row, index_row, length = packed
            return attend_row(query_row, key_cache[index_row], value_cache[index_row], length)
        attended = lax.map(one_row, (queries[micro_step], cache_index, lengths[micro_step]))
        mixed = jnp.dot(attended, out_weight, preferred_element_type=jnp.float32)
        stream = (hidden_in[micro_step].astype(jnp.float32) + mixed).astype(jnp.bfloat16)
        normed = rms_normed(stream, ffn_gain)
        gate_part = jnp.dot(normed, gate_weight, preferred_element_type=jnp.float32)
        upward = jnp.dot(normed, up_weight, preferred_element_type=jnp.float32)
        activated = (jax.nn.silu(gate_part) * upward).astype(jnp.bfloat16)
        lowered = jnp.dot(activated, down_weight, preferred_element_type=jnp.float32)
        results.append((stream.astype(jnp.float32) + lowered).astype(jnp.bfloat16))
    return jnp.stack(results, axis=0)
```

```python
import jax
import jax.numpy as jnp
from jax import lax
from jax.sharding import Mesh, PartitionSpec as P

EPSILON = 1e-06
MASKED = -1e30
Z = "z"
CORE = "core"
ATTN = (Z, CORE)
FFN = ("x", "y")
REP = "rep"


def attend_rows(query_heads, key_cache, value_cache, slot_rows, length_rows):
    pos_count = key_cache.shape[1]
    head_dim = key_cache.shape[2]
    key_rows = jnp.take(key_cache, slot_rows, axis=0)
    value_rows = jnp.take(value_cache, slot_rows, axis=0)
    scores = jnp.einsum(
        "rhd,rpd->rhp", query_heads, key_rows, preferred_element_type=jnp.float32
    ) * head_dim ** (-0.5)
    positions = jnp.arange(pos_count, dtype=jnp.int32)
    in_cache = (positions[None, :] < length_rows[:, None])[:, None, :]
    scores = jnp.where(in_cache, scores, MASKED)
    highest = jnp.max(scores, axis=2)
    softened = jnp.where(in_cache, jnp.exp(scores - highest[..., None]), 0.0)
    totals = jnp.sum(softened, axis=2)
    weighted = jnp.einsum(
        "rhp,rpd->rhd",
        softened.astype(jnp.bfloat16),
        value_rows,
        preferred_element_type=jnp.float32,
    )
    return (weighted / totals[..., None]).astype(jnp.bfloat16)


def per_device(
    hidden_in,
    queries,
    key_cache,
    value_cache,
    lengths,
    cache_slot,
    out_weight,
    ffn_gain,
    gate_weight,
    up_weight,
    down_weight,
):
    z_count = lax.axis_size(Z)
    core_count = lax.axis_size(CORE)
    attn_count = z_count * core_count
    ffn_count = lax.axis_size("x") * lax.axis_size("y")
    ffn_index = lax.axis_index(FFN)
    core_index = lax.axis_index(CORE)
    micro_count, total_rows, col_share = hidden_in.shape
    head_dim = key_cache.shape[2]
    model_width = col_share * attn_count
    hidden_share = gate_weight.shape[1]
    rows_chunk = attn_count * micro_count
    rows_all = ffn_count * rows_chunk
    swap = [(0, 1), (1, 0)]

    attended = attend_rows(
        queries.reshape(micro_count, -1, head_dim),
        key_cache,
        value_cache,
        cache_slot[:, 0],
        lengths[:, 0],
    )
    outgoing = attended.reshape(micro_count, ffn_count, -1).transpose(1, 0, 2)
    incoming = lax.all_to_all(outgoing, FFN, split_axis=0, concat_axis=0, tiled=True)
    gathered = lax.all_gather(incoming, ATTN, axis=0, tiled=False)
    rows_in = gathered.transpose(1, 0, 2, 3).reshape(rows_all, -1)
    mixed = jnp.dot(rows_in, out_weight, preferred_element_type=jnp.float32).astype(jnp.bfloat16)
    parts = lax.all_to_all(
        mixed.reshape(ffn_count, rows_chunk, col_share), FFN, split_axis=0, concat_axis=0, tiled=True
    )
    own_hidden = lax.dynamic_index_in_dim(
        hidden_in.reshape(micro_count, attn_count, ffn_count, col_share),
        ffn_index,
        axis=2,
        keepdims=False,
    ).transpose(1, 0, 2)
    stream = (
        own_hidden.reshape(rows_chunk, col_share).astype(jnp.float32)
        + jnp.sum(parts.astype(jnp.float32), axis=0)
    ).astype(jnp.bfloat16)
    copies = jnp.broadcast_to(stream[None], (ffn_count, rows_chunk, col_share))
    stream_all = lax.all_to_all(copies, FFN, split_axis=0, concat_axis=0, tiled=True)
    stream_all = stream_all.reshape(rows_all, col_share).astype(jnp.float32)
    squares = jnp.sum(stream_all * stream_all, axis=1, keepdims=True)
    squares_hi = squares.astype(jnp.bfloat16)
    squares_lo = (squares - squares_hi.astype(jnp.float32)).astype(jnp.bfloat16)
    scaled = (stream_all * ffn_gain.astype(jnp.float32)[None, :]).astype(jnp.bfloat16)
    gate_part = jnp.dot(scaled, gate_weight, preferred_element_type=jnp.float32)
    up_part = jnp.dot(scaled, up_weight, preferred_element_type=jnp.float32)
    pad = jnp.zeros((rows_all, 126), jnp.bfloat16)
    payload = jnp.concatenate(
        [gate_part.astype(jnp.bfloat16), up_part.astype(jnp.bfloat16), squares_hi, squares_lo, pad], axis=1
    )
    width = payload.shape[1]
    payload = payload.reshape(z_count, core_count, rows_all // attn_count, width)
    own_half = lax.dynamic_index_in_dim(payload, core_index, axis=1, keepdims=False)
    other_half = lax.dynamic_index_in_dim(payload, 1 - core_index, axis=1, keepdims=False)
    received = lax.ppermute(other_half, CORE, swap)
    pair = (own_half.astype(jnp.float32) + received.astype(jnp.float32))
    pair_hi = pair.astype(jnp.bfloat16)
    sq = pair[..., 2 * hidden_share : 2 * hidden_share + 1] + pair[..., 2 * hidden_share + 1 : 2 * hidden_share + 2]
    sq_hi = sq.astype(jnp.bfloat16)
    sq_lo = (sq - sq_hi.astype(jnp.float32)).astype(jnp.bfloat16)
    pair_out = jnp.concatenate(
        [pair_hi[..., : 2 * hidden_share], sq_hi, sq_lo, pair_hi[..., 2 * hidden_share + 2 :]], axis=-1
    )
    along = lax.all_to_all(pair_out, Z, split_axis=0, concat_axis=0, tiled=True)
    total = jnp.sum(along.astype(jnp.float32), axis=0)
    row_squares = total[:, 2 * hidden_share] + total[:, 2 * hidden_share + 1]
    scale = lax.rsqrt(row_squares / model_width + EPSILON)[:, None]
    gate_full = total[:, :hidden_share] * scale
    up_full = total[:, hidden_share : 2 * hidden_share] * scale
    activated = (jax.nn.silu(gate_full) * up_full).astype(jnp.bfloat16)
    activated_all = lax.all_gather(activated, ATTN, axis=0, tiled=True)
    lowered = jnp.dot(activated_all, down_weight, preferred_element_type=jnp.float32).astype(jnp.bfloat16)
    lowered_parts = lax.all_to_all(
        lowered.reshape(ffn_count, rows_chunk, col_share), FFN, split_axis=0, concat_axis=0, tiled=True
    )
    finished = (
        stream.astype(jnp.float32) + jnp.sum(lowered_parts.astype(jnp.float32), axis=0)
    ).astype(jnp.bfloat16)
    delivered = lax.all_to_all(
        finished.reshape(attn_count, micro_count, col_share), ATTN, split_axis=0, concat_axis=0, tiled=True
    )
    return delivered.transpose(1, 0, 2).reshape(micro_count, 1, model_width)


def solution(mesh):
    sizes = dict(mesh.shape)
    attn_count, ffn_count, rep_count = sizes["attn"], sizes["ffn"], sizes["rep"]
    side = int(round(ffn_count**0.5))
    fine = Mesh(
        mesh.devices.reshape(attn_count // 2, 2, side, ffn_count // side, rep_count),
        (Z, CORE, "x", "y", REP),
    )
    owners = (REP, Z, CORE, "x", "y")
    return jax.shard_map(
        per_device,
        mesh=fine,
        in_specs=(
            P(None, REP, ATTN),
            P(None, owners, None),
            P(owners, None, None),
            P(owners, None, None),
            P(None, owners),
            P(None, owners),
            P(FFN, ATTN),
            P(ATTN),
            P(ATTN, FFN),
            P(ATTN, FFN),
            P(FFN, ATTN),
        ),
        out_specs=P(None, owners, None),
        check_vma=False,
    )
```

```python
import functools

import jax
import jax.numpy as jnp
from jax import lax
from jax.experimental import pallas as pl
from jax.experimental.pallas import tpu as pltpu
from jax.sharding import Mesh, PartitionSpec as P

EPSILON = 1e-06
MASKED = -1e30
Z = "z"
CORE = "core"
ATTN = (Z, CORE)
FFN = ("x", "y")
REP = "rep"
LANES = 128
SQ_ROWS = 16
BF16 = jnp.bfloat16
F32 = jnp.float32


def whole():
    return pl.BlockSpec(memory_space=pltpu.VMEM)


def scalars():
    return pl.BlockSpec(memory_space=pltpu.SMEM)


def params(mib):
    return pltpu.CompilerParams(vmem_limit_bytes=mib * 1024 * 1024)


def one_hot(shape, source_of_row):
    rows = lax.broadcasted_iota(jnp.int32, shape, 0)
    cols = lax.broadcasted_iota(jnp.int32, shape, 1)
    return jnp.where(cols == source_of_row(rows), 1.0, 0.0)


def attention_kernel(slot_ref, length_ref, query_ref, key_ref, value_ref, out_ref):
    step = pl.program_id(0)
    head_dim = key_ref.shape[2]
    scores = lax.dot_general(
        query_ref[0], key_ref[0], (((1,), (1,)), ((), ())), preferred_element_type=F32
    ) * head_dim ** (-0.5)
    positions = lax.broadcasted_iota(jnp.int32, scores.shape, 1)
    in_cache = positions < length_ref[step]
    scores = jnp.where(in_cache, scores, MASKED)
    highest = jnp.max(scores, axis=1, keepdims=True)
    softened = jnp.where(in_cache, jnp.exp(scores - highest), 0.0)
    totals = jnp.sum(softened, axis=1, keepdims=True)
    weighted = jnp.dot(softened.astype(BF16), value_ref[0], preferred_element_type=F32)
    attended = (weighted / totals).astype(BF16)
    heads = attended.shape[0]
    pieces = head_dim // LANES
    tiles = None
    for piece in range(pieces):
        spread = one_hot((heads * pieces, heads), lambda r: jnp.where(r % pieces == piece, r // pieces, -1))
        part = jnp.dot(
            spread.astype(BF16), attended[:, piece * LANES : (piece + 1) * LANES], preferred_element_type=F32
        )
        tiles = part if tiles is None else tiles + part
    copies, blocks, _, tile_rows, _ = out_ref.shape
    tiles = tiles.reshape(blocks, tile_rows, LANES).astype(BF16)
    for copy in range(copies):
        out_ref[copy, :, 0] = tiles


def attend(queries, key_cache, value_cache, slots, lengths, copies, blocks):
    micro, heads, head_dim = queries.shape
    pos = key_cache.shape[1]
    tile_rows = heads * head_dim // blocks // LANES
    return pl.pallas_call(
        attention_kernel,
        grid_spec=pltpu.PrefetchScalarGridSpec(
            num_scalar_prefetch=2,
            grid=(micro,),
            in_specs=[
                pl.BlockSpec((1, heads, head_dim), lambda m, s, n: (m, 0, 0)),
                pl.BlockSpec((1, pos, head_dim), lambda m, s, n: (s[m], 0, 0)),
                pl.BlockSpec((1, pos, head_dim), lambda m, s, n: (s[m], 0, 0)),
            ],
            out_specs=pl.BlockSpec((copies, blocks, 1, tile_rows, LANES), lambda m, s, n: (0, 0, m, 0, 0)),
        ),
        out_shape=jax.ShapeDtypeStruct((copies, blocks, micro, tile_rows, LANES), BF16),
        compiler_params=params(16),
        name="attention",
    )(slots, lengths, queries, key_cache, value_cache)


def rows_kernel(in_ref, out_ref, wide):
    rows, tile_rows, lanes = in_ref.shape
    wide[...] = in_ref[...].astype(F32).reshape(rows * tile_rows, lanes)
    for j in range(tile_rows):
        out_ref[:, j * lanes : (j + 1) * lanes] = wide[pl.ds(j, rows, stride=tile_rows), :].astype(BF16)


def to_rows(tiles):
    rows, tile_rows, lanes = tiles.shape
    return pl.pallas_call(
        rows_kernel,
        out_shape=jax.ShapeDtypeStruct((rows, tile_rows * lanes), BF16),
        in_specs=[whole()],
        out_specs=whole(),
        scratch_shapes=[pltpu.VMEM((rows * tile_rows, lanes), F32)],
        compiler_params=params(8),
        name="to_rows",
    )(tiles)


def mix_kernel(order, rows_ref, weight_ref, out_ref):
    core_count, z_count, ffn_count, micro = order
    total = rows_ref.shape[0]
    product = jnp.dot(rows_ref[...], weight_ref[...], preferred_element_type=F32).astype(BF16)

    def source(r):
        m = r % micro
        c = (r // micro) % core_count
        z = (r // (micro * core_count)) % z_count
        f = r // (micro * core_count * z_count)
        return ((c * z_count + z) * ffn_count + f) * micro + m

    spread = one_hot((total, total), source).astype(BF16)
    out_ref[...] = jnp.dot(spread, product, preferred_element_type=F32).astype(BF16)


def mix(rows, weight, order):
    return pl.pallas_call(
        functools.partial(mix_kernel, order),
        out_shape=jax.ShapeDtypeStruct((rows.shape[0], weight.shape[1]), BF16),
        in_specs=[whole(), whole()],
        out_specs=whole(),
        compiler_params=params(16),
        name="mix",
    )(rows, weight)


def stream_kernel(parts_ref, hidden_ref, stream_ref, copies_ref):
    total = hidden_ref[...].astype(F32)
    partial = parts_ref[0].astype(F32)
    for j in range(1, parts_ref.shape[0]):
        partial = partial + parts_ref[j].astype(F32)
    stream = (total + partial).astype(BF16)
    stream_ref[...] = stream
    for j in range(copies_ref.shape[0]):
        copies_ref[j] = stream


def make_stream(parts, hidden):
    return pl.pallas_call(
        stream_kernel,
        out_shape=(
            jax.ShapeDtypeStruct(hidden.shape, BF16),
            jax.ShapeDtypeStruct(parts.shape, BF16),
        ),
        in_specs=[whole(), whole()],
        out_specs=(whole(), whole()),
        compiler_params=params(8),
        name="make_stream",
    )(parts, hidden)


def split(value):
    high = value.astype(BF16)
    low = (value - high.astype(F32)).astype(BF16)
    return high, low


def squares_rows(row_values, width):
    high = row_values.astype(BF16).astype(F32)
    low = row_values - high
    index = lax.broadcasted_iota(jnp.int32, (SQ_ROWS, width), 0)
    return jnp.where(index == 0, high, jnp.where(index == 1, low, 0.0)).astype(BF16)


def up_kernel(z_count, core_count, which_ref, stream_ref, gain_ref, gate_ref, up_ref, out_ref, scaled):
    rows = stream_ref.shape[0] // (z_count * core_count)
    core = which_ref[0]
    gain = gain_ref[...].astype(F32)
    hidden = gate_ref.shape[1]
    tiles = hidden // LANES
    for z in range(z_count):
        start = pl.multiple_of((z * core_count + core) * rows, 16)
        block = stream_ref[pl.ds(start, rows), :].astype(F32)
        scaled[pl.ds(z * rows, rows), :] = (block * gain).astype(BF16)
        squares = jnp.sum(block * block, axis=1, keepdims=True)
        spread = one_hot((rows, LANES), lambda r: r)
        out_ref[z, 2 * tiles * rows : 2 * tiles * rows + SQ_ROWS, :] = squares_rows(
            jnp.sum(spread * squares, axis=0, keepdims=True), LANES
        )
    for side, weight_ref in enumerate((gate_ref, up_ref)):
        product = jnp.dot(scaled[...], weight_ref[...], preferred_element_type=F32).astype(BF16)
        for z in range(z_count):
            for j in range(tiles):
                at = (side * tiles + j) * rows
                out_ref[z, at : at + rows, :] = product[
                    z * rows : (z + 1) * rows, j * LANES : (j + 1) * LANES
                ]


def up_part(which, stream_all, gain, gate_weight, up_weight, z_count, core_count):
    rows_all, width = stream_all.shape
    rows = rows_all // (z_count * core_count)
    hidden = gate_weight.shape[1]
    out_rows = 2 * hidden // LANES * rows + SQ_ROWS
    return pl.pallas_call(
        functools.partial(up_kernel, z_count, core_count),
        out_shape=jax.ShapeDtypeStruct((z_count, out_rows, LANES), BF16),
        in_specs=[scalars(), whole(), whole(), whole(), whole()],
        out_specs=whole(),
        scratch_shapes=[pltpu.VMEM((z_count * rows, width), BF16)],
        compiler_params=params(20),
        cost_estimate=pl.CostEstimate(
            flops=4 * z_count * rows * width * hidden, bytes_accessed=4 * width * hidden, transcendentals=0
        ),
        name="up_part",
    )(which, stream_all, gain, gate_weight, up_weight)


def pair_kernel(own_ref, other_ref, out_ref):
    z_count, out_rows, lanes = own_ref.shape
    body = out_rows - SQ_ROWS
    for z in range(z_count):
        out_ref[z, :body, :] = (
            own_ref[z, :body, :].astype(F32) + other_ref[z, :body, :].astype(F32)
        ).astype(BF16)
        tail = own_ref[z, body:, :].astype(F32) + other_ref[z, body:, :].astype(F32)
        out_ref[z, body:, :] = squares_rows(tail[0:1] + tail[1:2], lanes)


def add_pair(own, other):
    return pl.pallas_call(
        pair_kernel,
        out_shape=jax.ShapeDtypeStruct(own.shape, BF16),
        in_specs=[whole(), whole()],
        out_specs=whole(),
        compiler_params=params(8),
        name="add_pair",
    )(own, other)


def activate_kernel(model_width, parts_ref, out_ref):
    z_count, out_rows, lanes = parts_ref.shape
    rows, hidden = out_ref.shape
    tiles = hidden // lanes
    body = out_rows - SQ_ROWS

    def total(start, count):
        acc = parts_ref[0, start : start + count, :].astype(F32)
        for z in range(1, z_count):
            acc = acc + parts_ref[z, start : start + count, :].astype(F32)
        return acc

    tail = total(body, SQ_ROWS)
    lane_sums = tail[0:1] + tail[1:2]
    spread = one_hot((rows, lanes), lambda r: r)
    squares = jnp.sum(spread * lane_sums, axis=1, keepdims=True)
    scale = lax.rsqrt(squares / model_width + EPSILON)
    for j in range(tiles):
        gate = total(j * rows, rows) * scale
        upward = total((tiles + j) * rows, rows) * scale
        out_ref[:, j * lanes : (j + 1) * lanes] = (gate / (1.0 + jnp.exp(-gate)) * upward).astype(BF16)


def activate(parts, rows, hidden, model_width):
    return pl.pallas_call(
        functools.partial(activate_kernel, model_width),
        out_shape=jax.ShapeDtypeStruct((rows, hidden), BF16),
        in_specs=[whole()],
        out_specs=whole(),
        compiler_params=params(8),
        name="activate",
    )(parts)


def down_kernel(rows_ref, weight_ref, out_ref):
    out_ref[...] = jnp.dot(rows_ref[...], weight_ref[...], preferred_element_type=F32).astype(BF16)


def down(rows, weight):
    return pl.pallas_call(
        down_kernel,
        out_shape=jax.ShapeDtypeStruct((rows.shape[0], weight.shape[1]), BF16),
        in_specs=[whole(), whole()],
        out_specs=whole(),
        compiler_params=params(16),
        name="down",
    )(rows, weight)


def finish_kernel(parts_ref, stream_ref, out_ref):
    partial = parts_ref[0].astype(F32)
    for j in range(1, parts_ref.shape[0]):
        partial = partial + parts_ref[j].astype(F32)
    out_ref[...] = (stream_ref[...].astype(F32) + partial).astype(BF16)


def finish(parts, stream):
    return pl.pallas_call(
        finish_kernel,
        out_shape=jax.ShapeDtypeStruct(stream.shape, BF16),
        in_specs=[whole(), whole()],
        out_specs=whole(),
        compiler_params=params(8),
        name="finish",
    )(parts, stream)


def per_device(
    hidden_in,
    queries,
    key_cache,
    value_cache,
    lengths,
    cache_slot,
    out_weight,
    ffn_gain,
    gate_weight,
    up_weight,
    down_weight,
):
    z_count = lax.axis_size(Z)
    core_count = lax.axis_size(CORE)
    attn_count = z_count * core_count
    ffn_count = lax.axis_size("x") * lax.axis_size("y")
    ffn_index = lax.axis_index(FFN)
    core_index = lax.axis_index(CORE)
    micro, total_rows, col_share = hidden_in.shape
    head_dim = key_cache.shape[2]
    model_width = col_share * attn_count
    hidden_share = gate_weight.shape[1]
    rows_chunk = attn_count * micro
    rows_all = ffn_count * rows_chunk
    swap = [(i, core_count - 1 - i) for i in range(core_count)]

    payload = attend(
        queries.reshape(micro, -1, head_dim),
        key_cache,
        value_cache,
        cache_slot[:, 0],
        lengths[:, 0],
        z_count,
        ffn_count,
    )
    tile_rows = payload.shape[3]
    payload = payload.reshape(z_count * ffn_count, micro * tile_rows, LANES)
    incoming = lax.all_to_all(payload, (Z,) + FFN, split_axis=0, concat_axis=0, tiled=True)
    chip_rows = to_rows(incoming.reshape(z_count * ffn_count * micro, tile_rows, LANES))
    rows_in = lax.all_gather(chip_rows, CORE, axis=0, tiled=True)
    mixed = mix(rows_in, out_weight, (core_count, z_count, ffn_count, micro))

    parts = lax.all_to_all(
        mixed.reshape(ffn_count, rows_chunk, col_share), FFN, split_axis=0, concat_axis=0, tiled=True
    )
    own_hidden = lax.dynamic_index_in_dim(
        hidden_in.reshape(micro, attn_count, ffn_count, col_share), ffn_index, axis=2, keepdims=False
    )
    own_hidden = own_hidden.transpose(1, 0, 2).reshape(rows_chunk, col_share)
    stream, copies = make_stream(parts, own_hidden)
    stream_all = lax.all_to_all(copies, FFN, split_axis=0, concat_axis=0, tiled=True)
    stream_all = stream_all.reshape(rows_all, col_share)

    gain = ffn_gain[None, :]
    core = core_index.astype(jnp.int32)[None]
    other = up_part(core_count - 1 - core, stream_all, gain, gate_weight, up_weight, z_count, core_count)
    received = lax.ppermute(other, CORE, swap)
    own = up_part(core, stream_all, gain, gate_weight, up_weight, z_count, core_count)
    along = lax.all_to_all(add_pair(own, received), Z, split_axis=0, concat_axis=0, tiled=True)
    activated = activate(along, rows_all // attn_count, hidden_share, model_width)
    activated_all = lax.all_gather(activated, ATTN, axis=0, tiled=True)
    lowered = down(activated_all, down_weight)
    lowered_parts = lax.all_to_all(
        lowered.reshape(ffn_count, rows_chunk, col_share), FFN, split_axis=0, concat_axis=0, tiled=True
    )
    finished = finish(lowered_parts, stream)
    delivered = lax.all_to_all(
        finished.reshape(attn_count, micro, col_share), ATTN, split_axis=0, concat_axis=0, tiled=True
    )
    return delivered.transpose(1, 0, 2).reshape(micro, 1, model_width)


def solution(mesh):
    sizes = dict(mesh.shape)
    attn_count, ffn_count, rep_count = sizes["attn"], sizes["ffn"], sizes["rep"]
    side = int(round(ffn_count**0.5))
    fine = Mesh(
        mesh.devices.reshape(attn_count // 2, 2, side, ffn_count // side, rep_count),
        (Z, CORE, "x", "y", REP),
    )
    owners = (REP, Z, CORE, "x", "y")
    return jax.shard_map(
        per_device,
        mesh=fine,
        in_specs=(
            P(None, REP, ATTN),
            P(None, owners, None),
            P(owners, None, None),
            P(owners, None, None),
            P(None, owners),
            P(None, owners),
            P(FFN, ATTN),
            P(ATTN),
            P(ATTN, FFN),
            P(ATTN, FFN),
            P(FFN, ATTN),
        ),
        out_specs=P(None, owners, None),
        check_vma=False,
    )
```

```python
import functools

import jax
import jax.numpy as jnp
from jax import lax
from jax.experimental import pallas as pl
from jax.experimental.pallas import tpu as pltpu
from jax.sharding import Mesh, PartitionSpec as P

EPSILON = 1e-06
MASKED = -1e30
Z = "z"
CORE = "core"
ATTN = (Z, CORE)
FFN = ("x", "y")
REP = "rep"
LANES = 128
SQ_ROWS = 16
BF16 = jnp.bfloat16
F32 = jnp.float32
HEAVY = pl.CostEstimate(flops=10**10, bytes_accessed=10**7, transcendentals=0)


def whole():
    return pl.BlockSpec(memory_space=pltpu.VMEM)


def scalars():
    return pl.BlockSpec(memory_space=pltpu.SMEM)


def in_hbm():
    return pl.BlockSpec(memory_space=pltpu.HBM)


def params(mib):
    return pltpu.CompilerParams(vmem_limit_bytes=mib * 1024 * 1024)


def one_hot(shape, source_of_row):
    rows = lax.broadcasted_iota(jnp.int32, shape, 0)
    cols = lax.broadcasted_iota(jnp.int32, shape, 1)
    return jnp.where(cols == source_of_row(rows), 1.0, 0.0)


def attention_kernel(slot_ref, length_ref, query_ref, key_hbm, value_hbm, out_ref, keys, values, wide, key_sem, value_sem):
    micro, pos, head_dim = keys.shape
    heads = query_ref.shape[1] // head_dim
    copies, blocks, _, tile_rows, _ = out_ref.shape
    key_copies = [pltpu.make_async_copy(key_hbm.at[slot_ref[0, m]], keys.at[m], key_sem.at[m]) for m in range(micro)]
    value_copies = [
        pltpu.make_async_copy(value_hbm.at[slot_ref[0, m]], values.at[m], value_sem.at[m]) for m in range(micro)
    ]
    for copy in key_copies + value_copies:
        copy.start()
    for h in range(heads):
        wide[:, h, :] = query_ref[:, h * head_dim : (h + 1) * head_dim].astype(F32)
    pieces = head_dim // LANES
    group = heads // blocks
    positions = lax.broadcasted_iota(jnp.int32, (heads, pos), 1)
    softened = []
    totals = []
    for m in range(micro):
        key_copies[m].wait()
        scores = lax.dot_general(
            wide[m].astype(BF16), keys[m], (((1,), (1,)), ((), ())), preferred_element_type=F32
        ) * head_dim ** (-0.5)
        in_cache = positions < length_ref[0, m]
        scores = jnp.where(in_cache, scores, MASKED)
        highest = jnp.max(scores, axis=1, keepdims=True)
        weights = jnp.where(in_cache, jnp.exp(scores - highest), 0.0)
        totals.append(jnp.sum(weights, axis=1, keepdims=True))
        softened.append(weights.astype(BF16))
    for m in range(micro):
        value_copies[m].wait()
        weighted = jnp.dot(softened[m], values[m], preferred_element_type=F32)
        attended = weighted / totals[m]
        for piece in range(pieces):
            part = attended[:, piece * LANES : (piece + 1) * LANES].reshape(blocks, group, LANES).astype(BF16)
            for copy in range(copies):
                out_ref[copy, :, m, piece * group : (piece + 1) * group, :] = part


def attend(queries, key_cache, value_cache, slots, lengths, copies, blocks):
    slot_count, pos, head_dim = key_cache.shape
    micro, width = queries.shape
    tile_rows = width // blocks // LANES
    return pl.pallas_call(
        attention_kernel,
        in_specs=[scalars(), scalars(), whole(), in_hbm(), in_hbm()],
        out_specs=whole(),
        out_shape=jax.ShapeDtypeStruct((copies, blocks, micro, tile_rows, LANES), BF16),
        scratch_shapes=[
            pltpu.VMEM((micro, pos, head_dim), BF16),
            pltpu.VMEM((micro, pos, head_dim), BF16),
            pltpu.VMEM((micro, width // head_dim, head_dim), F32),
            pltpu.SemaphoreType.DMA((micro,)),
            pltpu.SemaphoreType.DMA((micro,)),
        ],
        compiler_params=params(60),
        name="attention",
    )(slots, lengths, queries, key_cache, value_cache)


def rows_kernel(pieces, in_ref, out_ref, wide):
    rows, tile_rows, lanes = in_ref.shape
    wide[...] = in_ref[...].astype(F32).reshape(rows * tile_rows, lanes)
    group = tile_rows // pieces
    for j in range(tile_rows):
        at = (j % pieces) * group + j // pieces
        out_ref[:, j * lanes : (j + 1) * lanes] = wide[pl.ds(at, rows, stride=tile_rows), :].astype(BF16)


def to_rows(tiles, pieces):
    rows, tile_rows, lanes = tiles.shape
    return pl.pallas_call(
        functools.partial(rows_kernel, pieces),
        out_shape=jax.ShapeDtypeStruct((rows, tile_rows * lanes), BF16),
        in_specs=[whole()],
        out_specs=whole(),
        scratch_shapes=[pltpu.VMEM((rows * tile_rows, lanes), F32)],
        compiler_params=params(8),
        name="to_rows",
    )(tiles)


def product_kernel(*refs):
    *piece_refs, weight_ref, out_ref = refs
    count = piece_refs[0].shape[0]
    rows = jnp.concatenate([ref[...] for ref in piece_refs], axis=0)
    product = jnp.dot(rows, weight_ref[...], preferred_element_type=F32).astype(BF16)
    for k in range(len(piece_refs)):
        out_ref[k] = product[k * count : (k + 1) * count]


def product_of(pieces, weight):
    count, depth = pieces[0].shape
    width = weight.shape[1]
    return pl.pallas_call(
        product_kernel,
        out_shape=jax.ShapeDtypeStruct((len(pieces), count, width), BF16),
        in_specs=[whole()] * (len(pieces) + 1),
        out_specs=whole(),
        compiler_params=params(12),
        cost_estimate=HEAVY,
        name="product",
    )(*pieces, weight)


def mix_kernel(order, *refs):
    core_count, z_count, ffn_count, micro = order
    core_ref, own_ref, rows_ref, weight_ref, out_ref = refs
    total = 2 * rows_ref.shape[0]
    product = jnp.dot(rows_ref[...], weight_ref[...], preferred_element_type=F32).astype(BF16)
    own = own_ref[0]
    core = core_ref[0]

    def source(r):
        m = r % micro
        c = (r // micro) % core_count
        from_z = (r // (micro * core_count)) % z_count
        f = r // (micro * core_count * z_count)
        return (((c ^ core) * z_count + from_z) * ffn_count + f) * micro + m

    spread = one_hot((total, total), source).astype(BF16)
    both = jnp.concatenate([own, product], axis=0)
    out_ref[...] = jnp.dot(spread, both, preferred_element_type=F32).astype(BF16)


def mix(core, own, rows, weight, order):
    total = 2 * rows.shape[0]
    return pl.pallas_call(
        functools.partial(mix_kernel, order),
        out_shape=jax.ShapeDtypeStruct((total, weight.shape[1]), BF16),
        in_specs=[scalars(), whole(), whole(), whole()],
        out_specs=whole(),
        compiler_params=params(12),
        name="mix",
    )(core, own, rows, weight)


def down_kernel(z_ref, core_ref, first_ref, own_ref, *refs):
    *piece_refs, weight_ref, out_ref = refs
    count = piece_refs[0].shape[0]
    rows = jnp.concatenate([ref[...] for ref in piece_refs], axis=0)
    product = jnp.dot(rows, weight_ref[...], preferred_element_type=F32).astype(BF16)
    z = z_ref[0]
    core = core_ref[0]
    out_ref[2 * z + core] = first_ref[0]
    out_ref[2 * z + 1 - core] = first_ref[1]
    for k in range(len(piece_refs)):
        out_ref[2 * (z ^ (k + 1)) + core] = own_ref[k]
        out_ref[2 * (z ^ (k + 1)) + 1 - core] = product[k * count : (k + 1) * count]


def down(z, core, first, own, pieces, weight):
    count = 2 * (len(pieces) + 1)
    return pl.pallas_call(
        down_kernel,
        out_shape=jax.ShapeDtypeStruct((count, pieces[0].shape[0], weight.shape[1]), BF16),
        in_specs=[scalars(), scalars()] + [whole()] * (len(pieces) + 3),
        out_specs=whole(),
        compiler_params=params(12),
        name="down",
    )(z, core, first, own, *pieces, weight)


def stream_kernel(order, f_ref, parts_ref, hidden_ref, stream_ref, copies_ref):
    attn_count, ffn_count, micro = order
    rows = stream_ref.shape[0]
    f = f_ref[0]

    def source(r):
        return ((r % micro) * attn_count + r // micro) * ffn_count + f

    spread = one_hot((rows, hidden_ref.shape[0]), source).astype(BF16)
    hidden = jnp.dot(spread, hidden_ref[...], preferred_element_type=F32)
    partial = parts_ref[0].astype(F32)
    for j in range(1, parts_ref.shape[0]):
        partial = partial + parts_ref[j].astype(F32)
    stream = (hidden + partial).astype(BF16)
    stream_ref[...] = stream
    for j in range(copies_ref.shape[0]):
        copies_ref[j] = stream


def make_stream(f, parts, hidden, order):
    return pl.pallas_call(
        functools.partial(stream_kernel, order),
        out_shape=(
            jax.ShapeDtypeStruct(parts.shape[1:], BF16),
            jax.ShapeDtypeStruct(parts.shape, BF16),
        ),
        in_specs=[scalars(), whole(), whole()],
        out_specs=(whole(), whole()),
        compiler_params=params(8),
        name="make_stream",
    )(f, parts, hidden)


def squares_rows(row_values, width):
    high = row_values.astype(BF16).astype(F32)
    low = row_values - high
    index = lax.broadcasted_iota(jnp.int32, (SQ_ROWS, width), 0)
    return jnp.where(index == 0, high, jnp.where(index == 1, low, 0.0)).astype(BF16)


def tile_places(tiles, rows):
    direct = tiles // 4
    places = {}
    for half in range(2):
        for j in range(tiles):
            if j < direct:
                places[half, j] = (half * direct + j) * rows
            else:
                places[half, j] = (2 * direct + half * (tiles - direct) + j - direct) * rows + SQ_ROWS
    return places, 2 * direct * rows


def up_kernel(hops, z_ref, core_ref, stream_ref, gain_ref, gate_ref, up_ref, own_ref, other_ref, scaled):
    tiles = gate_ref.shape[1] // LANES
    rows = (own_ref.shape[1] - SQ_ROWS) // (2 * tiles)
    tile_at, squares_at = tile_places(tiles, rows)
    gain = gain_ref[...].astype(F32)
    places = [(out_ref, side, k, hop) for side, out_ref in ((1, other_ref), (0, own_ref)) for k, hop in enumerate(hops)]
    for i, (out_ref, side, k, hop) in enumerate(places):
        start = pl.multiple_of(((z_ref[0] ^ hop) * 2 + (core_ref[0] ^ side)) * rows, 16)
        block = stream_ref[pl.ds(start, rows), :].astype(F32)
        scaled[i * rows : (i + 1) * rows, :] = (block * gain).astype(BF16)
        squares = jnp.sum(block * block, axis=1, keepdims=True)
        spread = one_hot((rows, LANES), lambda r: r)
        out_ref[k, squares_at : squares_at + SQ_ROWS, :] = squares_rows(
            jnp.sum(spread * squares, axis=0, keepdims=True), LANES
        )
    for half, weight_ref in enumerate((gate_ref, up_ref)):
        product = jnp.dot(scaled[...], weight_ref[...], preferred_element_type=F32).astype(BF16)
        for i, (out_ref, side, k, hop) in enumerate(places):
            for j in range(tiles):
                at = tile_at[half, j]
                out_ref[k, at : at + rows, :] = product[i * rows : (i + 1) * rows, j * LANES : (j + 1) * LANES]


def up_part(hops, z, core, stream_all, gain, gate_weight, up_weight, rows):
    width, hidden = gate_weight.shape
    out_rows = 2 * hidden // LANES * rows + SQ_ROWS
    shape = jax.ShapeDtypeStruct((len(hops), out_rows, LANES), BF16)
    return pl.pallas_call(
        functools.partial(up_kernel, hops),
        out_shape=(shape, shape),
        in_specs=[scalars(), scalars(), whole(), whole(), whole(), whole()],
        out_specs=(whole(), whole()),
        scratch_shapes=[pltpu.VMEM((2 * len(hops) * rows, width), BF16)],
        compiler_params=params(12),
        cost_estimate=HEAVY,
        name="up_part",
    )(z, core, stream_all, gain, gate_weight, up_weight)


def add_squares(first, second):
    total = first.astype(F32) + second.astype(F32)
    return squares_rows(total[0:1] + total[1:2], total.shape[1])


def far_kernel(squares_at, own_ref, other_ref, *out_refs):
    cut = squares_at + SQ_ROWS
    for k in range(2):
        direct_ref, relayed_ref = out_refs[2 * k], out_refs[2 * k + 1]
        direct_ref[:squares_at, :] = (
            own_ref[k, :squares_at, :].astype(F32) + other_ref[k, :squares_at, :].astype(F32)
        ).astype(BF16)
        direct_ref[squares_at:, :] = add_squares(own_ref[k, squares_at:cut, :], other_ref[k, squares_at:cut, :])
        relayed_ref[...] = (own_ref[k, cut:, :].astype(F32) + other_ref[k, cut:, :].astype(F32)).astype(BF16)


def add_far(own, other, squares_at):
    _, out_rows, lanes = own.shape
    cut = squares_at + SQ_ROWS
    direct = jax.ShapeDtypeStruct((cut, lanes), BF16)
    relayed = jax.ShapeDtypeStruct((out_rows - cut, lanes), BF16)
    return pl.pallas_call(
        functools.partial(far_kernel, squares_at),
        out_shape=[direct, relayed, direct, relayed],
        in_specs=[whole(), whole()],
        out_specs=[whole()] * 4,
        compiler_params=params(8),
        name="add_far",
    )(own, other)


def near_kernel(squares_at, own_ref, other_ref, *out_refs):
    cut = squares_at + SQ_ROWS
    for k, out_ref in enumerate(out_refs):
        out_ref[...] = (own_ref[k].astype(F32) + other_ref[k].astype(F32)).astype(BF16)
        out_ref[squares_at:cut, :] = add_squares(own_ref[k, squares_at:cut, :], other_ref[k, squares_at:cut, :])


def add_near(own, other, squares_at):
    count, out_rows, lanes = own.shape
    return pl.pallas_call(
        functools.partial(near_kernel, squares_at),
        out_shape=[jax.ShapeDtypeStruct((out_rows, lanes), BF16)] * count,
        in_specs=[whole(), whole()],
        out_specs=[whole()] * count,
        compiler_params=params(8),
        name="add_near",
    )(own, other)


def relay_kernel(first, second, out_ref):
    out_ref[...] = (first[...].astype(F32) + second[...].astype(F32)).astype(BF16)


def add_relayed(first, second):
    return pl.pallas_call(
        relay_kernel,
        out_shape=jax.ShapeDtypeStruct(first.shape, BF16),
        in_specs=[whole(), whole()],
        out_specs=whole(),
        compiler_params=params(8),
        name="add_relayed",
    )(first, second)


def activate_kernel(model_width, own_ref, near_ref, direct2_ref, direct3_ref, relayed_ref, out_ref):
    rows, hidden = out_ref.shape
    lanes = own_ref.shape[1]
    tiles = hidden // lanes
    tile_at, squares_at = tile_places(tiles, rows)
    cut = squares_at + SQ_ROWS

    def total(start, count):
        acc = own_ref[start : start + count, :].astype(F32) + near_ref[start : start + count, :].astype(F32)
        if start < cut:
            acc = acc + direct2_ref[start : start + count, :].astype(F32)
            return acc + direct3_ref[start : start + count, :].astype(F32)
        return acc + relayed_ref[start - cut : start - cut + count, :].astype(F32)

    tail = total(squares_at, SQ_ROWS)
    lane_sums = tail[0:1] + tail[1:2]
    spread = one_hot((rows, lanes), lambda r: r)
    squares = jnp.sum(spread * lane_sums, axis=1, keepdims=True)
    scale = lax.rsqrt(squares / model_width + EPSILON)
    for j in range(tiles):
        gate = total(tile_at[0, j], rows) * scale
        upward = total(tile_at[1, j], rows) * scale
        out_ref[:, j * lanes : (j + 1) * lanes] = (gate / (1.0 + jnp.exp(-gate)) * upward).astype(BF16)


def activate(parts, rows, hidden, model_width):
    return pl.pallas_call(
        functools.partial(activate_kernel, model_width),
        out_shape=jax.ShapeDtypeStruct((rows, hidden), BF16),
        in_specs=[whole()] * len(parts),
        out_specs=whole(),
        compiler_params=params(8),
        name="activate",
    )(*parts)


def finish_kernel(z_count, micro, z_ref, core_ref, parts_ref, stream_ref, own_ref, other_ref):
    partial = parts_ref[0].astype(F32)
    for j in range(1, parts_ref.shape[0]):
        partial = partial + parts_ref[j].astype(F32)
    finished = (stream_ref[...].astype(F32) + partial).astype(BF16)
    rows = finished.shape[0]
    slots = own_ref.shape[1]
    z = z_ref[0]
    for side, out_ref in enumerate((own_ref, other_ref)):
        core = core_ref[0] ^ side

        def source(r):
            m = r % slots - side * micro
            inside = jnp.logical_and(m >= 0, m < micro)
            return jnp.where(inside, (2 * ((r // slots) ^ z) + core) * micro + m, -1)

        spread = one_hot((z_count * slots, rows), source).astype(BF16)
        sorted_rows = jnp.dot(spread, finished, preferred_element_type=F32)
        out_ref[...] = sorted_rows.reshape(z_count, slots, sorted_rows.shape[1]).astype(BF16)


def finish(z, core, parts, stream, z_count, micro):
    slots = -(-2 * micro // 8) * 8
    shape = jax.ShapeDtypeStruct((z_count, slots, stream.shape[1]), BF16)
    return pl.pallas_call(
        functools.partial(finish_kernel, z_count, micro),
        out_shape=(shape, shape),
        in_specs=[scalars(), scalars(), whole(), whole()],
        out_specs=(whole(), whole()),
        compiler_params=params(8),
        name="finish",
    )(z, core, parts, stream)


def join_kernel(micro, own_ref, other_ref, *out_refs):
    for k, out_ref in enumerate(out_refs):
        own = own_ref[k].astype(F32)
        row = lax.broadcasted_iota(jnp.int32, own.shape, 0)
        out_ref[...] = jnp.where(row < micro, own, other_ref[k].astype(F32)).astype(BF16)


def join(own, other, micro):
    count, rows, width = own.shape
    return pl.pallas_call(
        functools.partial(join_kernel, micro),
        out_shape=[jax.ShapeDtypeStruct((rows, width), BF16)] * count,
        in_specs=[whole(), whole()],
        out_specs=[whole()] * count,
        compiler_params=params(8),
        name="join",
    )(own, other)


def place_kernel(z_ref, core_ref, *refs):
    *piece_refs, out_ref = refs
    width = piece_refs[0].shape[1]
    micro = out_ref.shape[0]
    for k, ref in enumerate(piece_refs):
        block = ref[...].astype(F32)
        for side in range(2):
            share = 2 * (z_ref[0] ^ k) + (core_ref[0] ^ side)
            at = pl.multiple_of(share * width, LANES)
            out_ref[:, pl.ds(at, width)] = block[side * micro : (side + 1) * micro].astype(BF16)


def place(z, core, pieces, micro):
    width = pieces[0].shape[1]
    return pl.pallas_call(
        place_kernel,
        out_shape=jax.ShapeDtypeStruct((micro, 2 * len(pieces) * width), BF16),
        in_specs=[scalars(), scalars()] + [whole()] * len(pieces),
        out_specs=whole(),
        compiler_params=params(8),
        name="place",
    )(z, core, *pieces)


def along_z(array, hop):
    return lax.ppermute(array, Z, [(i, i ^ hop) for i in range(lax.axis_size(Z))])


def swap_cores(array):
    return lax.ppermute(array, CORE, [(0, 1), (1, 0)])


def per_device(
    hidden_in,
    queries,
    key_cache,
    value_cache,
    lengths,
    cache_slot,
    out_weight,
    ffn_gain,
    gate_weight,
    up_weight,
    down_weight,
):
    z_count = lax.axis_size(Z)
    core_count = lax.axis_size(CORE)
    attn_count = z_count * core_count
    ffn_count = lax.axis_size("x") * lax.axis_size("y")
    f_index = lax.axis_index(FFN).astype(jnp.int32)[None]
    z_index = lax.axis_index(Z).astype(jnp.int32)[None]
    core_index = lax.axis_index(CORE).astype(jnp.int32)[None]
    micro, total_rows, col_share = hidden_in.shape
    head_dim = key_cache.shape[2]
    model_width = col_share * attn_count
    hidden_share = gate_weight.shape[1]
    rows_chunk = attn_count * micro
    rows_all = ffn_count * rows_chunk
    rows_block = rows_all // attn_count

    payload = attend(
        queries.reshape(micro, -1), key_cache, value_cache, cache_slot.T, lengths.T, z_count, ffn_count
    )
    tile_rows = payload.shape[3]
    payload, f_index, z_index, core_index = lax.optimization_barrier((payload, f_index, z_index, core_index))
    payload = payload.reshape(z_count * ffn_count, micro * tile_rows, LANES)
    incoming = lax.all_to_all(payload, (Z,) + FFN, split_axis=0, concat_axis=0, tiled=True)
    own_rows = to_rows(incoming.reshape(z_count * ffn_count * micro, tile_rows, LANES), head_dim // LANES)
    own_rows, ffn_gain = lax.optimization_barrier((own_rows, ffn_gain))
    other_rows = swap_cores(own_rows)
    gain = ffn_gain[None, :]
    own_mixed = product_of([own_rows], out_weight)
    own_mixed, other_rows, gain = lax.optimization_barrier((own_mixed, other_rows, gain))
    mixed = mix(core_index, own_mixed, other_rows, out_weight, (core_count, z_count, ffn_count, micro))

    parts = lax.all_to_all(
        mixed.reshape(ffn_count, rows_chunk, col_share), FFN, split_axis=0, concat_axis=0, tiled=True
    )
    stream, copies = make_stream(
        f_index, parts, hidden_in.reshape(rows_all, col_share), (attn_count, ffn_count, micro)
    )
    stream_all = lax.all_to_all(copies, FFN, split_axis=0, concat_axis=0, tiled=True)
    stream_all = stream_all.reshape(rows_all, col_share)

    up_args = (gain, gate_weight, up_weight, rows_block)
    far_own, far_other = up_part((2, 3), z_index, core_index, stream_all, *up_args)
    _, squares_at = tile_places(hidden_share // LANES, rows_block)
    direct2, relayed2, direct3, relayed3 = add_far(far_own, swap_cores(far_other), squares_at)
    relayed3, stream_near = lax.optimization_barrier((relayed3, stream_all))
    crossing = along_z(relayed3, 1)
    from_direct3 = along_z(direct3, 3)
    from_direct2 = along_z(direct2, 2)
    near_own, near_other = up_part((0, 1), z_index, core_index, stream_near, *up_args)
    relayed2, near_own, from_direct2, from_direct3 = lax.optimization_barrier(
        (relayed2, near_own, from_direct2, from_direct3)
    )
    relayed = add_relayed(relayed2, crossing)
    near0, near1 = add_near(near_own, swap_cores(near_other), squares_at)
    relayed, near1 = lax.optimization_barrier((relayed, near1))
    from_relayed = along_z(relayed, 2)
    from_near = along_z(near1, 1)
    activated = activate(
        (near0, from_near, from_direct2, from_direct3, from_relayed), rows_block, hidden_share, model_width
    )

    far = along_z(activated, 2)
    near = along_z(activated, 1)
    first_lowered = product_of([activated, swap_cores(activated)], down_weight)
    far, first_lowered = lax.optimization_barrier((far, first_lowered))
    own_pieces = [near, far, along_z(far, 1)]
    other_pieces = [swap_cores(piece) for piece in own_pieces]
    own_lowered = product_of(own_pieces, down_weight)
    lowered = down(z_index, core_index, first_lowered, own_lowered, other_pieces, down_weight)
    lowered_parts = lax.all_to_all(
        lowered.reshape(ffn_count, rows_chunk, col_share), FFN, split_axis=0, concat_axis=0, tiled=True
    )
    own_share, other_share = finish(z_index, core_index, lowered_parts, stream, z_count, micro)
    shares = join(own_share, swap_cores(other_share), micro)
    pieces = [shares[0]] + [along_z(shares[hop], hop) for hop in range(1, z_count)]
    return place(z_index, core_index, pieces, micro).reshape(micro, 1, model_width)


def solution(mesh):
    sizes = dict(mesh.shape)
    attn_count, ffn_count, rep_count = sizes["attn"], sizes["ffn"], sizes["rep"]
    side = int(round(ffn_count**0.5))
    fine = Mesh(
        mesh.devices.reshape(attn_count // 2, 2, side, ffn_count // side, rep_count),
        (Z, CORE, "x", "y", REP),
    )
    owners = (REP, Z, CORE, "x", "y")
    return jax.shard_map(
        per_device,
        mesh=fine,
        in_specs=(
            P(None, REP, ATTN),
            P(None, owners, None),
            P(owners, None, None),
            P(owners, None, None),
            P(None, owners),
            P(None, owners),
            P(FFN, ATTN),
            P(ATTN),
            P(ATTN, FFN),
            P(ATTN, FFN),
            P(FFN, ATTN),
        ),
        out_specs=P(None, owners, None),
        check_vma=False,
    )
```

```python
import functools

import jax
import jax.numpy as jnp
from jax import lax
from jax.experimental import pallas as pl
from jax.experimental.pallas import tpu as pltpu
from jax.sharding import Mesh, PartitionSpec as P

EPSILON = 1e-06
MASKED = -1e30
Z = "z"
CORE = "core"
ATTN = (Z, CORE)
FFN = ("x", "y")
REP = "rep"
LANES = 128
SQ_ROWS = 16
FEW = 16
BF16 = jnp.bfloat16
F32 = jnp.float32
HEAVY = pl.CostEstimate(flops=10**10, bytes_accessed=10**7, transcendentals=0)


def whole():
    return pl.BlockSpec(memory_space=pltpu.VMEM)


def scalars():
    return pl.BlockSpec(memory_space=pltpu.SMEM)


def in_hbm():
    return pl.BlockSpec(memory_space=pltpu.HBM)


def params(mib):
    return pltpu.CompilerParams(vmem_limit_bytes=mib * 1024 * 1024)


def one_hot(shape, source_of_row):
    rows = lax.broadcasted_iota(jnp.int32, shape, 0)
    cols = lax.broadcasted_iota(jnp.int32, shape, 1)
    return jnp.where(cols == source_of_row(rows), 1.0, 0.0)


def attention_kernel(
    slot_hbm,
    length_hbm,
    query_hbm,
    key_hbm,
    value_hbm,
    out_ref,
    slots,
    lengths,
    queries,
    keys,
    values,
    wide,
    small_sem,
    key_sem,
    value_sem,
):
    slot_count, pos, head_dim = keys.shape
    micro, width = queries.shape
    heads = width // head_dim
    copies, blocks, _, tile_rows, _ = out_ref.shape
    small = [
        pltpu.make_async_copy(source, target, small_sem.at[i])
        for i, (source, target) in enumerate(((query_hbm, queries), (slot_hbm, slots), (length_hbm, lengths)))
    ]
    key_copies = [pltpu.make_async_copy(key_hbm.at[s], keys.at[s], key_sem.at[s]) for s in range(slot_count)]
    value_copies = [pltpu.make_async_copy(value_hbm.at[s], values.at[s], value_sem.at[s]) for s in range(slot_count)]
    for copy in small + key_copies + value_copies:
        copy.start()
    for copy in small:
        copy.wait()
    for h in range(heads):
        wide[:, h, :] = queries[:, h * head_dim : (h + 1) * head_dim].astype(F32)
    pieces = head_dim // LANES
    group = heads // blocks
    positions = lax.broadcasted_iota(jnp.int32, (heads, pos), 1)
    softened = []
    totals = []
    for copy in key_copies:
        copy.wait()
    for m in range(micro):
        scores = lax.dot_general(
            wide[m].astype(BF16), keys[slots[0, m]], (((1,), (1,)), ((), ())), preferred_element_type=F32
        ) * head_dim ** (-0.5)
        in_cache = positions < lengths[0, m]
        scores = jnp.where(in_cache, scores, MASKED)
        highest = jnp.max(scores, axis=1, keepdims=True)
        weights = jnp.where(in_cache, jnp.exp(scores - highest), 0.0)
        totals.append(jnp.sum(weights, axis=1, keepdims=True))
        softened.append(weights.astype(BF16))
    for copy in value_copies:
        copy.wait()
    for m in range(micro):
        weighted = jnp.dot(softened[m], values[slots[0, m]], preferred_element_type=F32)
        attended = weighted / totals[m]
        for piece in range(pieces):
            part = attended[:, piece * LANES : (piece + 1) * LANES].reshape(blocks, group, LANES).astype(BF16)
            for copy in range(copies):
                out_ref[copy, :, m, piece * group : (piece + 1) * group, :] = part


def attend(queries, key_cache, value_cache, slots, lengths, z_count, ffn_count):
    slot_count, pos, head_dim = key_cache.shape
    micro, width = queries.shape
    tile_rows = width // ffn_count // LANES
    return pl.pallas_call(
        attention_kernel,
        in_specs=[in_hbm()] * 5,
        out_specs=whole(),
        out_shape=jax.ShapeDtypeStruct((z_count, ffn_count, micro, tile_rows, LANES), BF16),
        scratch_shapes=[
            pltpu.SMEM(slots.shape, jnp.int32),
            pltpu.SMEM(lengths.shape, jnp.int32),
            pltpu.VMEM(queries.shape, BF16),
            pltpu.VMEM((slot_count, pos, head_dim), BF16),
            pltpu.VMEM((slot_count, pos, head_dim), BF16),
            pltpu.VMEM((micro, width // head_dim, head_dim), F32),
            pltpu.SemaphoreType.DMA((3,)),
            pltpu.SemaphoreType.DMA((slot_count,)),
            pltpu.SemaphoreType.DMA((slot_count,)),
        ],
        compiler_params=params(60),
        name="attention",
    )(slots, lengths, queries, key_cache, value_cache)


def spread_shares(order, own, other, source):
    z_count, _, ffn_count, micro = order
    count = own.shape[0]

    def place_of(r):
        m = r % micro
        z = (r // micro) % z_count
        share = (r // (micro * z_count)) % 2
        f = r // (micro * z_count * 2)
        return share * count + source(z, f, m)

    spread = one_hot((2 * count, 2 * count), place_of).astype(BF16)
    return jnp.dot(spread, jnp.concatenate([own, other], axis=0), preferred_element_type=F32).astype(BF16)


def rows_kernel(pieces, in_ref, out_ref, wide):
    rows, tile_rows, lanes = in_ref.shape
    wide[...] = in_ref[...].astype(F32).reshape(rows * tile_rows, lanes)
    group = tile_rows // pieces
    for j in range(tile_rows):
        at = (j % pieces) * group + j // pieces
        out_ref[:, j * lanes : (j + 1) * lanes] = wide[pl.ds(at, rows, stride=tile_rows), :].astype(BF16)


def to_rows(tiles, pieces):
    rows, tile_rows, lanes = tiles.shape
    return pl.pallas_call(
        functools.partial(rows_kernel, pieces),
        out_shape=jax.ShapeDtypeStruct((rows, tile_rows * lanes), BF16),
        in_specs=[whole()],
        out_specs=whole(),
        scratch_shapes=[pltpu.VMEM((rows * tile_rows, lanes), F32)],
        compiler_params=params(8),
        name="to_rows",
    )(tiles)


def product_kernel(rows_ref, weight_ref, out_ref):
    out_ref[...] = jnp.dot(rows_ref[...], weight_ref[...], preferred_element_type=F32).astype(BF16)


def product_of(rows, weight):
    return pl.pallas_call(
        product_kernel,
        out_shape=jax.ShapeDtypeStruct((rows.shape[0], weight.shape[1]), BF16),
        in_specs=[whole(), whole()],
        out_specs=whole(),
        compiler_params=params(12),
        cost_estimate=HEAVY,
        name="product",
    )(rows, weight)


def mix_kernel(order, core_ref, own_ref, rows_ref, weight_ref, out_ref):
    z_count, core_count, ffn_count, micro = order
    total = 2 * rows_ref.shape[0]
    product = jnp.dot(rows_ref[...], weight_ref[...], preferred_element_type=F32).astype(BF16)
    core = core_ref[0]

    def source(r):
        m = r % micro
        c = (r // micro) % core_count
        z = (r // (micro * core_count)) % z_count
        f = r // (micro * core_count * z_count)
        return (((c ^ core) * z_count + z) * ffn_count + f) * micro + m

    spread = one_hot((total, total), source).astype(BF16)
    both = jnp.concatenate([own_ref[...], product], axis=0)
    out_ref[...] = jnp.dot(spread, both, preferred_element_type=F32).astype(BF16)


def mix(core, own, rows, weight, order):
    return pl.pallas_call(
        functools.partial(mix_kernel, order),
        out_shape=jax.ShapeDtypeStruct((2 * rows.shape[0], weight.shape[1]), BF16),
        in_specs=[scalars(), whole(), whole(), whole()],
        out_specs=whole(),
        compiler_params=params(12),
        name="mix",
    )(core, own, rows, weight)


def down_kernel(order, z_ref, *refs):
    *piece_refs, own_ref, other_ref, out_ref = refs
    _, _, ffn_count, micro = order
    rows = jnp.concatenate([ref[...] for ref in piece_refs], axis=0)
    own = jnp.dot(rows, own_ref[...], preferred_element_type=F32).astype(BF16)
    other = jnp.dot(rows, other_ref[...], preferred_element_type=F32).astype(BF16)
    me = z_ref[0]
    out_ref[...] = spread_shares(order, own, other, lambda z, f, m: ((z ^ me) * ffn_count + f) * micro + m)


def down(z, pieces, own_weight, other_weight, order):
    rows = len(pieces) * pieces[0].shape[0]
    return pl.pallas_call(
        functools.partial(down_kernel, order),
        out_shape=jax.ShapeDtypeStruct((2 * rows, own_weight.shape[1]), BF16),
        in_specs=[scalars()] + [whole()] * (len(pieces) + 2),
        out_specs=whole(),
        compiler_params=params(16),
        name="down",
    )(z, *pieces, own_weight, other_weight)


def fetch_kernel(cuts, *refs):
    count = (len(refs) - 1) // 2
    sources, targets, sems = refs[:count], refs[count : 2 * count], refs[2 * count]
    copies = []
    for i in range(count):
        rows = sources[i].shape[0] // cuts
        for j in range(cuts):
            part = pl.ds(j * rows, rows)
            copies.append(pltpu.make_async_copy(sources[i].at[part], targets[i].at[part], sems.at[i * cuts + j]))
    for copy in copies:
        copy.start()
    for copy in copies:
        copy.wait()


def fetch(*arrays):
    cuts = 4
    return pl.pallas_call(
        functools.partial(fetch_kernel, cuts),
        out_shape=[jax.ShapeDtypeStruct(array.shape, array.dtype) for array in arrays],
        in_specs=[in_hbm()] * len(arrays),
        out_specs=[whole()] * len(arrays),
        scratch_shapes=[pltpu.SemaphoreType.DMA((len(arrays) * cuts,))],
        compiler_params=params(16),
        cost_estimate=HEAVY,
        name="fetch",
    )(*arrays)


def sum_parts(parts_ref):
    total = parts_ref[0].astype(F32)
    for j in range(1, parts_ref.shape[0]):
        total = total + parts_ref[j].astype(F32)
    return total


def stream_kernel(order, f_ref, core_ref, parts_ref, hidden_ref, stream_ref, send_ref, copies_ref):
    z_count, core_count, ffn_count, micro = order
    rows = stream_ref.shape[0]
    f = f_ref[0]

    def source(r):
        return ((r % micro) * z_count * core_count + r // micro) * ffn_count + f

    spread = one_hot((rows, hidden_ref.shape[0]), source).astype(BF16)
    hidden = jnp.dot(spread, hidden_ref[...], preferred_element_type=F32)
    stream = (hidden + sum_parts(parts_ref)).astype(BF16)
    stream_ref[...] = stream
    for j in range(copies_ref.shape[0]):
        copies_ref[j] = stream

    def other(r):
        row = ((r // micro) * core_count + 1 - core_ref[0]) * micro + r % micro
        return jnp.where(r < z_count * micro, row, -1)

    pick = one_hot((FEW, rows), other).astype(BF16)
    send_ref[...] = jnp.dot(pick, stream, preferred_element_type=F32).astype(BF16)


def make_stream(f, core, parts, hidden, order):
    _, rows, width = parts.shape
    return pl.pallas_call(
        functools.partial(stream_kernel, order),
        out_shape=(
            jax.ShapeDtypeStruct((rows, width), BF16),
            jax.ShapeDtypeStruct((FEW, width), BF16),
            jax.ShapeDtypeStruct(parts.shape, BF16),
        ),
        in_specs=[scalars()] * 2 + [whole()] * 2,
        out_specs=(whole(), whole(), whole()),
        compiler_params=params(8),
        name="make_stream",
    )(f, core, parts, hidden)


def squares_rows(row_values, width):
    high = row_values.astype(BF16).astype(F32)
    low = row_values - high
    index = lax.broadcasted_iota(jnp.int32, (SQ_ROWS, width), 0)
    return jnp.where(index == 0, high, jnp.where(index == 1, low, 0.0)).astype(BF16)


def up_kernel(order, hops, z_ref, core_ref, stream_ref, gain_ref, gate_ref, up_ref, *out_refs):
    z_count, core_count, ffn_count, micro = order
    tiles = gate_ref.shape[1] // LANES
    rows = ffn_count * micro
    me = z_ref[0]
    core = core_ref[0]

    def source(r):
        m = r % micro
        f = (r // micro) % ffn_count
        block = r // rows
        side = block // len(hops)
        hop = hops[0] + block % len(hops)
        return ((f * z_count + (me ^ hop)) * core_count + (core ^ side)) * micro + m

    spread = one_hot((len(out_refs) * rows, stream_ref.shape[0]), source).astype(BF16)
    stream = jnp.dot(spread, stream_ref[...], preferred_element_type=F32)
    scaled = (stream * gain_ref[...].astype(F32)).astype(BF16)
    squares = jnp.sum(stream * stream, axis=1, keepdims=True)
    lane = one_hot((rows, LANES), lambda r: r)
    for i, out_ref in enumerate(out_refs):
        sums = jnp.sum(lane * squares[i * rows : (i + 1) * rows], axis=0, keepdims=True)
        out_ref[2 * tiles * rows :, :] = squares_rows(sums, LANES)
    for half, weight_ref in enumerate((gate_ref, up_ref)):
        product = jnp.dot(scaled, weight_ref[...], preferred_element_type=F32).astype(BF16)
        for i, out_ref in enumerate(out_refs):
            for j in range(tiles):
                at = (half * tiles + j) * rows
                out_ref[at : at + rows, :] = product[i * rows : (i + 1) * rows, j * LANES : (j + 1) * LANES]


def up_part(order, hops, z, core, stream_all, gain, gate_weight, up_weight):
    _, _, ffn_count, micro = order
    out_rows = 2 * gate_weight.shape[1] // LANES * ffn_count * micro + SQ_ROWS
    shape = jax.ShapeDtypeStruct((out_rows, LANES), BF16)
    return pl.pallas_call(
        functools.partial(up_kernel, order, hops),
        out_shape=[shape] * (2 * len(hops)),
        in_specs=[scalars(), scalars(), whole(), whole(), whole(), whole()],
        out_specs=[whole()] * (2 * len(hops)),
        compiler_params=params(16),
        cost_estimate=HEAVY,
        name="up_part",
    )(z, core, stream_all, gain, gate_weight, up_weight)


def sum_blocks(refs, start, stop):
    total = refs[0][start:stop, :].astype(F32)
    for ref in refs[1:]:
        total = total + ref[start:stop, :].astype(F32)
    return total


def add_kernel(*refs):
    *block_refs, out_ref = refs
    out_rows, lanes = out_ref.shape
    body = out_rows - SQ_ROWS
    out_ref[:body, :] = sum_blocks(block_refs, 0, body).astype(BF16)
    tail = sum_blocks(block_refs, body, out_rows)
    out_ref[body:, :] = squares_rows(tail[0:1] + tail[1:2], lanes)


def add(*blocks):
    return pl.pallas_call(
        add_kernel,
        out_shape=jax.ShapeDtypeStruct(blocks[0].shape, BF16),
        in_specs=[whole()] * len(blocks),
        out_specs=whole(),
        compiler_params=params(8),
        name="add",
    )(*blocks)


def activate_kernel(model_width, *refs):
    *block_refs, out_ref = refs
    out_rows, lanes = block_refs[0].shape
    rows, hidden = out_ref.shape
    tiles = hidden // lanes
    tail = sum_blocks(block_refs, out_rows - SQ_ROWS, out_rows)
    lane_sums = tail[0:1] + tail[1:2]
    spread = one_hot((rows, lanes), lambda r: r)
    squares = jnp.sum(spread * lane_sums, axis=1, keepdims=True)
    scale = lax.rsqrt(squares / model_width + EPSILON)
    for j in range(tiles):
        gate = sum_blocks(block_refs, j * rows, (j + 1) * rows) * scale
        upward = sum_blocks(block_refs, (tiles + j) * rows, (tiles + j + 1) * rows) * scale
        out_ref[:, j * lanes : (j + 1) * lanes] = (gate / (1.0 + jnp.exp(-gate)) * upward).astype(BF16)


def activate(blocks, rows, hidden, model_width):
    return pl.pallas_call(
        functools.partial(activate_kernel, model_width),
        out_shape=jax.ShapeDtypeStruct((rows, hidden), BF16),
        in_specs=[whole()] * len(blocks),
        out_specs=whole(),
        compiler_params=params(8),
        name="activate",
    )(*blocks)


def finish_kernel(order, z_ref, core_ref, parts_ref, stream_ref, received_ref, *out_refs):
    z_count, core_count, _, micro = order
    rows = stream_ref.shape[0]
    half = rows // 2

    def own(r):
        return jnp.where(r < half, ((r // micro) * core_count + core_ref[0]) * micro + r % micro, -1)

    first = one_hot((rows, rows), own).astype(BF16)
    second = one_hot((rows, FEW), lambda r: r - half).astype(BF16)
    stream = jnp.dot(first, stream_ref[...], preferred_element_type=F32)
    stream = stream + jnp.dot(second, received_ref[...], preferred_element_type=F32)
    finished = (stream + sum_parts(parts_ref)).astype(BF16)
    slots = out_refs[0].shape[0]
    me = z_ref[0]

    def source(r):
        q = r % slots
        at = (q // micro) * half + ((r // slots) ^ me) * micro + q % micro
        return jnp.where(q < 2 * micro, at, -1)

    spread = one_hot((len(out_refs) * slots, rows), source).astype(BF16)
    blocks = jnp.dot(spread, finished, preferred_element_type=F32)
    for k, out_ref in enumerate(out_refs):
        out_ref[...] = blocks[k * slots : (k + 1) * slots].astype(BF16)


def finish(z, core, parts, stream, received, order):
    z_count, _, _, micro = order
    slots = -(-2 * micro // 8) * 8
    return pl.pallas_call(
        functools.partial(finish_kernel, order),
        out_shape=[jax.ShapeDtypeStruct((slots, stream.shape[1]), BF16)] * z_count,
        in_specs=[scalars()] * 2 + [whole()] * 3,
        out_specs=[whole()] * z_count,
        compiler_params=params(8),
        name="finish",
    )(z, core, parts, stream, received)


def place_kernel(z_ref, core_ref, *refs):
    *piece_refs, out_ref = refs
    width = piece_refs[0].shape[1]
    micro = out_ref.shape[0]
    for k, ref in enumerate(piece_refs):
        block = ref[...].astype(F32)
        for side in range(2):
            share = 2 * (z_ref[0] ^ k) + (core_ref[0] ^ side)
            at = pl.multiple_of(share * width, LANES)
            out_ref[:, pl.ds(at, width)] = block[side * micro : (side + 1) * micro].astype(BF16)


def place(z, core, pieces, micro):
    width = pieces[0].shape[1]
    return pl.pallas_call(
        place_kernel,
        out_shape=jax.ShapeDtypeStruct((micro, 2 * len(pieces) * width), BF16),
        in_specs=[scalars(), scalars()] + [whole()] * len(pieces),
        out_specs=whole(),
        compiler_params=params(8),
        name="place",
    )(z, core, *pieces)


def along_z(array, hop):
    return lax.ppermute(array, Z, [(i, i ^ hop) for i in range(lax.axis_size(Z))])


def swap_cores(array):
    return lax.ppermute(array, CORE, [(0, 1), (1, 0)])


def per_device(
    hidden_in,
    queries,
    key_cache,
    value_cache,
    lengths,
    cache_slot,
    out_weight,
    ffn_gain,
    gate_weight,
    up_weight,
    down_weight,
):
    z_count = lax.axis_size(Z)
    core_count = lax.axis_size(CORE)
    attn_count = z_count * core_count
    ffn_count = lax.axis_size("x") * lax.axis_size("y")
    f_index = lax.axis_index(FFN).astype(jnp.int32)[None]
    z_index = lax.axis_index(Z).astype(jnp.int32)[None]
    core_index = lax.axis_index(CORE).astype(jnp.int32)[None]
    micro, total_rows, col_share = hidden_in.shape
    head_dim = key_cache.shape[2]
    model_width = col_share * attn_count
    hidden_share = gate_weight.shape[1]
    rows_chunk = attn_count * micro
    rows_all = ffn_count * rows_chunk
    rows_block = rows_all // attn_count

    order = (z_count, core_count, ffn_count, micro)
    payload = attend(
        queries.reshape(micro, -1), key_cache, value_cache, cache_slot.T, lengths.T, z_count, ffn_count
    )
    tile_rows = payload.shape[3]
    payload, f_index, z_index, core_index = lax.optimization_barrier((payload, f_index, z_index, core_index))
    payload = payload.reshape(z_count * ffn_count, micro * tile_rows, LANES)
    incoming = lax.all_to_all(payload, (Z,) + FFN, split_axis=0, concat_axis=0, tiled=True)
    own_rows = to_rows(incoming.reshape(z_count * ffn_count * micro, tile_rows, LANES), head_dim // LANES)
    own_rows, ffn_gain = lax.optimization_barrier((own_rows, ffn_gain))
    other_rows = swap_cores(own_rows)
    gain = ffn_gain[None, :]
    own_mixed = product_of(own_rows, out_weight)
    own_mixed, other_rows, gain = lax.optimization_barrier((own_mixed, other_rows, gain))
    mixed = mix(core_index, own_mixed, other_rows, out_weight, order)

    parts = lax.all_to_all(
        mixed.reshape(ffn_count, rows_chunk, col_share), FFN, split_axis=0, concat_axis=0, tiled=True
    )
    stream, send, copies = make_stream(f_index, core_index, parts, hidden_in.reshape(rows_all, col_share), order)
    stream_all = lax.all_to_all(copies, FFN, split_axis=0, concat_axis=0, tiled=True)
    stream_all = stream_all.reshape(rows_all, col_share)

    up_args = (gain, gate_weight, up_weight)
    own2, own3, other2, other3 = up_part(order, (2, 3), z_index, core_index, stream_all, *up_args)
    own0, own1, other0, other1 = up_part(order, (0, 1), z_index, core_index, stream_all, *up_args)
    received3, own0 = lax.optimization_barrier((swap_cores(other3), own0))
    relayed3 = add(own3, received3)
    relayed3, other0, other1, other2 = lax.optimization_barrier((relayed3, other0, other1, other2))
    crossing = along_z(relayed3, 1)
    near1 = add(own1, swap_cores(other1))
    received2, near1 = lax.optimization_barrier((swap_cores(other2), near1))
    relayed = add(own2, received2, crossing)
    relayed, down_weight, send = lax.optimization_barrier((relayed, down_weight, send))
    from_far = along_z(relayed, 2)
    from_near = along_z(near1, 1)
    down_other = swap_cores(down_weight)
    activated = activate(
        (own0, swap_cores(other0), from_near, from_far), rows_block, hidden_share, model_width
    )

    far = along_z(activated, 2)
    near = along_z(activated, 1)
    far, down_other, received = lax.optimization_barrier((far, down_other, swap_cores(send)))
    farthest = along_z(far, 1)
    down_own, down_other = fetch(down_weight, down_other)
    lowered = down(z_index, (activated, near, far, farthest), down_own, down_other, order)
    lowered_parts = lax.all_to_all(
        lowered.reshape(ffn_count, rows_chunk, col_share), FFN, split_axis=0, concat_axis=0, tiled=True
    )
    shares = finish(z_index, core_index, lowered_parts, stream, received, order)
    pieces = [shares[0]] + [along_z(shares[hop], hop) for hop in range(1, z_count)]
    return place(z_index, core_index, pieces, micro).reshape(micro, 1, model_width)


def solution(mesh):
    sizes = dict(mesh.shape)
    attn_count, ffn_count, rep_count = sizes["attn"], sizes["ffn"], sizes["rep"]
    side = int(round(ffn_count**0.5))
    fine = Mesh(
        mesh.devices.reshape(attn_count // 2, 2, side, ffn_count // side, rep_count),
        (Z, CORE, "x", "y", REP),
    )
    owners = (REP, Z, CORE, "x", "y")
    return jax.shard_map(
        per_device,
        mesh=fine,
        in_specs=(
            P(None, REP, ATTN),
            P(None, owners, None),
            P(owners, None, None),
            P(owners, None, None),
            P(None, owners),
            P(None, owners),
            P(FFN, ATTN),
            P(ATTN),
            P(ATTN, FFN),
            P(ATTN, FFN),
            P(FFN, ATTN),
        ),
        out_specs=P(None, owners, None),
        check_vma=False,
    )
```

```python
import functools

import jax
import jax.numpy as jnp
from jax import lax
from jax.experimental import pallas as pl
from jax.experimental.pallas import tpu as pltpu
from jax.sharding import Mesh, PartitionSpec as P

EPSILON = 1e-06
MASKED = -1e30
Z = "z"
CORE = "core"
ATTN = (Z, CORE)
FFN = ("x", "y")
REP = "rep"
LANES = 128
SQ_ROWS = 16
FEW = 16
BF16 = jnp.bfloat16
F32 = jnp.float32
HEAVY = pl.CostEstimate(flops=10**10, bytes_accessed=10**7, transcendentals=0)


def whole():
    return pl.BlockSpec(memory_space=pltpu.VMEM)


def scalars():
    return pl.BlockSpec(memory_space=pltpu.SMEM)


def in_hbm():
    return pl.BlockSpec(memory_space=pltpu.HBM)


def params(mib):
    return pltpu.CompilerParams(vmem_limit_bytes=mib * 1024 * 1024)


def one_hot(shape, source_of_row):
    rows = lax.broadcasted_iota(jnp.int32, (shape[0], 1), 0)
    cols = lax.broadcasted_iota(jnp.int32, shape, 1)
    return jnp.where(cols == source_of_row(rows), 1.0, 0.0)


def attention_kernel(
    slot_hbm,
    length_hbm,
    query_hbm,
    key_hbm,
    value_hbm,
    out_ref,
    slots,
    lengths,
    queries,
    keys,
    values,
    wide,
    small_sem,
    key_sem,
    value_sem,
):
    slot_count, pos, head_dim = keys.shape
    micro, width = queries.shape
    heads = width // head_dim
    copies, blocks, _, tile_rows, _ = out_ref.shape
    small = [
        pltpu.make_async_copy(source, target, small_sem.at[i])
        for i, (source, target) in enumerate(((query_hbm, queries), (slot_hbm, slots), (length_hbm, lengths)))
    ]
    key_copies = [pltpu.make_async_copy(key_hbm.at[s], keys.at[s], key_sem.at[s]) for s in range(slot_count)]
    value_copies = [pltpu.make_async_copy(value_hbm.at[s], values.at[s], value_sem.at[s]) for s in range(slot_count)]
    for copy in small + key_copies + value_copies:
        copy.start()
    for copy in small:
        copy.wait()
    for h in range(heads):
        wide[:, h, :] = queries[:, h * head_dim : (h + 1) * head_dim].astype(F32)
    pieces = head_dim // LANES
    group = heads // blocks
    positions = lax.broadcasted_iota(jnp.int32, (heads, pos), 1)
    softened = []
    totals = []
    for copy in key_copies:
        copy.wait()
    for m in range(micro):
        scores = lax.dot_general(
            wide[m].astype(BF16), keys[slots[0, m]], (((1,), (1,)), ((), ())), preferred_element_type=F32
        ) * head_dim ** (-0.5)
        in_cache = positions < lengths[0, m]
        scores = jnp.where(in_cache, scores, MASKED)
        highest = jnp.max(scores, axis=1, keepdims=True)
        weights = jnp.where(in_cache, jnp.exp(scores - highest), 0.0)
        totals.append(jnp.sum(weights, axis=1, keepdims=True))
        softened.append(weights.astype(BF16))
    for copy in value_copies:
        copy.wait()
    for m in range(micro):
        weighted = jnp.dot(softened[m], values[slots[0, m]], preferred_element_type=F32)
        attended = weighted / totals[m]
        for piece in range(pieces):
            part = attended[:, piece * LANES : (piece + 1) * LANES].reshape(blocks, group, LANES).astype(BF16)
            for copy in range(copies):
                out_ref[copy, :, m, piece * group : (piece + 1) * group, :] = part


def attend(queries, key_cache, value_cache, slots, lengths, z_count, ffn_count):
    slot_count, pos, head_dim = key_cache.shape
    micro, width = queries.shape
    tile_rows = width // ffn_count // LANES
    return pl.pallas_call(
        attention_kernel,
        in_specs=[in_hbm()] * 5,
        out_specs=whole(),
        out_shape=jax.ShapeDtypeStruct((z_count, ffn_count, micro, tile_rows, LANES), BF16),
        scratch_shapes=[
            pltpu.SMEM(slots.shape, jnp.int32),
            pltpu.SMEM(lengths.shape, jnp.int32),
            pltpu.VMEM(queries.shape, BF16),
            pltpu.VMEM((slot_count, pos, head_dim), BF16),
            pltpu.VMEM((slot_count, pos, head_dim), BF16),
            pltpu.VMEM((micro, width // head_dim, head_dim), F32),
            pltpu.SemaphoreType.DMA((3,)),
            pltpu.SemaphoreType.DMA((slot_count,)),
            pltpu.SemaphoreType.DMA((slot_count,)),
        ],
        compiler_params=params(60),
        name="attention",
    )(slots, lengths, queries, key_cache, value_cache)


def spread_shares(order, own, other, source):
    z_count, _, ffn_count, micro = order
    count = own.shape[0]

    def place_of(r):
        m = r % micro
        z = (r // micro) % z_count
        share = (r // (micro * z_count)) % 2
        f = r // (micro * z_count * 2)
        return share * count + source(z, f, m)

    spread = one_hot((2 * count, 2 * count), place_of).astype(BF16)
    return jnp.dot(spread, jnp.concatenate([own, other], axis=0), preferred_element_type=F32).astype(BF16)


def rows_kernel(pieces, in_ref, out_ref, wide):
    rows, tile_rows, lanes = in_ref.shape
    wide[...] = in_ref[...].astype(F32).reshape(rows * tile_rows, lanes)
    group = tile_rows // pieces
    for j in range(tile_rows):
        at = (j % pieces) * group + j // pieces
        out_ref[:, j * lanes : (j + 1) * lanes] = wide[pl.ds(at, rows, stride=tile_rows), :].astype(BF16)


def to_rows(tiles, pieces):
    rows, tile_rows, lanes = tiles.shape
    return pl.pallas_call(
        functools.partial(rows_kernel, pieces),
        out_shape=jax.ShapeDtypeStruct((rows, tile_rows * lanes), BF16),
        in_specs=[whole()],
        out_specs=whole(),
        scratch_shapes=[pltpu.VMEM((rows * tile_rows, lanes), F32)],
        compiler_params=params(8),
        name="to_rows",
    )(tiles)


def product_kernel(rows_ref, weight_ref, out_ref):
    out_ref[...] = jnp.dot(rows_ref[...], weight_ref[...], preferred_element_type=F32).astype(BF16)


def product_of(rows, weight):
    return pl.pallas_call(
        product_kernel,
        out_shape=jax.ShapeDtypeStruct((rows.shape[0], weight.shape[1]), BF16),
        in_specs=[whole(), whole()],
        out_specs=whole(),
        compiler_params=params(12),
        cost_estimate=HEAVY,
        name="product",
    )(rows, weight)


def mix_kernel(order, core_ref, own_ref, rows_ref, weight_ref, out_ref):
    z_count, core_count, ffn_count, micro = order
    total = 2 * rows_ref.shape[0]
    product = jnp.dot(rows_ref[...], weight_ref[...], preferred_element_type=F32).astype(BF16)
    core = core_ref[0]

    def source(r):
        m = r % micro
        c = (r // micro) % core_count
        z = (r // (micro * core_count)) % z_count
        f = r // (micro * core_count * z_count)
        return (((c ^ core) * z_count + z) * ffn_count + f) * micro + m

    spread = one_hot((total, total), source).astype(BF16)
    both = jnp.concatenate([own_ref[...], product], axis=0)
    out_ref[...] = jnp.dot(spread, both, preferred_element_type=F32).astype(BF16)


def mix(core, own, rows, weight, order):
    return pl.pallas_call(
        functools.partial(mix_kernel, order),
        out_shape=jax.ShapeDtypeStruct((2 * rows.shape[0], weight.shape[1]), BF16),
        in_specs=[scalars(), whole(), whole(), whole()],
        out_specs=whole(),
        compiler_params=params(12),
        name="mix",
    )(core, own, rows, weight)


def down_most_kernel(*refs):
    *piece_refs, own_ref, other_ref, own_out_ref, other_out_ref = refs
    rows = jnp.concatenate([ref[...] for ref in piece_refs], axis=0)
    own_out_ref[...] = jnp.dot(rows, own_ref[...], preferred_element_type=F32).astype(BF16)
    other_out_ref[...] = jnp.dot(rows, other_ref[...], preferred_element_type=F32).astype(BF16)


def down_most(pieces, own_weight, other_weight):
    shape = jax.ShapeDtypeStruct((len(pieces) * pieces[0].shape[0], own_weight.shape[1]), BF16)
    return pl.pallas_call(
        down_most_kernel,
        out_shape=(shape, shape),
        in_specs=[whole()] * (len(pieces) + 2),
        out_specs=(whole(), whole()),
        compiler_params=params(16),
        cost_estimate=HEAVY,
        name="down_most",
    )(*pieces, own_weight, other_weight)


def down_kernel(order, z_ref, own_most_ref, other_most_ref, rows_ref, own_ref, other_ref, out_ref):
    _, _, ffn_count, micro = order
    shares = []
    for most_ref, weight_ref in ((own_most_ref, own_ref), (other_most_ref, other_ref)):
        last = jnp.dot(rows_ref[...], weight_ref[...], preferred_element_type=F32).astype(BF16)
        shares.append(jnp.concatenate([most_ref[...], last], axis=0))
    me = z_ref[0]
    out_ref[...] = spread_shares(order, *shares, lambda z, f, m: ((z ^ me) * ffn_count + f) * micro + m)


def down(z, most, last, own_weight, other_weight, order):
    rows = most[0].shape[0] + last.shape[0]
    return pl.pallas_call(
        functools.partial(down_kernel, order),
        out_shape=jax.ShapeDtypeStruct((2 * rows, own_weight.shape[1]), BF16),
        in_specs=[scalars()] + [whole()] * 5,
        out_specs=whole(),
        compiler_params=params(16),
        name="down",
    )(z, *most, last, own_weight, other_weight)


def fetch_kernel(cuts, *refs):
    count = (len(refs) - 1) // 2
    sources, targets, sems = refs[:count], refs[count : 2 * count], refs[2 * count]
    copies = []
    for i in range(count):
        rows = sources[i].shape[0] // cuts
        for j in range(cuts):
            part = pl.ds(j * rows, rows)
            copies.append(pltpu.make_async_copy(sources[i].at[part], targets[i].at[part], sems.at[i * cuts + j]))
    for copy in copies:
        copy.start()
    for copy in copies:
        copy.wait()


def fetch(*arrays):
    cuts = 4
    return pl.pallas_call(
        functools.partial(fetch_kernel, cuts),
        out_shape=[jax.ShapeDtypeStruct(array.shape, array.dtype) for array in arrays],
        in_specs=[in_hbm()] * len(arrays),
        out_specs=[whole()] * len(arrays),
        scratch_shapes=[pltpu.SemaphoreType.DMA((len(arrays) * cuts,))],
        compiler_params=params(16),
        cost_estimate=HEAVY,
        name="fetch",
    )(*arrays)


def sum_parts(parts_ref):
    total = parts_ref[0].astype(F32)
    for j in range(1, parts_ref.shape[0]):
        total = total + parts_ref[j].astype(F32)
    return total


def stream_kernel(order, f_ref, core_ref, parts_ref, hidden_ref, stream_ref, send_ref, copies_ref):
    z_count, core_count, ffn_count, micro = order
    rows = stream_ref.shape[0]
    f = f_ref[0]

    def source(r):
        return ((r % micro) * z_count * core_count + r // micro) * ffn_count + f

    spread = one_hot((rows, hidden_ref.shape[0]), source).astype(BF16)
    hidden = jnp.dot(spread, hidden_ref[...], preferred_element_type=F32)
    stream = (hidden + sum_parts(parts_ref)).astype(BF16)
    stream_ref[...] = stream
    for j in range(copies_ref.shape[0]):
        copies_ref[j] = stream

    def other(r):
        row = ((r // micro) * core_count + 1 - core_ref[0]) * micro + r % micro
        return jnp.where(r < z_count * micro, row, -1)

    pick = one_hot((FEW, rows), other).astype(BF16)
    send_ref[...] = jnp.dot(pick, stream, preferred_element_type=F32).astype(BF16)


def make_stream(f, core, parts, hidden, order):
    _, rows, width = parts.shape
    return pl.pallas_call(
        functools.partial(stream_kernel, order),
        out_shape=(
            jax.ShapeDtypeStruct((rows, width), BF16),
            jax.ShapeDtypeStruct((FEW, width), BF16),
            jax.ShapeDtypeStruct(parts.shape, BF16),
        ),
        in_specs=[scalars()] * 2 + [whole()] * 2,
        out_specs=(whole(), whole(), whole()),
        compiler_params=params(8),
        name="make_stream",
    )(f, core, parts, hidden)


def squares_rows(row_values, width):
    high = row_values.astype(BF16).astype(F32)
    low = row_values - high
    index = lax.broadcasted_iota(jnp.int32, (SQ_ROWS, width), 0)
    return jnp.where(index == 0, high, jnp.where(index == 1, low, 0.0)).astype(BF16)


def up_kernel(order, hops, z_ref, core_ref, stream_ref, gain_ref, gate_ref, up_ref, *out_refs):
    z_count, core_count, ffn_count, micro = order
    tiles = gate_ref.shape[1] // LANES
    rows = ffn_count * micro
    me = z_ref[0]
    core = core_ref[0]

    def source(r):
        m = r % micro
        f = (r // micro) % ffn_count
        block = r // rows
        side = block // len(hops)
        hop = hops[0] + block % len(hops)
        return ((f * z_count + (me ^ hop)) * core_count + (core ^ side)) * micro + m

    spread = one_hot((len(out_refs) * rows, stream_ref.shape[0]), source).astype(BF16)
    stream = jnp.dot(spread, stream_ref[...], preferred_element_type=F32)
    scaled = (stream * gain_ref[...].astype(F32)).astype(BF16)
    squares = jnp.sum(stream * stream, axis=1, keepdims=True)
    lane = one_hot((rows, LANES), lambda r: r)
    for i, out_ref in enumerate(out_refs):
        sums = jnp.sum(lane * squares[i * rows : (i + 1) * rows], axis=0, keepdims=True)
        out_ref[2 * tiles * rows :, :] = squares_rows(sums, LANES)
    for half, weight_ref in enumerate((gate_ref, up_ref)):
        product = jnp.dot(scaled, weight_ref[...], preferred_element_type=F32).astype(BF16)
        for i, out_ref in enumerate(out_refs):
            for j in range(tiles):
                at = (half * tiles + j) * rows
                out_ref[at : at + rows, :] = product[i * rows : (i + 1) * rows, j * LANES : (j + 1) * LANES]


def up_part(order, hops, z, core, stream_all, gain, gate_weight, up_weight):
    _, _, ffn_count, micro = order
    out_rows = 2 * gate_weight.shape[1] // LANES * ffn_count * micro + SQ_ROWS
    shape = jax.ShapeDtypeStruct((out_rows, LANES), BF16)
    return pl.pallas_call(
        functools.partial(up_kernel, order, hops),
        out_shape=[shape] * (2 * len(hops)),
        in_specs=[scalars(), scalars(), whole(), whole(), whole(), whole()],
        out_specs=[whole()] * (2 * len(hops)),
        compiler_params=params(16),
        cost_estimate=HEAVY,
        name="up_part",
    )(z, core, stream_all, gain, gate_weight, up_weight)


def sum_blocks(refs, start, stop):
    total = refs[0][start:stop, :].astype(F32)
    for ref in refs[1:]:
        total = total + ref[start:stop, :].astype(F32)
    return total


def add_kernel(*refs):
    *block_refs, out_ref = refs
    out_rows, lanes = out_ref.shape
    body = out_rows - SQ_ROWS
    out_ref[:body, :] = sum_blocks(block_refs, 0, body).astype(BF16)
    tail = sum_blocks(block_refs, body, out_rows)
    out_ref[body:, :] = squares_rows(tail[0:1] + tail[1:2], lanes)


def add(*blocks):
    return pl.pallas_call(
        add_kernel,
        out_shape=jax.ShapeDtypeStruct(blocks[0].shape, BF16),
        in_specs=[whole()] * len(blocks),
        out_specs=whole(),
        compiler_params=params(8),
        name="add",
    )(*blocks)


def activate_kernel(model_width, *refs):
    *block_refs, out_ref = refs
    out_rows, lanes = block_refs[0].shape
    rows, hidden = out_ref.shape
    tiles = hidden // lanes
    tail = sum_blocks(block_refs, out_rows - SQ_ROWS, out_rows)
    lane_sums = tail[0:1] + tail[1:2]
    spread = one_hot((rows, lanes), lambda r: r)
    squares = jnp.sum(spread * lane_sums, axis=1, keepdims=True)
    scale = lax.rsqrt(squares / model_width + EPSILON)
    for j in range(tiles):
        gate = sum_blocks(block_refs, j * rows, (j + 1) * rows) * scale
        upward = sum_blocks(block_refs, (tiles + j) * rows, (tiles + j + 1) * rows) * scale
        out_ref[:, j * lanes : (j + 1) * lanes] = (gate / (1.0 + jnp.exp(-gate)) * upward).astype(BF16)


def activate(blocks, rows, hidden, model_width):
    return pl.pallas_call(
        functools.partial(activate_kernel, model_width),
        out_shape=jax.ShapeDtypeStruct((rows, hidden), BF16),
        in_specs=[whole()] * len(blocks),
        out_specs=whole(),
        compiler_params=params(8),
        name="activate",
    )(*blocks)


def finish_kernel(order, z_ref, core_ref, parts_ref, stream_ref, received_ref, *out_refs):
    z_count, core_count, _, micro = order
    rows = stream_ref.shape[0]
    half = rows // 2

    def own(r):
        return jnp.where(r < half, ((r // micro) * core_count + core_ref[0]) * micro + r % micro, -1)

    first = one_hot((rows, rows), own).astype(BF16)
    second = one_hot((rows, FEW), lambda r: r - half).astype(BF16)
    stream = jnp.dot(first, stream_ref[...], preferred_element_type=F32)
    stream = stream + jnp.dot(second, received_ref[...], preferred_element_type=F32)
    finished = (stream + sum_parts(parts_ref)).astype(BF16)
    slots = out_refs[0].shape[0]
    me = z_ref[0]

    def source(r):
        q = r % slots
        at = (q // micro) * half + ((r // slots) ^ me) * micro + q % micro
        return jnp.where(q < 2 * micro, at, -1)

    spread = one_hot((len(out_refs) * slots, rows), source).astype(BF16)
    blocks = jnp.dot(spread, finished, preferred_element_type=F32)
    for k, out_ref in enumerate(out_refs):
        out_ref[...] = blocks[k * slots : (k + 1) * slots].astype(BF16)


def finish(z, core, parts, stream, received, order):
    z_count, _, _, micro = order
    slots = -(-2 * micro // 8) * 8
    return pl.pallas_call(
        functools.partial(finish_kernel, order),
        out_shape=[jax.ShapeDtypeStruct((slots, stream.shape[1]), BF16)] * z_count,
        in_specs=[scalars()] * 2 + [whole()] * 3,
        out_specs=[whole()] * z_count,
        compiler_params=params(8),
        name="finish",
    )(z, core, parts, stream, received)


def place_kernel(z_ref, core_ref, *refs):
    *piece_refs, out_ref = refs
    width = piece_refs[0].shape[1]
    micro = out_ref.shape[0]
    for k, ref in enumerate(piece_refs):
        block = ref[...].astype(F32)
        for side in range(2):
            share = 2 * (z_ref[0] ^ k) + (core_ref[0] ^ side)
            at = pl.multiple_of(share * width, LANES)
            out_ref[:, pl.ds(at, width)] = block[side * micro : (side + 1) * micro].astype(BF16)


def place(z, core, pieces, micro):
    width = pieces[0].shape[1]
    return pl.pallas_call(
        place_kernel,
        out_shape=jax.ShapeDtypeStruct((micro, 2 * len(pieces) * width), BF16),
        in_specs=[scalars(), scalars()] + [whole()] * len(pieces),
        out_specs=whole(),
        compiler_params=params(8),
        name="place",
    )(z, core, *pieces)


def along_z(array, hop):
    return lax.ppermute(array, Z, [(i, i ^ hop) for i in range(lax.axis_size(Z))])


def swap_cores(array):
    return lax.ppermute(array, CORE, [(0, 1), (1, 0)])


def per_device(
    hidden_in,
    queries,
    key_cache,
    value_cache,
    lengths,
    cache_slot,
    out_weight,
    ffn_gain,
    gate_weight,
    up_weight,
    down_weight,
):
    z_count = lax.axis_size(Z)
    core_count = lax.axis_size(CORE)
    attn_count = z_count * core_count
    ffn_count = lax.axis_size("x") * lax.axis_size("y")
    f_index = lax.axis_index(FFN).astype(jnp.int32)[None]
    z_index = lax.axis_index(Z).astype(jnp.int32)[None]
    core_index = lax.axis_index(CORE).astype(jnp.int32)[None]
    micro, total_rows, col_share = hidden_in.shape
    head_dim = key_cache.shape[2]
    model_width = col_share * attn_count
    hidden_share = gate_weight.shape[1]
    rows_chunk = attn_count * micro
    rows_all = ffn_count * rows_chunk
    rows_block = rows_all // attn_count

    order = (z_count, core_count, ffn_count, micro)
    payload = attend(
        queries.reshape(micro, -1), key_cache, value_cache, cache_slot.T, lengths.T, z_count, ffn_count
    )
    tile_rows = payload.shape[3]
    payload, f_index, z_index, core_index = lax.optimization_barrier((payload, f_index, z_index, core_index))
    payload = payload.reshape(z_count * ffn_count, micro * tile_rows, LANES)
    incoming = lax.all_to_all(payload, (Z,) + FFN, split_axis=0, concat_axis=0, tiled=True)
    own_rows = to_rows(incoming.reshape(z_count * ffn_count * micro, tile_rows, LANES), head_dim // LANES)
    own_rows, ffn_gain = lax.optimization_barrier((own_rows, ffn_gain))
    other_rows = swap_cores(own_rows)
    gain = ffn_gain[None, :]
    own_mixed = product_of(own_rows, out_weight)
    own_mixed, other_rows, gain = lax.optimization_barrier((own_mixed, other_rows, gain))
    mixed = mix(core_index, own_mixed, other_rows, out_weight, order)

    parts = lax.all_to_all(
        mixed.reshape(ffn_count, rows_chunk, col_share), FFN, split_axis=0, concat_axis=0, tiled=True
    )
    stream, send, copies = make_stream(f_index, core_index, parts, hidden_in.reshape(rows_all, col_share), order)
    stream_all = lax.all_to_all(copies, FFN, split_axis=0, concat_axis=0, tiled=True)
    stream_all = stream_all.reshape(rows_all, col_share)

    up_args = (gain, gate_weight, up_weight)
    own2, own3, other2, other3 = up_part(order, (2, 3), z_index, core_index, stream_all, *up_args)
    own0, own1, other0, other1 = up_part(order, (0, 1), z_index, core_index, stream_all, *up_args)
    received3, own0 = lax.optimization_barrier((swap_cores(other3), own0))
    relayed3 = add(own3, received3)
    relayed3, other0, other1, other2 = lax.optimization_barrier((relayed3, other0, other1, other2))
    crossing = along_z(relayed3, 1)
    near1 = add(own1, swap_cores(other1))
    received2, near1 = lax.optimization_barrier((swap_cores(other2), near1))
    relayed = add(own2, received2, crossing)
    relayed, send = lax.optimization_barrier((relayed, send))
    from_far = along_z(relayed, 2)
    from_near = along_z(near1, 1)
    down_weight, near1 = lax.optimization_barrier((down_weight, near1))
    down_own, down_other = fetch(down_weight, swap_cores(down_weight))
    from_far, down_own, down_other = lax.optimization_barrier((from_far, down_own, down_other))
    activated = activate((own0, swap_cores(other0), from_near, from_far), rows_block, hidden_share, model_width)

    far = along_z(activated, 2)
    near = along_z(activated, 1)
    far, received = lax.optimization_barrier((far, swap_cores(send)))
    most = down_most((activated, near, far), down_own, down_other)
    lowered = down(z_index, most, along_z(far, 1), down_own, down_other, order)
    lowered_parts = lax.all_to_all(
        lowered.reshape(ffn_count, rows_chunk, col_share), FFN, split_axis=0, concat_axis=0, tiled=True
    )
    shares = finish(z_index, core_index, lowered_parts, stream, received, order)
    pieces = [shares[0]] + [along_z(shares[hop], hop) for hop in range(1, z_count)]
    return place(z_index, core_index, pieces, micro).reshape(micro, 1, model_width)


def solution(mesh):
    sizes = dict(mesh.shape)
    attn_count, ffn_count, rep_count = sizes["attn"], sizes["ffn"], sizes["rep"]
    side = int(round(ffn_count**0.5))
    fine = Mesh(
        mesh.devices.reshape(attn_count // 2, 2, side, ffn_count // side, rep_count),
        (Z, CORE, "x", "y", REP),
    )
    owners = (REP, Z, CORE, "x", "y")
    return jax.shard_map(
        per_device,
        mesh=fine,
        in_specs=(
            P(None, REP, ATTN),
            P(None, owners, None),
            P(owners, None, None),
            P(owners, None, None),
            P(None, owners),
            P(None, owners),
            P(FFN, ATTN),
            P(ATTN),
            P(ATTN, FFN),
            P(ATTN, FFN),
            P(FFN, ATTN),
        ),
        out_specs=P(None, owners, None),
        check_vma=False,
    )
```

```python
import functools

import jax
import jax.numpy as jnp
from jax import lax
from jax.experimental import pallas as pl
from jax.experimental.pallas import tpu as pltpu
from jax.sharding import Mesh, PartitionSpec as P

EPSILON = 1e-06
MASKED = -1e30
Z = "z"
CORE = "core"
ATTN = (Z, CORE)
FFN = ("x", "y")
REP = "rep"
LANES = 128
SQ_ROWS = 16
FEW = 16
BF16 = jnp.bfloat16
F32 = jnp.float32
HEAVY = pl.CostEstimate(flops=10**10, bytes_accessed=10**7, transcendentals=0)


def whole():
    return pl.BlockSpec(memory_space=pltpu.VMEM)


def scalars():
    return pl.BlockSpec(memory_space=pltpu.SMEM)


def in_hbm():
    return pl.BlockSpec(memory_space=pltpu.HBM)


def params(mib):
    return pltpu.CompilerParams(vmem_limit_bytes=mib * 1024 * 1024)


def one_hot(shape, source_of_row):
    rows = lax.broadcasted_iota(jnp.int32, (shape[0], 1), 0)
    cols = lax.broadcasted_iota(jnp.int32, shape, 1)
    return jnp.where(cols == source_of_row(rows), 1.0, 0.0)


def attention_kernel(
    slot_hbm,
    length_hbm,
    query_hbm,
    key_hbm,
    value_hbm,
    out_ref,
    slots,
    lengths,
    queries,
    keys,
    values,
    wide,
    small_sem,
    key_sem,
    value_sem,
):
    slot_count, pos, head_dim = keys.shape
    micro, width = queries.shape
    heads = width // head_dim
    copies, blocks, _, tile_rows, _ = out_ref.shape
    small = [
        pltpu.make_async_copy(source, target, small_sem.at[i])
        for i, (source, target) in enumerate(((query_hbm, queries), (slot_hbm, slots), (length_hbm, lengths)))
    ]
    key_copies = [pltpu.make_async_copy(key_hbm.at[s], keys.at[s], key_sem.at[s]) for s in range(slot_count)]
    value_copies = [pltpu.make_async_copy(value_hbm.at[s], values.at[s], value_sem.at[s]) for s in range(slot_count)]
    for copy in small + key_copies + value_copies:
        copy.start()
    for copy in small:
        copy.wait()
    for h in range(heads):
        wide[:, h, :] = queries[:, h * head_dim : (h + 1) * head_dim].astype(F32)
    pieces = head_dim // LANES
    group = heads // blocks
    positions = lax.broadcasted_iota(jnp.int32, (heads, pos), 1)
    softened = []
    totals = []
    for copy in key_copies:
        copy.wait()
    for m in range(micro):
        scores = lax.dot_general(
            wide[m].astype(BF16), keys[slots[0, m]], (((1,), (1,)), ((), ())), preferred_element_type=F32
        ) * head_dim ** (-0.5)
        in_cache = positions < lengths[0, m]
        scores = jnp.where(in_cache, scores, MASKED)
        highest = jnp.max(scores, axis=1, keepdims=True)
        weights = jnp.where(in_cache, jnp.exp(scores - highest), 0.0)
        totals.append(jnp.sum(weights, axis=1, keepdims=True))
        softened.append(weights.astype(BF16))
    for copy in value_copies:
        copy.wait()
    for m in range(micro):
        weighted = jnp.dot(softened[m], values[slots[0, m]], preferred_element_type=F32)
        attended = weighted / totals[m]
        for piece in range(pieces):
            part = attended[:, piece * LANES : (piece + 1) * LANES].reshape(blocks, group, LANES).astype(BF16)
            for copy in range(copies):
                out_ref[copy, :, m, piece * group : (piece + 1) * group, :] = part


def attend(queries, key_cache, value_cache, slots, lengths, z_count, ffn_count):
    slot_count, pos, head_dim = key_cache.shape
    micro, width = queries.shape
    tile_rows = width // ffn_count // LANES
    return pl.pallas_call(
        attention_kernel,
        in_specs=[in_hbm()] * 5,
        out_specs=whole(),
        out_shape=jax.ShapeDtypeStruct((z_count, ffn_count, micro, tile_rows, LANES), BF16),
        scratch_shapes=[
            pltpu.SMEM(slots.shape, jnp.int32),
            pltpu.SMEM(lengths.shape, jnp.int32),
            pltpu.VMEM(queries.shape, BF16),
            pltpu.VMEM((slot_count, pos, head_dim), BF16),
            pltpu.VMEM((slot_count, pos, head_dim), BF16),
            pltpu.VMEM((micro, width // head_dim, head_dim), F32),
            pltpu.SemaphoreType.DMA((3,)),
            pltpu.SemaphoreType.DMA((slot_count,)),
            pltpu.SemaphoreType.DMA((slot_count,)),
        ],
        compiler_params=params(60),
        name="attention",
    )(slots, lengths, queries, key_cache, value_cache)


def spread_shares(order, own, other, source):
    z_count, _, ffn_count, micro = order
    count = own.shape[0]

    def place_of(r):
        m = r % micro
        z = (r // micro) % z_count
        share = (r // (micro * z_count)) % 2
        f = r // (micro * z_count * 2)
        return share * count + source(z, f, m)

    spread = one_hot((2 * count, 2 * count), place_of).astype(BF16)
    return jnp.dot(spread, jnp.concatenate([own, other], axis=0), preferred_element_type=F32).astype(BF16)


def rows_kernel(pieces, in_ref, out_ref, wide):
    rows, tile_rows, lanes = in_ref.shape
    wide[...] = in_ref[...].astype(F32).reshape(rows * tile_rows, lanes)
    group = tile_rows // pieces
    for j in range(tile_rows):
        at = (j % pieces) * group + j // pieces
        out_ref[:, j * lanes : (j + 1) * lanes] = wide[pl.ds(at, rows, stride=tile_rows), :].astype(BF16)


def to_rows(tiles, pieces):
    rows, tile_rows, lanes = tiles.shape
    return pl.pallas_call(
        functools.partial(rows_kernel, pieces),
        out_shape=jax.ShapeDtypeStruct((rows, tile_rows * lanes), BF16),
        in_specs=[whole()],
        out_specs=whole(),
        scratch_shapes=[pltpu.VMEM((rows * tile_rows, lanes), F32)],
        compiler_params=params(8),
        name="to_rows",
    )(tiles)


def product_kernel(rows_ref, weight_ref, out_ref):
    out_ref[...] = jnp.dot(rows_ref[...], weight_ref[...], preferred_element_type=F32).astype(BF16)


def product_of(rows, weight):
    return pl.pallas_call(
        product_kernel,
        out_shape=jax.ShapeDtypeStruct((rows.shape[0], weight.shape[1]), BF16),
        in_specs=[whole(), whole()],
        out_specs=whole(),
        compiler_params=params(12),
        cost_estimate=HEAVY,
        name="product",
    )(rows, weight)


def mix_kernel(order, core_ref, own_ref, rows_ref, weight_ref, out_ref):
    z_count, core_count, ffn_count, micro = order
    total = 2 * rows_ref.shape[0]
    product = jnp.dot(rows_ref[...], weight_ref[...], preferred_element_type=F32).astype(BF16)
    core = core_ref[0]

    def source(r):
        m = r % micro
        c = (r // micro) % core_count
        z = (r // (micro * core_count)) % z_count
        f = r // (micro * core_count * z_count)
        return (((c ^ core) * z_count + z) * ffn_count + f) * micro + m

    spread = one_hot((total, total), source).astype(BF16)
    both = jnp.concatenate([own_ref[...], product], axis=0)
    out_ref[...] = jnp.dot(spread, both, preferred_element_type=F32).astype(BF16)


def mix(core, own, rows, weight, order):
    return pl.pallas_call(
        functools.partial(mix_kernel, order),
        out_shape=jax.ShapeDtypeStruct((2 * rows.shape[0], weight.shape[1]), BF16),
        in_specs=[scalars(), whole(), whole(), whole()],
        out_specs=whole(),
        compiler_params=params(12),
        name="mix",
    )(core, own, rows, weight)


def down_most_kernel(*refs):
    *piece_refs, own_ref, other_ref, own_out_ref, other_out_ref = refs
    rows = jnp.concatenate([ref[...] for ref in piece_refs], axis=0)
    own_out_ref[...] = jnp.dot(rows, own_ref[...], preferred_element_type=F32).astype(BF16)
    other_out_ref[...] = jnp.dot(rows, other_ref[...], preferred_element_type=F32).astype(BF16)


def down_most(pieces, own_weight, other_weight):
    shape = jax.ShapeDtypeStruct((len(pieces) * pieces[0].shape[0], own_weight.shape[1]), BF16)
    return pl.pallas_call(
        down_most_kernel,
        out_shape=(shape, shape),
        in_specs=[whole()] * (len(pieces) + 2),
        out_specs=(whole(), whole()),
        compiler_params=params(16),
        cost_estimate=HEAVY,
        name="down_most",
    )(*pieces, own_weight, other_weight)


def down_kernel(order, z_ref, own_most_ref, other_most_ref, rows_ref, own_ref, other_ref, out_ref):
    _, _, ffn_count, micro = order
    shares = []
    for most_ref, weight_ref in ((own_most_ref, own_ref), (other_most_ref, other_ref)):
        last = jnp.dot(rows_ref[...], weight_ref[...], preferred_element_type=F32).astype(BF16)
        shares.append(jnp.concatenate([most_ref[...], last], axis=0))
    me = z_ref[0]
    out_ref[...] = spread_shares(order, *shares, lambda z, f, m: ((z ^ me) * ffn_count + f) * micro + m)


def down(z, most, last, own_weight, other_weight, order):
    rows = most[0].shape[0] + last.shape[0]
    return pl.pallas_call(
        functools.partial(down_kernel, order),
        out_shape=jax.ShapeDtypeStruct((2 * rows, own_weight.shape[1]), BF16),
        in_specs=[scalars()] + [whole()] * 5,
        out_specs=whole(),
        compiler_params=params(16),
        name="down",
    )(z, *most, last, own_weight, other_weight)


def fetch_kernel(cuts, *refs):
    count = (len(refs) - 1) // 2
    sources, targets, sems = refs[:count], refs[count : 2 * count], refs[2 * count]
    copies = []
    for i in range(count):
        rows = sources[i].shape[0] // cuts
        for j in range(cuts):
            part = pl.ds(j * rows, rows)
            copies.append(pltpu.make_async_copy(sources[i].at[part], targets[i].at[part], sems.at[i * cuts + j]))
    for copy in copies:
        copy.start()
    for copy in copies:
        copy.wait()


def fetch(*arrays):
    cuts = 4
    return pl.pallas_call(
        functools.partial(fetch_kernel, cuts),
        out_shape=[jax.ShapeDtypeStruct(array.shape, array.dtype) for array in arrays],
        in_specs=[in_hbm()] * len(arrays),
        out_specs=[whole()] * len(arrays),
        scratch_shapes=[pltpu.SemaphoreType.DMA((len(arrays) * cuts,))],
        compiler_params=params(16),
        cost_estimate=HEAVY,
        name="fetch",
    )(*arrays)


def sum_parts(parts_ref):
    total = parts_ref[0].astype(F32)
    for j in range(1, parts_ref.shape[0]):
        total = total + parts_ref[j].astype(F32)
    return total


def stream_kernel(order, f_ref, core_ref, parts_ref, hidden_ref, stream_ref, send_ref, copies_ref):
    z_count, core_count, ffn_count, micro = order
    rows = stream_ref.shape[0]
    f = f_ref[0]

    def source(r):
        return ((r % micro) * z_count * core_count + r // micro) * ffn_count + f

    spread = one_hot((rows, hidden_ref.shape[0]), source).astype(BF16)
    hidden = jnp.dot(spread, hidden_ref[...], preferred_element_type=F32)
    stream = (hidden + sum_parts(parts_ref)).astype(BF16)
    stream_ref[...] = stream
    for j in range(copies_ref.shape[0]):
        copies_ref[j] = stream

    def other(r):
        row = ((r // micro) * core_count + 1 - core_ref[0]) * micro + r % micro
        return jnp.where(r < z_count * micro, row, -1)

    pick = one_hot((FEW, rows), other).astype(BF16)
    send_ref[...] = jnp.dot(pick, stream, preferred_element_type=F32).astype(BF16)


def make_stream(f, core, parts, hidden, order):
    _, rows, width = parts.shape
    return pl.pallas_call(
        functools.partial(stream_kernel, order),
        out_shape=(
            jax.ShapeDtypeStruct((rows, width), BF16),
            jax.ShapeDtypeStruct((FEW, width), BF16),
            jax.ShapeDtypeStruct(parts.shape, BF16),
        ),
        in_specs=[scalars()] * 2 + [whole()] * 2,
        out_specs=(whole(), whole(), whole()),
        compiler_params=params(8),
        name="make_stream",
    )(f, core, parts, hidden)


def squares_rows(row_values, width):
    high = row_values.astype(BF16).astype(F32)
    low = row_values - high
    index = lax.broadcasted_iota(jnp.int32, (SQ_ROWS, width), 0)
    return jnp.where(index == 0, high, jnp.where(index == 1, low, 0.0)).astype(BF16)


def up_kernel(order, hops, z_ref, core_ref, stream_ref, gain_ref, gate_ref, up_ref, *out_refs):
    z_count, core_count, ffn_count, micro = order
    tiles = gate_ref.shape[1] // LANES
    rows = ffn_count * micro
    me = z_ref[0]
    core = core_ref[0]

    def source(r):
        m = r % micro
        f = (r // micro) % ffn_count
        block = r // rows
        side = block // len(hops)
        hop = hops[0] + (hops[1] - hops[0]) * (block % len(hops))
        return ((f * z_count + (me ^ hop)) * core_count + (core ^ side)) * micro + m

    spread = one_hot((len(out_refs) * rows, stream_ref.shape[0]), source).astype(BF16)
    stream = jnp.dot(spread, stream_ref[...], preferred_element_type=F32)
    scaled = (stream * gain_ref[...].astype(F32)).astype(BF16)
    squares = jnp.sum(stream * stream, axis=1, keepdims=True)
    lane = one_hot((rows, LANES), lambda r: r)
    for i, out_ref in enumerate(out_refs):
        sums = jnp.sum(lane * squares[i * rows : (i + 1) * rows], axis=0, keepdims=True)
        out_ref[2 * tiles * rows :, :] = squares_rows(sums, LANES)
    for half, weight_ref in enumerate((gate_ref, up_ref)):
        product = jnp.dot(scaled, weight_ref[...], preferred_element_type=F32).astype(BF16)
        for i, out_ref in enumerate(out_refs):
            for j in range(tiles):
                at = (half * tiles + j) * rows
                out_ref[at : at + rows, :] = product[i * rows : (i + 1) * rows, j * LANES : (j + 1) * LANES]


def up_part(order, hops, z, core, stream_all, gain, gate_weight, up_weight):
    _, _, ffn_count, micro = order
    out_rows = 2 * gate_weight.shape[1] // LANES * ffn_count * micro + SQ_ROWS
    shape = jax.ShapeDtypeStruct((out_rows, LANES), BF16)
    return pl.pallas_call(
        functools.partial(up_kernel, order, hops),
        out_shape=[shape] * (2 * len(hops)),
        in_specs=[scalars(), scalars(), whole(), whole(), whole(), whole()],
        out_specs=[whole()] * (2 * len(hops)),
        compiler_params=params(16),
        cost_estimate=HEAVY,
        name="up_part",
    )(z, core, stream_all, gain, gate_weight, up_weight)


def sum_blocks(refs, start, stop):
    total = refs[0][start:stop, :].astype(F32)
    for ref in refs[1:]:
        total = total + ref[start:stop, :].astype(F32)
    return total


def add_kernel(*refs):
    *block_refs, out_ref = refs
    out_rows, lanes = out_ref.shape
    body = out_rows - SQ_ROWS
    out_ref[:body, :] = sum_blocks(block_refs, 0, body).astype(BF16)
    tail = sum_blocks(block_refs, body, out_rows)
    out_ref[body:, :] = squares_rows(tail[0:1] + tail[1:2], lanes)


def add(*blocks):
    return pl.pallas_call(
        add_kernel,
        out_shape=jax.ShapeDtypeStruct(blocks[0].shape, BF16),
        in_specs=[whole()] * len(blocks),
        out_specs=whole(),
        compiler_params=params(8),
        name="add",
    )(*blocks)


def activate_kernel(model_width, *refs):
    *block_refs, out_ref = refs
    out_rows, lanes = block_refs[0].shape
    rows, hidden = out_ref.shape
    tiles = hidden // lanes
    tail = sum_blocks(block_refs, out_rows - SQ_ROWS, out_rows)
    lane_sums = tail[0:1] + tail[1:2]
    spread = one_hot((rows, lanes), lambda r: r)
    squares = jnp.sum(spread * lane_sums, axis=1, keepdims=True)
    scale = lax.rsqrt(squares / model_width + EPSILON)
    for j in range(tiles):
        gate = sum_blocks(block_refs, j * rows, (j + 1) * rows) * scale
        upward = sum_blocks(block_refs, (tiles + j) * rows, (tiles + j + 1) * rows) * scale
        out_ref[:, j * lanes : (j + 1) * lanes] = (gate / (1.0 + jnp.exp(-gate)) * upward).astype(BF16)


def activate(blocks, rows, hidden, model_width):
    return pl.pallas_call(
        functools.partial(activate_kernel, model_width),
        out_shape=jax.ShapeDtypeStruct((rows, hidden), BF16),
        in_specs=[whole()] * len(blocks),
        out_specs=whole(),
        compiler_params=params(8),
        name="activate",
    )(*blocks)


def finish_kernel(order, z_ref, core_ref, parts_ref, stream_ref, received_ref, *out_refs):
    z_count, core_count, _, micro = order
    rows = stream_ref.shape[0]
    half = rows // 2

    def own(r):
        return jnp.where(r < half, ((r // micro) * core_count + core_ref[0]) * micro + r % micro, -1)

    first = one_hot((rows, rows), own).astype(BF16)
    second = one_hot((rows, FEW), lambda r: r - half).astype(BF16)
    stream = jnp.dot(first, stream_ref[...], preferred_element_type=F32)
    stream = stream + jnp.dot(second, received_ref[...], preferred_element_type=F32)
    finished = (stream + sum_parts(parts_ref)).astype(BF16)
    slots = out_refs[0].shape[0]
    me = z_ref[0]

    def source(r):
        q = r % slots
        at = (q // micro) * half + ((r // slots) ^ me) * micro + q % micro
        return jnp.where(q < 2 * micro, at, -1)

    spread = one_hot((len(out_refs) * slots, rows), source).astype(BF16)
    blocks = jnp.dot(spread, finished, preferred_element_type=F32)
    for k, out_ref in enumerate(out_refs):
        out_ref[...] = blocks[k * slots : (k + 1) * slots].astype(BF16)


def finish(z, core, parts, stream, received, order):
    z_count, _, _, micro = order
    slots = -(-2 * micro // 8) * 8
    return pl.pallas_call(
        functools.partial(finish_kernel, order),
        out_shape=[jax.ShapeDtypeStruct((slots, stream.shape[1]), BF16)] * z_count,
        in_specs=[scalars()] * 2 + [whole()] * 3,
        out_specs=[whole()] * z_count,
        compiler_params=params(8),
        name="finish",
    )(z, core, parts, stream, received)


def place_kernel(z_ref, core_ref, *refs):
    *piece_refs, out_ref = refs
    width = piece_refs[0].shape[1]
    micro = out_ref.shape[0]
    for k, ref in enumerate(piece_refs):
        block = ref[...].astype(F32)
        for side in range(2):
            share = 2 * (z_ref[0] ^ k) + (core_ref[0] ^ side)
            at = pl.multiple_of(share * width, LANES)
            out_ref[:, pl.ds(at, width)] = block[side * micro : (side + 1) * micro].astype(BF16)


def place(z, core, pieces, micro):
    width = pieces[0].shape[1]
    return pl.pallas_call(
        place_kernel,
        out_shape=jax.ShapeDtypeStruct((micro, 2 * len(pieces) * width), BF16),
        in_specs=[scalars(), scalars()] + [whole()] * len(pieces),
        out_specs=whole(),
        compiler_params=params(8),
        name="place",
    )(z, core, *pieces)


def along_z(array, hop):
    return lax.ppermute(array, Z, [(i, i ^ hop) for i in range(lax.axis_size(Z))])


def swap_cores(array):
    return lax.ppermute(array, CORE, [(0, 1), (1, 0)])


def per_device(
    hidden_in,
    queries,
    key_cache,
    value_cache,
    lengths,
    cache_slot,
    out_weight,
    ffn_gain,
    gate_weight,
    up_weight,
    down_weight,
):
    z_count = lax.axis_size(Z)
    core_count = lax.axis_size(CORE)
    attn_count = z_count * core_count
    ffn_count = lax.axis_size("x") * lax.axis_size("y")
    f_index = lax.axis_index(FFN).astype(jnp.int32)[None]
    z_index = lax.axis_index(Z).astype(jnp.int32)[None]
    core_index = lax.axis_index(CORE).astype(jnp.int32)[None]
    micro, total_rows, col_share = hidden_in.shape
    head_dim = key_cache.shape[2]
    model_width = col_share * attn_count
    hidden_share = gate_weight.shape[1]
    rows_chunk = attn_count * micro
    rows_all = ffn_count * rows_chunk
    rows_block = rows_all // attn_count

    order = (z_count, core_count, ffn_count, micro)
    payload = attend(
        queries.reshape(micro, -1), key_cache, value_cache, cache_slot.T, lengths.T, z_count, ffn_count
    )
    tile_rows = payload.shape[3]
    payload, f_index, z_index, core_index = lax.optimization_barrier((payload, f_index, z_index, core_index))
    payload = payload.reshape(z_count * ffn_count, micro * tile_rows, LANES)
    incoming = lax.all_to_all(payload, (Z,) + FFN, split_axis=0, concat_axis=0, tiled=True)
    own_rows = to_rows(incoming.reshape(z_count * ffn_count * micro, tile_rows, LANES), head_dim // LANES)
    own_rows, ffn_gain = lax.optimization_barrier((own_rows, ffn_gain))
    other_rows = swap_cores(own_rows)
    gain = ffn_gain[None, :]
    own_mixed = product_of(own_rows, out_weight)
    own_mixed, other_rows, gain = lax.optimization_barrier((own_mixed, other_rows, gain))
    mixed = mix(core_index, own_mixed, other_rows, out_weight, order)

    parts = lax.all_to_all(
        mixed.reshape(ffn_count, rows_chunk, col_share), FFN, split_axis=0, concat_axis=0, tiled=True
    )
    stream, send, copies = make_stream(f_index, core_index, parts, hidden_in.reshape(rows_all, col_share), order)
    stream_all = lax.all_to_all(copies, FFN, split_axis=0, concat_axis=0, tiled=True)
    stream_all = stream_all.reshape(rows_all, col_share)

    up_args = (z_index, core_index, stream_all, gain, gate_weight, up_weight)
    own3, own1, other3, other1 = up_part(order, (3, 1), *up_args)
    own0, own2, other0, other2 = up_part(order, (0, 2), *up_args)
    received3, received1, own0 = lax.optimization_barrier((swap_cores(other3), swap_cores(other1), own0))
    relayed3 = add(own3, received3)
    near1 = add(own1, received1)
    relayed3, other0, other2 = lax.optimization_barrier((relayed3, other0, other2))
    crossing = along_z(relayed3, 1)
    relayed = add(own2, swap_cores(other2), crossing)
    relayed, send = lax.optimization_barrier((relayed, send))
    from_far = along_z(relayed, 2)
    from_near = along_z(near1, 1)
    down_weight, near1 = lax.optimization_barrier((down_weight, near1))
    down_own, down_other = fetch(down_weight, swap_cores(down_weight))
    from_far, down_own, down_other = lax.optimization_barrier((from_far, down_own, down_other))
    activated = activate((own0, swap_cores(other0), from_near, from_far), rows_block, hidden_share, model_width)

    far = along_z(activated, 2)
    near = along_z(activated, 1)
    far, received = lax.optimization_barrier((far, swap_cores(send)))
    most = down_most((activated, near, far), down_own, down_other)
    lowered = down(z_index, most, along_z(far, 1), down_own, down_other, order)
    lowered_parts = lax.all_to_all(
        lowered.reshape(ffn_count, rows_chunk, col_share), FFN, split_axis=0, concat_axis=0, tiled=True
    )
    shares = finish(z_index, core_index, lowered_parts, stream, received, order)
    pieces = [shares[0]] + [along_z(shares[hop], hop) for hop in range(1, z_count)]
    return place(z_index, core_index, pieces, micro).reshape(micro, 1, model_width)


def solution(mesh):
    sizes = dict(mesh.shape)
    attn_count, ffn_count, rep_count = sizes["attn"], sizes["ffn"], sizes["rep"]
    side = int(round(ffn_count**0.5))
    fine = Mesh(
        mesh.devices.reshape(attn_count // 2, 2, side, ffn_count // side, rep_count),
        (Z, CORE, "x", "y", REP),
    )
    owners = (REP, Z, CORE, "x", "y")
    return jax.shard_map(
        per_device,
        mesh=fine,
        in_specs=(
            P(None, REP, ATTN),
            P(None, owners, None),
            P(owners, None, None),
            P(owners, None, None),
            P(None, owners),
            P(None, owners),
            P(FFN, ATTN),
            P(ATTN),
            P(ATTN, FFN),
            P(ATTN, FFN),
            P(FFN, ATTN),
        ),
        out_specs=P(None, owners, None),
        check_vma=False,
    )
```

```python
import functools

import jax
import jax.numpy as jnp
from jax import lax
from jax.experimental import pallas as pl
from jax.experimental.pallas import tpu as pltpu
from jax.sharding import Mesh, PartitionSpec as P

EPSILON = 1e-06
MASKED = -1e30
Z = "z"
CORE = "core"
ATTN = (Z, CORE)
FFN = ("x", "y")
REP = "rep"
LANES = 128
SQ_ROWS = 16
FEW = 16
BF16 = jnp.bfloat16
F32 = jnp.float32
HEAVY = pl.CostEstimate(flops=10**10, bytes_accessed=10**7, transcendentals=0)


def whole():
    return pl.BlockSpec(memory_space=pltpu.VMEM)


def scalars():
    return pl.BlockSpec(memory_space=pltpu.SMEM)


def in_hbm():
    return pl.BlockSpec(memory_space=pltpu.HBM)


def params(mib):
    return pltpu.CompilerParams(vmem_limit_bytes=mib * 1024 * 1024)


def one_hot(shape, source_of_row):
    rows = lax.broadcasted_iota(jnp.int32, (shape[0], 1), 0)
    cols = lax.broadcasted_iota(jnp.int32, shape, 1)
    return jnp.where(cols == source_of_row(rows), 1.0, 0.0)


def attention_kernel(
    slot_hbm,
    length_hbm,
    query_hbm,
    key_hbm,
    value_hbm,
    out_ref,
    slots,
    lengths,
    queries,
    keys,
    values,
    wide,
    small_sem,
    key_sem,
    value_sem,
):
    slot_count, pos, head_dim = keys.shape
    micro, width = queries.shape
    heads = width // head_dim
    copies, blocks, _, tile_rows, _ = out_ref.shape
    small = [
        pltpu.make_async_copy(source, target, small_sem.at[i])
        for i, (source, target) in enumerate(((query_hbm, queries), (slot_hbm, slots), (length_hbm, lengths)))
    ]
    key_copies = [pltpu.make_async_copy(key_hbm.at[s], keys.at[s], key_sem.at[s]) for s in range(slot_count)]
    value_copies = [pltpu.make_async_copy(value_hbm.at[s], values.at[s], value_sem.at[s]) for s in range(slot_count)]
    for copy in small + key_copies + value_copies:
        copy.start()
    for copy in small:
        copy.wait()
    for h in range(heads):
        wide[:, h, :] = queries[:, h * head_dim : (h + 1) * head_dim].astype(F32)
    pieces = head_dim // LANES
    group = heads // blocks
    positions = lax.broadcasted_iota(jnp.int32, (heads, pos), 1)
    requests = []
    scores = []
    for s in range(slot_count):
        request = micro - 1
        for m in range(micro - 1):
            request = jnp.where(slots[0, m] == s, m, request)
        requests.append(request)
        query = wide[request].astype(BF16)
        key_copies[s].wait()
        scores.append(lax.dot_general(query, keys[s], (((1,), (1,)), ((), ())), preferred_element_type=F32))
    softened = []
    totals = []
    for s in range(slot_count):
        in_cache = positions < lengths[0, requests[s]]
        masked = jnp.where(in_cache, scores[s] * head_dim ** (-0.5), MASKED)
        highest = jnp.max(masked, axis=1, keepdims=True)
        weights = jnp.where(in_cache, jnp.exp(masked - highest), 0.0)
        totals.append(jnp.sum(weights, axis=1, keepdims=True))
        softened.append(weights.astype(BF16))
    for copy in value_copies:
        copy.wait()
    for s in range(slot_count):
        weighted = jnp.dot(softened[s], values[s], preferred_element_type=F32)
        attended = weighted / totals[s]
        for piece in range(pieces):
            part = attended[:, piece * LANES : (piece + 1) * LANES].reshape(blocks, group, LANES).astype(BF16)
            for copy in range(copies):
                out_ref[copy, :, requests[s], piece * group : (piece + 1) * group, :] = part


def attend(queries, key_cache, value_cache, slots, lengths, z_count, ffn_count):
    slot_count, pos, head_dim = key_cache.shape
    micro, width = queries.shape
    tile_rows = width // ffn_count // LANES
    return pl.pallas_call(
        attention_kernel,
        in_specs=[in_hbm()] * 5,
        out_specs=whole(),
        out_shape=jax.ShapeDtypeStruct((z_count, ffn_count, micro, tile_rows, LANES), BF16),
        scratch_shapes=[
            pltpu.SMEM(slots.shape, jnp.int32),
            pltpu.SMEM(lengths.shape, jnp.int32),
            pltpu.VMEM(queries.shape, BF16),
            pltpu.VMEM((slot_count, pos, head_dim), BF16),
            pltpu.VMEM((slot_count, pos, head_dim), BF16),
            pltpu.VMEM((micro, width // head_dim, head_dim), F32),
            pltpu.SemaphoreType.DMA((3,)),
            pltpu.SemaphoreType.DMA((slot_count,)),
            pltpu.SemaphoreType.DMA((slot_count,)),
        ],
        compiler_params=params(60),
        name="attention",
    )(slots, lengths, queries, key_cache, value_cache)


def spread_shares(order, own, other, source):
    z_count, _, ffn_count, micro = order
    count = own.shape[0]

    def place_of(r):
        m = r % micro
        z = (r // micro) % z_count
        share = (r // (micro * z_count)) % 2
        f = r // (micro * z_count * 2)
        return share * count + source(z, f, m)

    spread = one_hot((2 * count, 2 * count), place_of).astype(BF16)
    return jnp.dot(spread, jnp.concatenate([own, other], axis=0), preferred_element_type=F32).astype(BF16)


def rows_kernel(pieces, in_ref, out_ref, wide):
    rows, tile_rows, lanes = in_ref.shape
    wide[...] = in_ref[...].astype(F32).reshape(rows * tile_rows, lanes)
    group = tile_rows // pieces
    for j in range(tile_rows):
        at = (j % pieces) * group + j // pieces
        out_ref[:, j * lanes : (j + 1) * lanes] = wide[pl.ds(at, rows, stride=tile_rows), :].astype(BF16)


def to_rows(tiles, pieces):
    rows, tile_rows, lanes = tiles.shape
    return pl.pallas_call(
        functools.partial(rows_kernel, pieces),
        out_shape=jax.ShapeDtypeStruct((rows, tile_rows * lanes), BF16),
        in_specs=[whole()],
        out_specs=whole(),
        scratch_shapes=[pltpu.VMEM((rows * tile_rows, lanes), F32)],
        compiler_params=params(8),
        name="to_rows",
    )(tiles)


def mixed_rows(order, core, rows_ref, weight_ref):
    z_count, core_count, ffn_count, micro = order
    product = jnp.dot(rows_ref[...], weight_ref[...], preferred_element_type=F32).astype(BF16)

    def source(r):
        m = r % micro
        c = (r // micro) % core_count
        z = (r // (micro * core_count)) % z_count
        f = r // (micro * core_count * z_count)
        return jnp.where(c == core, (z * ffn_count + f) * micro + m, -1)

    spread = one_hot((core_count * product.shape[0], product.shape[0]), source).astype(BF16)
    return jnp.dot(spread, product, preferred_element_type=F32)


def product_kernel(order, core_ref, rows_ref, weight_ref, out_ref):
    out_ref[...] = mixed_rows(order, core_ref[0], rows_ref, weight_ref).astype(BF16)


def product_of(core, rows, weight, order):
    return pl.pallas_call(
        functools.partial(product_kernel, order),
        out_shape=jax.ShapeDtypeStruct((2 * rows.shape[0], weight.shape[1]), BF16),
        in_specs=[scalars(), whole(), whole()],
        out_specs=whole(),
        compiler_params=params(12),
        cost_estimate=HEAVY,
        name="product",
    )(core, rows, weight)


def mix_kernel(order, core_ref, own_ref, rows_ref, weight_ref, out_ref):
    other = mixed_rows(order, 1 - core_ref[0], rows_ref, weight_ref)
    out_ref[...] = (own_ref[...].astype(F32) + other).astype(BF16)


def mix(core, own, rows, weight, order):
    return pl.pallas_call(
        functools.partial(mix_kernel, order),
        out_shape=jax.ShapeDtypeStruct(own.shape, BF16),
        in_specs=[scalars(), whole(), whole(), whole()],
        out_specs=whole(),
        compiler_params=params(12),
        name="mix",
    )(core, own, rows, weight)


def down_most_kernel(*refs):
    *piece_refs, own_ref, other_ref, own_out_ref, other_out_ref = refs
    rows = jnp.concatenate([ref[...] for ref in piece_refs], axis=0)
    own_out_ref[...] = jnp.dot(rows, own_ref[...], preferred_element_type=F32).astype(BF16)
    other_out_ref[...] = jnp.dot(rows, other_ref[...], preferred_element_type=F32).astype(BF16)


def down_most(pieces, own_weight, other_weight):
    shape = jax.ShapeDtypeStruct((len(pieces) * pieces[0].shape[0], own_weight.shape[1]), BF16)
    return pl.pallas_call(
        down_most_kernel,
        out_shape=(shape, shape),
        in_specs=[whole()] * (len(pieces) + 2),
        out_specs=(whole(), whole()),
        compiler_params=params(16),
        cost_estimate=HEAVY,
        name="down_most",
    )(*pieces, own_weight, other_weight)


def down_kernel(order, z_ref, own_most_ref, other_most_ref, rows_ref, own_ref, other_ref, out_ref):
    _, _, ffn_count, micro = order
    shares = []
    for most_ref, weight_ref in ((own_most_ref, own_ref), (other_most_ref, other_ref)):
        last = jnp.dot(rows_ref[...], weight_ref[...], preferred_element_type=F32).astype(BF16)
        shares.append(jnp.concatenate([most_ref[...], last], axis=0))
    me = z_ref[0]
    out_ref[...] = spread_shares(order, *shares, lambda z, f, m: ((z ^ me) * ffn_count + f) * micro + m)


def down(z, most, last, own_weight, other_weight, order):
    rows = most[0].shape[0] + last.shape[0]
    return pl.pallas_call(
        functools.partial(down_kernel, order),
        out_shape=jax.ShapeDtypeStruct((2 * rows, own_weight.shape[1]), BF16),
        in_specs=[scalars()] + [whole()] * 5,
        out_specs=whole(),
        compiler_params=params(16),
        name="down",
    )(z, *most, last, own_weight, other_weight)


def fetch_kernel(cuts, *refs):
    count = (len(refs) - 1) // 2
    sources, targets, sems = refs[:count], refs[count : 2 * count], refs[2 * count]
    copies = []
    for i in range(count):
        rows = sources[i].shape[0] // cuts
        for j in range(cuts):
            part = pl.ds(j * rows, rows)
            copies.append(pltpu.make_async_copy(sources[i].at[part], targets[i].at[part], sems.at[i * cuts + j]))
    for copy in copies:
        copy.start()
    for copy in copies:
        copy.wait()


def fetch(*arrays):
    cuts = 4
    return pl.pallas_call(
        functools.partial(fetch_kernel, cuts),
        out_shape=[jax.ShapeDtypeStruct(array.shape, array.dtype) for array in arrays],
        in_specs=[in_hbm()] * len(arrays),
        out_specs=[whole()] * len(arrays),
        scratch_shapes=[pltpu.SemaphoreType.DMA((len(arrays) * cuts,))],
        compiler_params=params(16),
        cost_estimate=HEAVY,
        name="fetch",
    )(*arrays)


def sum_parts(parts_ref):
    total = parts_ref[0].astype(F32)
    for j in range(1, parts_ref.shape[0]):
        total = total + parts_ref[j].astype(F32)
    return total


def stream_kernel(order, f_ref, core_ref, parts_ref, hidden_ref, stream_ref, send_ref, copies_ref):
    z_count, core_count, ffn_count, micro = order
    rows = stream_ref.shape[0]
    f = f_ref[0]

    def source(r):
        return ((r % micro) * z_count * core_count + r // micro) * ffn_count + f

    spread = one_hot((rows, hidden_ref.shape[0]), source).astype(BF16)
    hidden = jnp.dot(spread, hidden_ref[...], preferred_element_type=F32)
    stream = (hidden + sum_parts(parts_ref)).astype(BF16)
    stream_ref[...] = stream
    for j in range(copies_ref.shape[0]):
        copies_ref[j] = stream

    def other(r):
        row = ((r // micro) * core_count + 1 - core_ref[0]) * micro + r % micro
        return jnp.where(r < z_count * micro, row, -1)

    pick = one_hot((FEW, rows), other).astype(BF16)
    send_ref[...] = jnp.dot(pick, stream, preferred_element_type=F32).astype(BF16)


def make_stream(f, core, parts, hidden, order):
    _, rows, width = parts.shape
    return pl.pallas_call(
        functools.partial(stream_kernel, order),
        out_shape=(
            jax.ShapeDtypeStruct((rows, width), BF16),
            jax.ShapeDtypeStruct((FEW, width), BF16),
            jax.ShapeDtypeStruct(parts.shape, BF16),
        ),
        in_specs=[scalars()] * 2 + [whole()] * 2,
        out_specs=(whole(), whole(), whole()),
        compiler_params=params(8),
        name="make_stream",
    )(f, core, parts, hidden)


def squares_rows(row_values, width):
    high = row_values.astype(BF16).astype(F32)
    low = row_values - high
    index = lax.broadcasted_iota(jnp.int32, (SQ_ROWS, width), 0)
    return jnp.where(index == 0, high, jnp.where(index == 1, low, 0.0)).astype(BF16)


def up_kernel(order, hops, z_ref, core_ref, stream_ref, gain_ref, gate_ref, up_ref, *out_refs):
    z_count, core_count, ffn_count, micro = order
    tiles = gate_ref.shape[1] // LANES
    rows = ffn_count * micro
    me = z_ref[0]
    core = core_ref[0]

    def source(r):
        m = r % micro
        f = (r // micro) % ffn_count
        block = r // rows
        side = block // len(hops)
        hop = hops[0] + (hops[1] - hops[0]) * (block % len(hops))
        return ((f * z_count + (me ^ hop)) * core_count + (core ^ side)) * micro + m

    spread = one_hot((len(out_refs) * rows, stream_ref.shape[0]), source).astype(BF16)
    stream = jnp.dot(spread, stream_ref[...], preferred_element_type=F32)
    scaled = (stream * gain_ref[...].astype(F32)).astype(BF16)
    squares = jnp.sum(stream * stream, axis=1, keepdims=True)
    lane = one_hot((rows, LANES), lambda r: r)
    for i, out_ref in enumerate(out_refs):
        sums = jnp.sum(lane * squares[i * rows : (i + 1) * rows], axis=0, keepdims=True)
        out_ref[2 * tiles * rows :, :] = squares_rows(sums, LANES)
    for half, weight_ref in enumerate((gate_ref, up_ref)):
        product = jnp.dot(scaled, weight_ref[...], preferred_element_type=F32).astype(BF16)
        for i, out_ref in enumerate(out_refs):
            for j in range(tiles):
                at = (half * tiles + j) * rows
                out_ref[at : at + rows, :] = product[i * rows : (i + 1) * rows, j * LANES : (j + 1) * LANES]


def up_part(order, hops, z, core, stream_all, gain, gate_weight, up_weight):
    _, _, ffn_count, micro = order
    out_rows = 2 * gate_weight.shape[1] // LANES * ffn_count * micro + SQ_ROWS
    shape = jax.ShapeDtypeStruct((out_rows, LANES), BF16)
    return pl.pallas_call(
        functools.partial(up_kernel, order, hops),
        out_shape=[shape] * (2 * len(hops)),
        in_specs=[scalars(), scalars(), whole(), whole(), whole(), whole()],
        out_specs=[whole()] * (2 * len(hops)),
        compiler_params=params(16),
        cost_estimate=HEAVY,
        name="up_part",
    )(z, core, stream_all, gain, gate_weight, up_weight)


def sum_blocks(refs, start, stop):
    total = refs[0][start:stop, :].astype(F32)
    for ref in refs[1:]:
        total = total + ref[start:stop, :].astype(F32)
    return total


def add_kernel(*refs):
    *block_refs, out_ref = refs
    out_rows, lanes = out_ref.shape
    body = out_rows - SQ_ROWS
    out_ref[:body, :] = sum_blocks(block_refs, 0, body).astype(BF16)
    tail = sum_blocks(block_refs, body, out_rows)
    out_ref[body:, :] = squares_rows(tail[0:1] + tail[1:2], lanes)


def add(*blocks):
    return pl.pallas_call(
        add_kernel,
        out_shape=jax.ShapeDtypeStruct(blocks[0].shape, BF16),
        in_specs=[whole()] * len(blocks),
        out_specs=whole(),
        compiler_params=params(8),
        name="add",
    )(*blocks)


def activate_kernel(model_width, *refs):
    *block_refs, out_ref = refs
    out_rows, lanes = block_refs[0].shape
    rows, hidden = out_ref.shape
    tiles = hidden // lanes
    tail = sum_blocks(block_refs, out_rows - SQ_ROWS, out_rows)
    lane_sums = tail[0:1] + tail[1:2]
    spread = one_hot((rows, lanes), lambda r: r)
    squares = jnp.sum(spread * lane_sums, axis=1, keepdims=True)
    scale = lax.rsqrt(squares / model_width + EPSILON)
    for j in range(tiles):
        gate = sum_blocks(block_refs, j * rows, (j + 1) * rows) * scale
        upward = sum_blocks(block_refs, (tiles + j) * rows, (tiles + j + 1) * rows) * scale
        out_ref[:, j * lanes : (j + 1) * lanes] = (gate / (1.0 + jnp.exp(-gate)) * upward).astype(BF16)


def activate(blocks, rows, hidden, model_width):
    return pl.pallas_call(
        functools.partial(activate_kernel, model_width),
        out_shape=jax.ShapeDtypeStruct((rows, hidden), BF16),
        in_specs=[whole()] * len(blocks),
        out_specs=whole(),
        compiler_params=params(8),
        name="activate",
    )(*blocks)


def finish_kernel(order, z_ref, core_ref, parts_ref, stream_ref, received_ref, *out_refs):
    z_count, core_count, _, micro = order
    rows = stream_ref.shape[0]
    half = rows // 2

    def own(r):
        return jnp.where(r < half, ((r // micro) * core_count + core_ref[0]) * micro + r % micro, -1)

    first = one_hot((rows, rows), own).astype(BF16)
    second = one_hot((rows, FEW), lambda r: r - half).astype(BF16)
    stream = jnp.dot(first, stream_ref[...], preferred_element_type=F32)
    stream = stream + jnp.dot(second, received_ref[...], preferred_element_type=F32)
    finished = (stream + sum_parts(parts_ref)).astype(BF16)
    slots = out_refs[0].shape[0]
    me = z_ref[0]

    def source(r):
        q = r % slots
        at = (q // micro) * half + ((r // slots) ^ me) * micro + q % micro
        return jnp.where(q < 2 * micro, at, -1)

    spread = one_hot((len(out_refs) * slots, rows), source).astype(BF16)
    blocks = jnp.dot(spread, finished, preferred_element_type=F32)
    for k, out_ref in enumerate(out_refs):
        out_ref[...] = blocks[k * slots : (k + 1) * slots].astype(BF16)


def finish(z, core, parts, stream, received, order):
    z_count, _, _, micro = order
    slots = -(-2 * micro // 8) * 8
    return pl.pallas_call(
        functools.partial(finish_kernel, order),
        out_shape=[jax.ShapeDtypeStruct((slots, stream.shape[1]), BF16)] * z_count,
        in_specs=[scalars()] * 2 + [whole()] * 3,
        out_specs=[whole()] * z_count,
        compiler_params=params(8),
        name="finish",
    )(z, core, parts, stream, received)


def place_kernel(z_ref, core_ref, *refs):
    *piece_refs, out_ref = refs
    width = piece_refs[0].shape[1]
    micro = out_ref.shape[0]
    for k, ref in enumerate(piece_refs):
        block = ref[...].astype(F32)
        for side in range(2):
            share = 2 * (z_ref[0] ^ k) + (core_ref[0] ^ side)
            at = pl.multiple_of(share * width, LANES)
            out_ref[:, pl.ds(at, width)] = block[side * micro : (side + 1) * micro].astype(BF16)


def place(z, core, pieces, micro):
    width = pieces[0].shape[1]
    return pl.pallas_call(
        place_kernel,
        out_shape=jax.ShapeDtypeStruct((micro, 2 * len(pieces) * width), BF16),
        in_specs=[scalars(), scalars()] + [whole()] * len(pieces),
        out_specs=whole(),
        compiler_params=params(8),
        name="place",
    )(z, core, *pieces)


def along_z(array, hop):
    return lax.ppermute(array, Z, [(i, i ^ hop) for i in range(lax.axis_size(Z))])


def swap_cores(array):
    return lax.ppermute(array, CORE, [(0, 1), (1, 0)])


def per_device(
    hidden_in,
    queries,
    key_cache,
    value_cache,
    lengths,
    cache_slot,
    out_weight,
    ffn_gain,
    gate_weight,
    up_weight,
    down_weight,
):
    z_count = lax.axis_size(Z)
    core_count = lax.axis_size(CORE)
    attn_count = z_count * core_count
    ffn_count = lax.axis_size("x") * lax.axis_size("y")
    f_index = lax.axis_index(FFN).astype(jnp.int32)[None]
    z_index = lax.axis_index(Z).astype(jnp.int32)[None]
    core_index = lax.axis_index(CORE).astype(jnp.int32)[None]
    micro, total_rows, col_share = hidden_in.shape
    head_dim = key_cache.shape[2]
    model_width = col_share * attn_count
    hidden_share = gate_weight.shape[1]
    rows_chunk = attn_count * micro
    rows_all = ffn_count * rows_chunk
    rows_block = rows_all // attn_count

    order = (z_count, core_count, ffn_count, micro)
    payload = attend(
        queries.reshape(micro, -1), key_cache, value_cache, cache_slot.T, lengths.T, z_count, ffn_count
    )
    tile_rows = payload.shape[3]
    payload, f_index, z_index, core_index = lax.optimization_barrier((payload, f_index, z_index, core_index))
    payload = payload.reshape(z_count * ffn_count, micro * tile_rows, LANES)
    incoming = lax.all_to_all(payload, (Z,) + FFN, split_axis=0, concat_axis=0, tiled=True)
    own_rows = to_rows(incoming.reshape(z_count * ffn_count * micro, tile_rows, LANES), head_dim // LANES)
    own_rows, ffn_gain = lax.optimization_barrier((own_rows, ffn_gain))
    other_rows = swap_cores(own_rows)
    gain = ffn_gain[None, :]
    own_mixed = product_of(core_index, own_rows, out_weight, order)
    own_mixed, other_rows, gain = lax.optimization_barrier((own_mixed, other_rows, gain))
    mixed = mix(core_index, own_mixed, other_rows, out_weight, order)

    parts = lax.all_to_all(
        mixed.reshape(ffn_count, rows_chunk, col_share), FFN, split_axis=0, concat_axis=0, tiled=True
    )
    stream, send, copies = make_stream(f_index, core_index, parts, hidden_in.reshape(rows_all, col_share), order)
    stream_all = lax.all_to_all(copies, FFN, split_axis=0, concat_axis=0, tiled=True)
    stream_all = stream_all.reshape(rows_all, col_share)

    up_args = (z_index, core_index, stream_all, gain, gate_weight, up_weight)
    own3, own1, other3, other1 = up_part(order, (3, 1), *up_args)
    own0, own2, other0, other2 = up_part(order, (0, 2), *up_args)
    received3, received1, own0 = lax.optimization_barrier((swap_cores(other3), swap_cores(other1), own0))
    relayed3 = add(own3, received3)
    near1 = add(own1, received1)
    relayed3, other0, other2 = lax.optimization_barrier((relayed3, other0, other2))
    crossing = along_z(relayed3, 1)
    relayed = add(own2, swap_cores(other2), crossing)
    relayed, send = lax.optimization_barrier((relayed, send))
    from_far = along_z(relayed, 2)
    from_near = along_z(near1, 1)
    down_weight, near1 = lax.optimization_barrier((down_weight, near1))
    down_own, down_other = fetch(down_weight, swap_cores(down_weight))
    from_far, down_own, down_other = lax.optimization_barrier((from_far, down_own, down_other))
    activated = activate((own0, swap_cores(other0), from_near, from_far), rows_block, hidden_share, model_width)

    far = along_z(activated, 2)
    near = along_z(activated, 1)
    far, received = lax.optimization_barrier((far, swap_cores(send)))
    most = down_most((activated, near, far), down_own, down_other)
    lowered = down(z_index, most, along_z(far, 1), down_own, down_other, order)
    lowered_parts = lax.all_to_all(
        lowered.reshape(ffn_count, rows_chunk, col_share), FFN, split_axis=0, concat_axis=0, tiled=True
    )
    shares = finish(z_index, core_index, lowered_parts, stream, received, order)
    pieces = [shares[0]] + [along_z(shares[hop], hop) for hop in range(1, z_count)]
    return place(z_index, core_index, pieces, micro).reshape(micro, 1, model_width)


def solution(mesh):
    sizes = dict(mesh.shape)
    attn_count, ffn_count, rep_count = sizes["attn"], sizes["ffn"], sizes["rep"]
    side = int(round(ffn_count**0.5))
    fine = Mesh(
        mesh.devices.reshape(attn_count // 2, 2, side, ffn_count // side, rep_count),
        (Z, CORE, "x", "y", REP),
    )
    owners = (REP, Z, CORE, "x", "y")
    return jax.shard_map(
        per_device,
        mesh=fine,
        in_specs=(
            P(None, REP, ATTN),
            P(None, owners, None),
            P(owners, None, None),
            P(owners, None, None),
            P(None, owners),
            P(None, owners),
            P(FFN, ATTN),
            P(ATTN),
            P(ATTN, FFN),
            P(ATTN, FFN),
            P(FFN, ATTN),
        ),
        out_specs=P(None, owners, None),
        check_vma=False,
    )
```

```python
import functools

import jax
import jax.numpy as jnp
from jax import lax
from jax.experimental import pallas as pl
from jax.experimental.pallas import tpu as pltpu
from jax.sharding import Mesh, PartitionSpec as P

EPSILON = 1e-06
MASKED = -1e30
Z = "z"
CORE = "core"
ATTN = (Z, CORE)
FFN = ("x", "y")
REP = "rep"
LANES = 128
SQ_ROWS = 16
FEW = 16
BF16 = jnp.bfloat16
F32 = jnp.float32
HEAVY = pl.CostEstimate(flops=10**10, bytes_accessed=10**7, transcendentals=0)


def whole():
    return pl.BlockSpec(memory_space=pltpu.VMEM)


def scalars():
    return pl.BlockSpec(memory_space=pltpu.SMEM)


def in_hbm():
    return pl.BlockSpec(memory_space=pltpu.HBM)


def params(mib):
    return pltpu.CompilerParams(vmem_limit_bytes=mib * 1024 * 1024)


def one_hot(shape, source_of_row):
    rows = lax.broadcasted_iota(jnp.int32, (shape[0], 1), 0)
    cols = lax.broadcasted_iota(jnp.int32, shape, 1)
    return jnp.where(cols == source_of_row(rows), 1.0, 0.0)


def attention_kernel(
    slot_hbm,
    length_hbm,
    query_hbm,
    key_hbm,
    value_hbm,
    out_ref,
    slots,
    lengths,
    queries,
    keys,
    values,
    wide,
    small_sem,
    key_sem,
    value_sem,
):
    slot_count, pos, head_dim = keys.shape
    micro, width = queries.shape
    heads = width // head_dim
    copies, blocks, _, tile_rows, _ = out_ref.shape
    small = [
        pltpu.make_async_copy(source, target, small_sem.at[i])
        for i, (source, target) in enumerate(((query_hbm, queries), (slot_hbm, slots), (length_hbm, lengths)))
    ]
    key_copies = [pltpu.make_async_copy(key_hbm.at[s], keys.at[s], key_sem.at[s]) for s in range(slot_count)]
    value_copies = [pltpu.make_async_copy(value_hbm.at[s], values.at[s], value_sem.at[s]) for s in range(slot_count)]
    for copy in small + key_copies + value_copies:
        copy.start()
    for copy in small:
        copy.wait()
    for h in range(heads):
        wide[:, h, :] = queries[:, h * head_dim : (h + 1) * head_dim].astype(F32)
    pieces = head_dim // LANES
    group = heads // blocks
    positions = lax.broadcasted_iota(jnp.int32, (heads, pos), 1)
    requests = []
    scores = []
    for s in range(slot_count):
        request = micro - 1
        for m in range(micro - 1):
            request = jnp.where(slots[0, m] == s, m, request)
        requests.append(request)
        query = wide[request].astype(BF16)
        key_copies[s].wait()
        scores.append(lax.dot_general(query, keys[s], (((1,), (1,)), ((), ())), preferred_element_type=F32))
    softened = []
    totals = []
    for s in range(slot_count):
        in_cache = positions < lengths[0, requests[s]]
        masked = jnp.where(in_cache, scores[s] * head_dim ** (-0.5), MASKED)
        highest = jnp.max(masked, axis=1, keepdims=True)
        weights = jnp.where(in_cache, jnp.exp(masked - highest), 0.0)
        totals.append(jnp.sum(weights, axis=1, keepdims=True))
        softened.append(weights.astype(BF16))
    for copy in value_copies:
        copy.wait()
    for s in range(slot_count):
        weighted = jnp.dot(softened[s], values[s], preferred_element_type=F32)
        attended = weighted / totals[s]
        for piece in range(pieces):
            part = attended[:, piece * LANES : (piece + 1) * LANES].reshape(blocks, group, LANES).astype(BF16)
            for copy in range(copies):
                out_ref[copy, :, requests[s], piece * group : (piece + 1) * group, :] = part


def attend(queries, key_cache, value_cache, slots, lengths, z_count, ffn_count):
    slot_count, pos, head_dim = key_cache.shape
    micro, width = queries.shape
    tile_rows = width // ffn_count // LANES
    return pl.pallas_call(
        attention_kernel,
        in_specs=[in_hbm()] * 5,
        out_specs=whole(),
        out_shape=jax.ShapeDtypeStruct((z_count, ffn_count, micro, tile_rows, LANES), BF16),
        scratch_shapes=[
            pltpu.SMEM(slots.shape, jnp.int32),
            pltpu.SMEM(lengths.shape, jnp.int32),
            pltpu.VMEM(queries.shape, BF16),
            pltpu.VMEM((slot_count, pos, head_dim), BF16),
            pltpu.VMEM((slot_count, pos, head_dim), BF16),
            pltpu.VMEM((micro, width // head_dim, head_dim), F32),
            pltpu.SemaphoreType.DMA((3,)),
            pltpu.SemaphoreType.DMA((slot_count,)),
            pltpu.SemaphoreType.DMA((slot_count,)),
        ],
        compiler_params=params(60),
        name="attention",
    )(slots, lengths, queries, key_cache, value_cache)


def rows_kernel(pieces, in_ref, out_ref, wide):
    rows, tile_rows, lanes = in_ref.shape
    wide[...] = in_ref[...].astype(F32).reshape(rows * tile_rows, lanes)
    group = tile_rows // pieces
    for j in range(tile_rows):
        at = (j % pieces) * group + j // pieces
        out_ref[:, j * lanes : (j + 1) * lanes] = wide[pl.ds(at, rows, stride=tile_rows), :].astype(BF16)


def to_rows(tiles, pieces):
    rows, tile_rows, lanes = tiles.shape
    return pl.pallas_call(
        functools.partial(rows_kernel, pieces),
        out_shape=jax.ShapeDtypeStruct((rows, tile_rows * lanes), BF16),
        in_specs=[whole()],
        out_specs=whole(),
        scratch_shapes=[pltpu.VMEM((rows * tile_rows, lanes), F32)],
        compiler_params=params(8),
        name="to_rows",
    )(tiles)


def mixed_rows(order, core, rows_ref, weight_ref):
    z_count, core_count, ffn_count, micro = order
    product = jnp.dot(rows_ref[...], weight_ref[...], preferred_element_type=F32).astype(BF16)

    def source(r):
        m = r % micro
        c = (r // micro) % core_count
        z = (r // (micro * core_count)) % z_count
        f = r // (micro * core_count * z_count)
        return jnp.where(c == core, (z * ffn_count + f) * micro + m, -1)

    spread = one_hot((core_count * product.shape[0], product.shape[0]), source).astype(BF16)
    return jnp.dot(spread, product, preferred_element_type=F32)


def product_kernel(order, core_ref, rows_ref, weight_ref, out_ref):
    out_ref[...] = mixed_rows(order, core_ref[0], rows_ref, weight_ref).astype(BF16)


def product_of(core, rows, weight, order):
    return pl.pallas_call(
        functools.partial(product_kernel, order),
        out_shape=jax.ShapeDtypeStruct((2 * rows.shape[0], weight.shape[1]), BF16),
        in_specs=[scalars(), whole(), whole()],
        out_specs=whole(),
        compiler_params=params(12),
        cost_estimate=HEAVY,
        name="product",
    )(core, rows, weight)


def mix_kernel(order, core_ref, own_ref, rows_ref, weight_ref, out_ref):
    other = mixed_rows(order, 1 - core_ref[0], rows_ref, weight_ref)
    out_ref[...] = (own_ref[...].astype(F32) + other).astype(BF16)


def mix(core, own, rows, weight, order):
    return pl.pallas_call(
        functools.partial(mix_kernel, order),
        out_shape=jax.ShapeDtypeStruct(own.shape, BF16),
        in_specs=[scalars(), whole(), whole(), whole()],
        out_specs=whole(),
        compiler_params=params(12),
        name="mix",
    )(core, own, rows, weight)


def placed_rows(order, me, hops, rows, own_ref, other_ref):
    z_count, _, ffn_count, micro = order
    count = rows.shape[0]
    shares = [
        jnp.dot(rows, ref[...], preferred_element_type=F32).astype(BF16) for ref in (own_ref, other_ref)
    ]

    def source(r):
        m = r % micro
        hop = ((r // micro) % z_count) ^ me
        share = (r // (micro * z_count)) % 2
        f = r // (micro * z_count * 2)
        at = share * count + ((hop - hops[0]) * ffn_count + f) * micro + m
        return jnp.where(jnp.logical_and(hop >= hops[0], hop <= hops[-1]), at, -1)

    spread = one_hot((2 * z_count * ffn_count * micro, 2 * count), source).astype(BF16)
    return jnp.dot(spread, jnp.concatenate(shares, axis=0), preferred_element_type=F32)


def down_most_kernel(order, z_ref, *refs):
    *piece_refs, own_ref, other_ref, out_ref = refs
    rows = jnp.concatenate([ref[...] for ref in piece_refs], axis=0)
    hops = range(len(piece_refs))
    out_ref[...] = placed_rows(order, z_ref[0], hops, rows, own_ref, other_ref).astype(BF16)


def down_most(z, pieces, own_weight, other_weight, order):
    z_count, _, ffn_count, micro = order
    return pl.pallas_call(
        functools.partial(down_most_kernel, order),
        out_shape=jax.ShapeDtypeStruct((2 * z_count * ffn_count * micro, own_weight.shape[1]), BF16),
        in_specs=[scalars()] + [whole()] * (len(pieces) + 2),
        out_specs=whole(),
        compiler_params=params(16),
        cost_estimate=HEAVY,
        name="down_most",
    )(z, *pieces, own_weight, other_weight)


def down_kernel(order, z_ref, most_ref, rows_ref, own_ref, other_ref, out_ref):
    last = placed_rows(order, z_ref[0], (order[0] - 1,), rows_ref[...], own_ref, other_ref)
    out_ref[...] = (most_ref[...].astype(F32) + last).astype(BF16)


def down(z, most, last, own_weight, other_weight, order):
    return pl.pallas_call(
        functools.partial(down_kernel, order),
        out_shape=jax.ShapeDtypeStruct(most.shape, BF16),
        in_specs=[scalars()] + [whole()] * 4,
        out_specs=whole(),
        compiler_params=params(16),
        name="down",
    )(z, most, last, own_weight, other_weight)


def fetch_kernel(cuts, *refs):
    count = (len(refs) - 1) // 2
    sources, targets, sems = refs[:count], refs[count : 2 * count], refs[2 * count]
    copies = []
    for i in range(count):
        rows = sources[i].shape[0] // cuts
        for j in range(cuts):
            part = pl.ds(j * rows, rows)
            copies.append(pltpu.make_async_copy(sources[i].at[part], targets[i].at[part], sems.at[i * cuts + j]))
    for copy in copies:
        copy.start()
    for copy in copies:
        copy.wait()


def fetch(*arrays):
    cuts = 4
    return pl.pallas_call(
        functools.partial(fetch_kernel, cuts),
        out_shape=[jax.ShapeDtypeStruct(array.shape, array.dtype) for array in arrays],
        in_specs=[in_hbm()] * len(arrays),
        out_specs=[whole()] * len(arrays),
        scratch_shapes=[pltpu.SemaphoreType.DMA((len(arrays) * cuts,))],
        compiler_params=params(16),
        cost_estimate=HEAVY,
        name="fetch",
    )(*arrays)


def sum_parts(parts_ref):
    total = parts_ref[0].astype(F32)
    for j in range(1, parts_ref.shape[0]):
        total = total + parts_ref[j].astype(F32)
    return total


def stream_kernel(order, f_ref, core_ref, parts_ref, hidden_ref, stream_ref, send_ref, copies_ref):
    z_count, core_count, ffn_count, micro = order
    rows = stream_ref.shape[0]
    f = f_ref[0]

    def source(r):
        return ((r % micro) * z_count * core_count + r // micro) * ffn_count + f

    spread = one_hot((rows, hidden_ref.shape[0]), source).astype(BF16)
    hidden = jnp.dot(spread, hidden_ref[...], preferred_element_type=F32)
    stream = (hidden + sum_parts(parts_ref)).astype(BF16)
    stream_ref[...] = stream
    for j in range(copies_ref.shape[0]):
        copies_ref[j] = stream

    def other(r):
        row = ((r // micro) * core_count + 1 - core_ref[0]) * micro + r % micro
        return jnp.where(r < z_count * micro, row, -1)

    pick = one_hot((FEW, rows), other).astype(BF16)
    send_ref[...] = jnp.dot(pick, stream, preferred_element_type=F32).astype(BF16)


def make_stream(f, core, parts, hidden, order):
    _, rows, width = parts.shape
    return pl.pallas_call(
        functools.partial(stream_kernel, order),
        out_shape=(
            jax.ShapeDtypeStruct((rows, width), BF16),
            jax.ShapeDtypeStruct((FEW, width), BF16),
            jax.ShapeDtypeStruct(parts.shape, BF16),
        ),
        in_specs=[scalars()] * 2 + [whole()] * 2,
        out_specs=(whole(), whole(), whole()),
        compiler_params=params(8),
        name="make_stream",
    )(f, core, parts, hidden)


def squares_rows(row_values, width):
    high = row_values.astype(BF16).astype(F32)
    low = row_values - high
    index = lax.broadcasted_iota(jnp.int32, (SQ_ROWS, width), 0)
    return jnp.where(index == 0, high, jnp.where(index == 1, low, 0.0)).astype(BF16)


def up_kernel(order, hops, z_ref, core_ref, stream_ref, gain_ref, gate_ref, up_ref, *out_refs):
    z_count, core_count, ffn_count, micro = order
    tiles = gate_ref.shape[1] // LANES
    rows = ffn_count * micro
    me = z_ref[0]
    core = core_ref[0]

    def source(r):
        m = r % micro
        f = (r // micro) % ffn_count
        block = r // rows
        side = block // len(hops)
        hop = hops[0] + (hops[1] - hops[0]) * (block % len(hops))
        return ((f * z_count + (me ^ hop)) * core_count + (core ^ side)) * micro + m

    spread = one_hot((len(out_refs) * rows, stream_ref.shape[0]), source).astype(BF16)
    stream = jnp.dot(spread, stream_ref[...], preferred_element_type=F32)
    scaled = (stream * gain_ref[...].astype(F32)).astype(BF16)
    squares = jnp.sum(stream * stream, axis=1, keepdims=True)
    lane = one_hot((rows, LANES), lambda r: r)
    for i, out_ref in enumerate(out_refs):
        sums = jnp.sum(lane * squares[i * rows : (i + 1) * rows], axis=0, keepdims=True)
        out_ref[2 * tiles * rows :, :] = squares_rows(sums, LANES)
    for half, weight_ref in enumerate((gate_ref, up_ref)):
        product = jnp.dot(scaled, weight_ref[...], preferred_element_type=F32).astype(BF16)
        for i, out_ref in enumerate(out_refs):
            for j in range(tiles):
                at = (half * tiles + j) * rows
                out_ref[at : at + rows, :] = product[i * rows : (i + 1) * rows, j * LANES : (j + 1) * LANES]


def up_part(order, hops, z, core, stream_all, gain, gate_weight, up_weight):
    _, _, ffn_count, micro = order
    out_rows = 2 * gate_weight.shape[1] // LANES * ffn_count * micro + SQ_ROWS
    shape = jax.ShapeDtypeStruct((out_rows, LANES), BF16)
    return pl.pallas_call(
        functools.partial(up_kernel, order, hops),
        out_shape=[shape] * (2 * len(hops)),
        in_specs=[scalars(), scalars(), whole(), whole(), whole(), whole()],
        out_specs=[whole()] * (2 * len(hops)),
        compiler_params=params(16),
        cost_estimate=HEAVY,
        name="up_part",
    )(z, core, stream_all, gain, gate_weight, up_weight)


def sum_blocks(refs, start, stop):
    total = refs[0][start:stop, :].astype(F32)
    for ref in refs[1:]:
        total = total + ref[start:stop, :].astype(F32)
    return total


def add_kernel(*refs):
    *block_refs, out_ref = refs
    out_rows, lanes = out_ref.shape
    body = out_rows - SQ_ROWS
    out_ref[:body, :] = sum_blocks(block_refs, 0, body).astype(BF16)
    tail = sum_blocks(block_refs, body, out_rows)
    out_ref[body:, :] = squares_rows(tail[0:1] + tail[1:2], lanes)


def add(*blocks):
    return pl.pallas_call(
        add_kernel,
        out_shape=jax.ShapeDtypeStruct(blocks[0].shape, BF16),
        in_specs=[whole()] * len(blocks),
        out_specs=whole(),
        compiler_params=params(8),
        name="add",
    )(*blocks)


def activate_kernel(model_width, *refs):
    *block_refs, out_ref = refs
    out_rows, lanes = block_refs[0].shape
    rows, hidden = out_ref.shape
    tiles = hidden // lanes
    tail = sum_blocks(block_refs, out_rows - SQ_ROWS, out_rows)
    lane_sums = tail[0:1] + tail[1:2]
    spread = one_hot((rows, lanes), lambda r: r)
    squares = jnp.sum(spread * lane_sums, axis=1, keepdims=True)
    scale = lax.rsqrt(squares / model_width + EPSILON)
    for j in range(tiles):
        gate = sum_blocks(block_refs, j * rows, (j + 1) * rows) * scale
        upward = sum_blocks(block_refs, (tiles + j) * rows, (tiles + j + 1) * rows) * scale
        out_ref[:, j * lanes : (j + 1) * lanes] = (gate / (1.0 + jnp.exp(-gate)) * upward).astype(BF16)


def activate(blocks, rows, hidden, model_width):
    return pl.pallas_call(
        functools.partial(activate_kernel, model_width),
        out_shape=jax.ShapeDtypeStruct((rows, hidden), BF16),
        in_specs=[whole()] * len(blocks),
        out_specs=whole(),
        compiler_params=params(8),
        name="activate",
    )(*blocks)


def finish_kernel(order, z_ref, core_ref, parts_ref, stream_ref, received_ref, *out_refs):
    z_count, core_count, _, micro = order
    rows = stream_ref.shape[0]
    half = rows // 2

    def own(r):
        return jnp.where(r < half, ((r // micro) * core_count + core_ref[0]) * micro + r % micro, -1)

    first = one_hot((rows, rows), own).astype(BF16)
    second = one_hot((rows, FEW), lambda r: r - half).astype(BF16)
    stream = jnp.dot(first, stream_ref[...], preferred_element_type=F32)
    stream = stream + jnp.dot(second, received_ref[...], preferred_element_type=F32)
    finished = (stream + sum_parts(parts_ref)).astype(BF16)
    slots = out_refs[0].shape[0]
    me = z_ref[0]

    def source(r):
        q = r % slots
        at = (q // micro) * half + ((r // slots) ^ me) * micro + q % micro
        return jnp.where(q < 2 * micro, at, -1)

    spread = one_hot((len(out_refs) * slots, rows), source).astype(BF16)
    blocks = jnp.dot(spread, finished, preferred_element_type=F32)
    for k, out_ref in enumerate(out_refs):
        out_ref[...] = blocks[k * slots : (k + 1) * slots].astype(BF16)


def finish(z, core, parts, stream, received, order):
    z_count, _, _, micro = order
    slots = -(-2 * micro // 8) * 8
    return pl.pallas_call(
        functools.partial(finish_kernel, order),
        out_shape=[jax.ShapeDtypeStruct((slots, stream.shape[1]), BF16)] * z_count,
        in_specs=[scalars()] * 2 + [whole()] * 3,
        out_specs=[whole()] * z_count,
        compiler_params=params(8),
        name="finish",
    )(z, core, parts, stream, received)


def place_kernel(z_ref, core_ref, *refs):
    *piece_refs, out_ref = refs
    width = piece_refs[0].shape[1]
    micro = out_ref.shape[0]
    for k, ref in enumerate(piece_refs):
        block = ref[...].astype(F32)
        for side in range(2):
            share = 2 * (z_ref[0] ^ k) + (core_ref[0] ^ side)
            at = pl.multiple_of(share * width, LANES)
            out_ref[:, pl.ds(at, width)] = block[side * micro : (side + 1) * micro].astype(BF16)


def place(z, core, pieces, micro):
    width = pieces[0].shape[1]
    return pl.pallas_call(
        place_kernel,
        out_shape=jax.ShapeDtypeStruct((micro, 2 * len(pieces) * width), BF16),
        in_specs=[scalars(), scalars()] + [whole()] * len(pieces),
        out_specs=whole(),
        compiler_params=params(8),
        name="place",
    )(z, core, *pieces)


def along_z(array, hop):
    return lax.ppermute(array, Z, [(i, i ^ hop) for i in range(lax.axis_size(Z))])


def swap_cores(array):
    return lax.ppermute(array, CORE, [(0, 1), (1, 0)])


def per_device(
    hidden_in,
    queries,
    key_cache,
    value_cache,
    lengths,
    cache_slot,
    out_weight,
    ffn_gain,
    gate_weight,
    up_weight,
    down_weight,
):
    z_count = lax.axis_size(Z)
    core_count = lax.axis_size(CORE)
    attn_count = z_count * core_count
    ffn_count = lax.axis_size("x") * lax.axis_size("y")
    f_index = lax.axis_index(FFN).astype(jnp.int32)[None]
    z_index = lax.axis_index(Z).astype(jnp.int32)[None]
    core_index = lax.axis_index(CORE).astype(jnp.int32)[None]
    micro, total_rows, col_share = hidden_in.shape
    head_dim = key_cache.shape[2]
    model_width = col_share * attn_count
    hidden_share = gate_weight.shape[1]
    rows_chunk = attn_count * micro
    rows_all = ffn_count * rows_chunk
    rows_block = rows_all // attn_count

    order = (z_count, core_count, ffn_count, micro)
    payload = attend(
        queries.reshape(micro, -1), key_cache, value_cache, cache_slot.T, lengths.T, z_count, ffn_count
    )
    tile_rows = payload.shape[3]
    payload, f_index, z_index, core_index = lax.optimization_barrier((payload, f_index, z_index, core_index))
    payload = payload.reshape(z_count * ffn_count, micro * tile_rows, LANES)
    incoming = lax.all_to_all(payload, (Z,) + FFN, split_axis=0, concat_axis=0, tiled=True)
    own_rows = to_rows(incoming.reshape(z_count * ffn_count * micro, tile_rows, LANES), head_dim // LANES)
    own_rows, ffn_gain = lax.optimization_barrier((own_rows, ffn_gain))
    other_rows = swap_cores(own_rows)
    gain = ffn_gain[None, :]
    own_mixed = product_of(core_index, own_rows, out_weight, order)
    own_mixed, other_rows, gain = lax.optimization_barrier((own_mixed, other_rows, gain))
    mixed = mix(core_index, own_mixed, other_rows, out_weight, order)

    parts = lax.all_to_all(
        mixed.reshape(ffn_count, rows_chunk, col_share), FFN, split_axis=0, concat_axis=0, tiled=True
    )
    stream, send, copies = make_stream(f_index, core_index, parts, hidden_in.reshape(rows_all, col_share), order)
    stream_all = lax.all_to_all(copies, FFN, split_axis=0, concat_axis=0, tiled=True)
    stream_all = stream_all.reshape(rows_all, col_share)

    up_args = (z_index, core_index, stream_all, gain, gate_weight, up_weight)
    own3, own1, other3, other1 = up_part(order, (3, 1), *up_args)
    own0, own2, other0, other2 = up_part(order, (0, 2), *up_args)
    received3, received1, own0 = lax.optimization_barrier((swap_cores(other3), swap_cores(other1), own0))
    relayed3 = add(own3, received3)
    near1 = add(own1, received1)
    relayed3, other0, other2 = lax.optimization_barrier((relayed3, other0, other2))
    crossing = along_z(relayed3, 1)
    relayed = add(own2, swap_cores(other2), crossing)
    relayed, send = lax.optimization_barrier((relayed, send))
    from_far = along_z(relayed, 2)
    from_near = along_z(near1, 1)
    down_weight, near1 = lax.optimization_barrier((down_weight, near1))
    down_own, down_other = fetch(down_weight, swap_cores(down_weight))
    from_far, down_own, down_other = lax.optimization_barrier((from_far, down_own, down_other))
    activated = activate((own0, swap_cores(other0), from_near, from_far), rows_block, hidden_share, model_width)

    far = along_z(activated, 2)
    near = along_z(activated, 1)
    far, received = lax.optimization_barrier((far, swap_cores(send)))
    most = down_most(z_index, (activated, near, far), down_own, down_other, order)
    lowered = down(z_index, most, along_z(far, 1), down_own, down_other, order)
    lowered_parts = lax.all_to_all(
        lowered.reshape(ffn_count, rows_chunk, col_share), FFN, split_axis=0, concat_axis=0, tiled=True
    )
    shares = finish(z_index, core_index, lowered_parts, stream, received, order)
    pieces = [shares[0]] + [along_z(shares[hop], hop) for hop in range(1, z_count)]
    return place(z_index, core_index, pieces, micro).reshape(micro, 1, model_width)


def solution(mesh):
    sizes = dict(mesh.shape)
    attn_count, ffn_count, rep_count = sizes["attn"], sizes["ffn"], sizes["rep"]
    side = int(round(ffn_count**0.5))
    fine = Mesh(
        mesh.devices.reshape(attn_count // 2, 2, side, ffn_count // side, rep_count),
        (Z, CORE, "x", "y", REP),
    )
    owners = (REP, Z, CORE, "x", "y")
    return jax.shard_map(
        per_device,
        mesh=fine,
        in_specs=(
            P(None, REP, ATTN),
            P(None, owners, None),
            P(owners, None, None),
            P(owners, None, None),
            P(None, owners),
            P(None, owners),
            P(FFN, ATTN),
            P(ATTN),
            P(ATTN, FFN),
            P(ATTN, FFN),
            P(FFN, ATTN),
        ),
        out_specs=P(None, owners, None),
        check_vma=False,
    )
```

```python
import functools

import jax
import jax.numpy as jnp
from jax import lax
from jax.experimental import pallas as pl
from jax.experimental.pallas import tpu as pltpu
from jax.sharding import Mesh, PartitionSpec as P

EPSILON = 1e-06
MASKED = -1e30
Z = "z"
CORE = "core"
ATTN = (Z, CORE)
FFN = ("x", "y")
REP = "rep"
LANES = 128
SQ_ROWS = 16
FEW = 16
BF16 = jnp.bfloat16
F32 = jnp.float32
HEAVY = pl.CostEstimate(flops=10**10, bytes_accessed=10**7, transcendentals=0)


def whole():
    return pl.BlockSpec(memory_space=pltpu.VMEM)


def scalars():
    return pl.BlockSpec(memory_space=pltpu.SMEM)


def in_hbm():
    return pl.BlockSpec(memory_space=pltpu.HBM)


def params(mib):
    return pltpu.CompilerParams(vmem_limit_bytes=mib * 1024 * 1024)


def one_hot(shape, source_of_row):
    rows = lax.broadcasted_iota(jnp.int32, (shape[0], 1), 0)
    cols = lax.broadcasted_iota(jnp.int32, shape, 1)
    return jnp.where(cols == source_of_row(rows), 1.0, 0.0)


def attention_kernel(
    slot_hbm,
    length_hbm,
    query_hbm,
    key_hbm,
    value_hbm,
    out_ref,
    slots,
    lengths,
    queries,
    keys,
    values,
    wide,
    small_sem,
    key_sem,
    value_sem,
):
    slot_count, pos, head_dim = keys.shape
    micro, width = queries.shape
    heads = width // head_dim
    copies, blocks, _, tile_rows, _ = out_ref.shape
    small = [
        pltpu.make_async_copy(source, target, small_sem.at[i])
        for i, (source, target) in enumerate(((query_hbm, queries), (slot_hbm, slots), (length_hbm, lengths)))
    ]
    key_copies = [pltpu.make_async_copy(key_hbm.at[s], keys.at[s], key_sem.at[s]) for s in range(slot_count)]
    value_copies = [pltpu.make_async_copy(value_hbm.at[s], values.at[s], value_sem.at[s]) for s in range(slot_count)]
    for copy in small + key_copies + value_copies:
        copy.start()
    for copy in small:
        copy.wait()
    for h in range(heads):
        wide[:, h, :] = queries[:, h * head_dim : (h + 1) * head_dim].astype(F32)
    pieces = head_dim // LANES
    group = heads // blocks
    positions = lax.broadcasted_iota(jnp.int32, (heads, pos), 1)
    requests = []
    scores = []
    for s in range(slot_count):
        request = micro - 1
        for m in range(micro - 1):
            request = jnp.where(slots[0, m] == s, m, request)
        requests.append(request)
        query = wide[request].astype(BF16)
        key_copies[s].wait()
        scores.append(lax.dot_general(query, keys[s], (((1,), (1,)), ((), ())), preferred_element_type=F32))
    softened = []
    totals = []
    for s in range(slot_count):
        in_cache = positions < lengths[0, requests[s]]
        masked = jnp.where(in_cache, scores[s] * head_dim ** (-0.5), MASKED)
        highest = jnp.max(masked, axis=1, keepdims=True)
        weights = jnp.where(in_cache, jnp.exp(masked - highest), 0.0)
        totals.append(jnp.sum(weights, axis=1, keepdims=True))
        softened.append(weights.astype(BF16))
    for copy in value_copies:
        copy.wait()
    for s in range(slot_count):
        weighted = jnp.dot(softened[s], values[s], preferred_element_type=F32)
        attended = weighted / totals[s]
        for piece in range(pieces):
            part = attended[:, piece * LANES : (piece + 1) * LANES].reshape(blocks, group, LANES).astype(BF16)
            for copy in range(copies):
                out_ref[copy, :, requests[s], piece * group : (piece + 1) * group, :] = part


def attend(queries, key_cache, value_cache, slots, lengths, z_count, ffn_count):
    slot_count, pos, head_dim = key_cache.shape
    micro, width = queries.shape
    tile_rows = width // ffn_count // LANES
    return pl.pallas_call(
        attention_kernel,
        in_specs=[in_hbm()] * 5,
        out_specs=whole(),
        out_shape=jax.ShapeDtypeStruct((z_count, ffn_count, micro, tile_rows, LANES), BF16),
        scratch_shapes=[
            pltpu.SMEM(slots.shape, jnp.int32),
            pltpu.SMEM(lengths.shape, jnp.int32),
            pltpu.VMEM(queries.shape, BF16),
            pltpu.VMEM((slot_count, pos, head_dim), BF16),
            pltpu.VMEM((slot_count, pos, head_dim), BF16),
            pltpu.VMEM((micro, width // head_dim, head_dim), F32),
            pltpu.SemaphoreType.DMA((3,)),
            pltpu.SemaphoreType.DMA((slot_count,)),
            pltpu.SemaphoreType.DMA((slot_count,)),
        ],
        compiler_params=params(60),
        name="attention",
    )(slots, lengths, queries, key_cache, value_cache)


def rows_kernel(pieces, in_ref, out_ref, wide):
    rows, tile_rows, lanes = in_ref.shape
    wide[...] = in_ref[...].astype(F32).reshape(rows * tile_rows, lanes)
    group = tile_rows // pieces
    for j in range(tile_rows):
        at = (j % pieces) * group + j // pieces
        out_ref[:, j * lanes : (j + 1) * lanes] = wide[pl.ds(at, rows, stride=tile_rows), :].astype(BF16)


def to_rows(tiles, pieces):
    rows, tile_rows, lanes = tiles.shape
    return pl.pallas_call(
        functools.partial(rows_kernel, pieces),
        out_shape=jax.ShapeDtypeStruct((rows, tile_rows * lanes), BF16),
        in_specs=[whole()],
        out_specs=whole(),
        scratch_shapes=[pltpu.VMEM((rows * tile_rows, lanes), F32)],
        compiler_params=params(8),
        name="to_rows",
    )(tiles)


def mixed_rows(order, core, rows_ref, weight_ref):
    z_count, core_count, ffn_count, micro = order
    product = jnp.dot(rows_ref[...], weight_ref[...], preferred_element_type=F32).astype(BF16)

    def source(r):
        m = r % micro
        c = (r // micro) % core_count
        z = (r // (micro * core_count)) % z_count
        f = r // (micro * core_count * z_count)
        return jnp.where(c == core, (z * ffn_count + f) * micro + m, -1)

    spread = one_hot((core_count * product.shape[0], product.shape[0]), source).astype(BF16)
    return jnp.dot(spread, product, preferred_element_type=F32)


def product_kernel(order, core_ref, rows_ref, weight_ref, out_ref):
    out_ref[...] = mixed_rows(order, core_ref[0], rows_ref, weight_ref).astype(BF16)


def product_of(core, rows, weight, order):
    return pl.pallas_call(
        functools.partial(product_kernel, order),
        out_shape=jax.ShapeDtypeStruct((2 * rows.shape[0], weight.shape[1]), BF16),
        in_specs=[scalars(), whole(), whole()],
        out_specs=whole(),
        compiler_params=params(12),
        cost_estimate=HEAVY,
        name="product",
    )(core, rows, weight)


def mix_kernel(order, core_ref, own_ref, rows_ref, weight_ref, out_ref):
    other = mixed_rows(order, 1 - core_ref[0], rows_ref, weight_ref)
    out_ref[...] = (own_ref[...].astype(F32) + other).astype(BF16)


def mix(core, own, rows, weight, order):
    return pl.pallas_call(
        functools.partial(mix_kernel, order),
        out_shape=jax.ShapeDtypeStruct(own.shape, BF16),
        in_specs=[scalars(), whole(), whole(), whole()],
        out_specs=whole(),
        compiler_params=params(12),
        name="mix",
    )(core, own, rows, weight)


def placed_rows(order, me, hops, rows, own_ref, other_ref):
    z_count, _, ffn_count, micro = order
    count = rows.shape[0]
    shares = [
        jnp.dot(rows, ref[...], preferred_element_type=F32).astype(BF16) for ref in (own_ref, other_ref)
    ]

    def source(r):
        m = r % micro
        hop = ((r // micro) % z_count) ^ me
        share = (r // (micro * z_count)) % 2
        f = r // (micro * z_count * 2)
        at = share * count + ((hop - hops[0]) * ffn_count + f) * micro + m
        return jnp.where(jnp.logical_and(hop >= hops[0], hop <= hops[-1]), at, -1)

    spread = one_hot((2 * z_count * ffn_count * micro, 2 * count), source).astype(BF16)
    return jnp.dot(spread, jnp.concatenate(shares, axis=0), preferred_element_type=F32)


def down_most_kernel(order, z_ref, *refs):
    *piece_refs, own_ref, other_ref, out_ref = refs
    rows = jnp.concatenate([ref[...] for ref in piece_refs], axis=0)
    hops = range(len(piece_refs))
    out_ref[...] = placed_rows(order, z_ref[0], hops, rows, own_ref, other_ref).astype(BF16)


def down_most(z, pieces, own_weight, other_weight, order):
    z_count, _, ffn_count, micro = order
    return pl.pallas_call(
        functools.partial(down_most_kernel, order),
        out_shape=jax.ShapeDtypeStruct((2 * z_count * ffn_count * micro, own_weight.shape[1]), BF16),
        in_specs=[scalars()] + [whole()] * (len(pieces) + 2),
        out_specs=whole(),
        compiler_params=params(16),
        cost_estimate=HEAVY,
        name="down_most",
    )(z, *pieces, own_weight, other_weight)


def down_kernel(order, z_ref, most_ref, rows_ref, own_ref, other_ref, out_ref):
    last = placed_rows(order, z_ref[0], (order[0] - 1,), rows_ref[...], own_ref, other_ref)
    out_ref[...] = (most_ref[...].astype(F32) + last).astype(BF16)


def down(z, most, last, own_weight, other_weight, order):
    return pl.pallas_call(
        functools.partial(down_kernel, order),
        out_shape=jax.ShapeDtypeStruct(most.shape, BF16),
        in_specs=[scalars()] + [whole()] * 4,
        out_specs=whole(),
        compiler_params=params(16),
        name="down",
    )(z, most, last, own_weight, other_weight)


def fetch_kernel(cuts, *refs):
    count = (len(refs) - 1) // 2
    sources, targets, sems = refs[:count], refs[count : 2 * count], refs[2 * count]
    copies = []
    for i in range(count):
        rows = sources[i].shape[0] // cuts
        for j in range(cuts):
            part = pl.ds(j * rows, rows)
            copies.append(pltpu.make_async_copy(sources[i].at[part], targets[i].at[part], sems.at[i * cuts + j]))
    for copy in copies:
        copy.start()
    for copy in copies:
        copy.wait()


def fetch(*arrays):
    cuts = 4
    return pl.pallas_call(
        functools.partial(fetch_kernel, cuts),
        out_shape=[jax.ShapeDtypeStruct(array.shape, array.dtype) for array in arrays],
        in_specs=[in_hbm()] * len(arrays),
        out_specs=[whole()] * len(arrays),
        scratch_shapes=[pltpu.SemaphoreType.DMA((len(arrays) * cuts,))],
        compiler_params=params(16),
        cost_estimate=HEAVY,
        name="fetch",
    )(*arrays)


def sum_parts(parts_ref):
    total = parts_ref[0].astype(F32)
    for j in range(1, parts_ref.shape[0]):
        total = total + parts_ref[j].astype(F32)
    return total


def stream_kernel(order, f_ref, core_ref, parts_ref, hidden_ref, stream_ref, send_ref, copies_ref):
    z_count, core_count, ffn_count, micro = order
    rows = stream_ref.shape[0]
    f = f_ref[0]

    def source(r):
        return ((r % micro) * z_count * core_count + r // micro) * ffn_count + f

    spread = one_hot((rows, hidden_ref.shape[0]), source).astype(BF16)
    hidden = jnp.dot(spread, hidden_ref[...], preferred_element_type=F32)
    stream = (hidden + sum_parts(parts_ref)).astype(BF16)
    stream_ref[...] = stream
    for j in range(copies_ref.shape[0]):
        copies_ref[j] = stream

    def other(r):
        row = ((r // micro) * core_count + 1 - core_ref[0]) * micro + r % micro
        return jnp.where(r < z_count * micro, row, -1)

    pick = one_hot((FEW, rows), other).astype(BF16)
    send_ref[...] = jnp.dot(pick, stream, preferred_element_type=F32).astype(BF16)


def make_stream(f, core, parts, hidden, order):
    _, rows, width = parts.shape
    return pl.pallas_call(
        functools.partial(stream_kernel, order),
        out_shape=(
            jax.ShapeDtypeStruct((rows, width), BF16),
            jax.ShapeDtypeStruct((FEW, width), BF16),
            jax.ShapeDtypeStruct(parts.shape, BF16),
        ),
        in_specs=[scalars()] * 2 + [whole()] * 2,
        out_specs=(whole(), whole(), whole()),
        compiler_params=params(8),
        name="make_stream",
    )(f, core, parts, hidden)


def squares_rows(row_values, width):
    high = row_values.astype(BF16).astype(F32)
    low = row_values - high
    index = lax.broadcasted_iota(jnp.int32, (SQ_ROWS, width), 0)
    return jnp.where(index == 0, high, jnp.where(index == 1, low, 0.0)).astype(BF16)


def up_kernel(order, hops, z_ref, core_ref, stream_ref, gain_ref, gate_ref, up_ref, *out_refs):
    z_count, core_count, ffn_count, micro = order
    tiles = gate_ref.shape[1] // LANES
    rows = ffn_count * micro
    me = z_ref[0]
    core = core_ref[0]

    def source(r):
        m = r % micro
        f = (r // micro) % ffn_count
        block = r // rows
        side = block // len(hops)
        hop = hops[0] + (hops[1] - hops[0]) * (block % len(hops))
        return ((f * z_count + (me ^ hop)) * core_count + (core ^ side)) * micro + m

    spread = one_hot((len(out_refs) * rows, stream_ref.shape[0]), source).astype(BF16)
    stream = jnp.dot(spread, stream_ref[...], preferred_element_type=F32)
    scaled = (stream * gain_ref[...].astype(F32)).astype(BF16)
    squares = jnp.sum(stream * stream, axis=1, keepdims=True)
    lane = one_hot((rows, LANES), lambda r: r)
    for i, out_ref in enumerate(out_refs):
        sums = jnp.sum(lane * squares[i * rows : (i + 1) * rows], axis=0, keepdims=True)
        out_ref[2 * tiles * rows :, :] = squares_rows(sums, LANES)
    for half, weight_ref in enumerate((gate_ref, up_ref)):
        product = jnp.dot(scaled, weight_ref[...], preferred_element_type=F32).astype(BF16)
        for i, out_ref in enumerate(out_refs):
            for j in range(tiles):
                at = (half * tiles + j) * rows
                out_ref[at : at + rows, :] = product[i * rows : (i + 1) * rows, j * LANES : (j + 1) * LANES]


def up_part(order, hops, z, core, stream_all, gain, gate_weight, up_weight):
    _, _, ffn_count, micro = order
    out_rows = 2 * gate_weight.shape[1] // LANES * ffn_count * micro + SQ_ROWS
    shape = jax.ShapeDtypeStruct((out_rows, LANES), BF16)
    return pl.pallas_call(
        functools.partial(up_kernel, order, hops),
        out_shape=[shape] * (2 * len(hops)),
        in_specs=[scalars(), scalars(), whole(), whole(), whole(), whole()],
        out_specs=[whole()] * (2 * len(hops)),
        compiler_params=params(16),
        cost_estimate=HEAVY,
        name="up_part",
    )(z, core, stream_all, gain, gate_weight, up_weight)


def sum_blocks(refs, start, stop):
    total = refs[0][start:stop, :].astype(F32)
    for ref in refs[1:]:
        total = total + ref[start:stop, :].astype(F32)
    return total


def add_kernel(*refs):
    *block_refs, out_ref = refs
    out_rows, lanes = out_ref.shape
    body = out_rows - SQ_ROWS
    out_ref[:body, :] = sum_blocks(block_refs, 0, body).astype(BF16)
    tail = sum_blocks(block_refs, body, out_rows)
    out_ref[body:, :] = squares_rows(tail[0:1] + tail[1:2], lanes)


def add(*blocks):
    return pl.pallas_call(
        add_kernel,
        out_shape=jax.ShapeDtypeStruct(blocks[0].shape, BF16),
        in_specs=[whole()] * len(blocks),
        out_specs=whole(),
        compiler_params=params(8),
        name="add",
    )(*blocks)


def activate_kernel(model_width, *refs):
    *block_refs, out_ref = refs
    out_rows, lanes = block_refs[0].shape
    rows, hidden = out_ref.shape
    tiles = hidden // lanes
    tail = sum_blocks(block_refs, out_rows - SQ_ROWS, out_rows)
    lane_sums = tail[0:1] + tail[1:2]
    spread = one_hot((rows, lanes), lambda r: r)
    squares = jnp.sum(spread * lane_sums, axis=1, keepdims=True)
    scale = lax.rsqrt(squares / model_width + EPSILON)
    for j in range(tiles):
        gate = sum_blocks(block_refs, j * rows, (j + 1) * rows) * scale
        upward = sum_blocks(block_refs, (tiles + j) * rows, (tiles + j + 1) * rows) * scale
        out_ref[:, j * lanes : (j + 1) * lanes] = (gate / (1.0 + jnp.exp(-gate)) * upward).astype(BF16)


def activate(blocks, rows, hidden, model_width):
    return pl.pallas_call(
        functools.partial(activate_kernel, model_width),
        out_shape=jax.ShapeDtypeStruct((rows, hidden), BF16),
        in_specs=[whole()] * len(blocks),
        out_specs=whole(),
        compiler_params=params(8),
        name="activate",
    )(*blocks)


def finish_kernel(order, z_ref, core_ref, parts_ref, stream_ref, received_ref, *out_refs):
    z_count, core_count, _, micro = order
    rows = stream_ref.shape[0]
    half = rows // 2

    def own(r):
        return jnp.where(r < half, ((r // micro) * core_count + core_ref[0]) * micro + r % micro, -1)

    first = one_hot((rows, rows), own).astype(BF16)
    second = one_hot((rows, FEW), lambda r: r - half).astype(BF16)
    stream = jnp.dot(first, stream_ref[...], preferred_element_type=F32)
    stream = stream + jnp.dot(second, received_ref[...], preferred_element_type=F32)
    finished = (stream + sum_parts(parts_ref)).astype(BF16)
    slots = out_refs[0].shape[0]
    me = z_ref[0]

    def source(r):
        q = r % slots
        at = (q // micro) * half + ((r // slots) ^ me) * micro + q % micro
        return jnp.where(q < 2 * micro, at, -1)

    spread = one_hot((len(out_refs) * slots, rows), source).astype(BF16)
    blocks = jnp.dot(spread, finished, preferred_element_type=F32)
    for k, out_ref in enumerate(out_refs):
        out_ref[...] = blocks[k * slots : (k + 1) * slots].astype(BF16)


def finish(z, core, parts, stream, received, order):
    z_count, _, _, micro = order
    slots = -(-2 * micro // 8) * 8
    return pl.pallas_call(
        functools.partial(finish_kernel, order),
        out_shape=[jax.ShapeDtypeStruct((slots, stream.shape[1]), BF16)] * z_count,
        in_specs=[scalars()] * 2 + [whole()] * 3,
        out_specs=[whole()] * z_count,
        compiler_params=params(8),
        name="finish",
    )(z, core, parts, stream, received)


def place_kernel(z_ref, core_ref, *refs):
    *piece_refs, out_ref = refs
    width = piece_refs[0].shape[1]
    micro = out_ref.shape[0]
    for k, ref in enumerate(piece_refs):
        block = ref[...].astype(F32)
        for side in range(2):
            share = 2 * (z_ref[0] ^ k) + (core_ref[0] ^ side)
            at = pl.multiple_of(share * width, LANES)
            out_ref[:, pl.ds(at, width)] = block[side * micro : (side + 1) * micro].astype(BF16)


def place(z, core, pieces, micro):
    width = pieces[0].shape[1]
    return pl.pallas_call(
        place_kernel,
        out_shape=jax.ShapeDtypeStruct((micro, 2 * len(pieces) * width), BF16),
        in_specs=[scalars(), scalars()] + [whole()] * len(pieces),
        out_specs=whole(),
        compiler_params=params(8),
        name="place",
    )(z, core, *pieces)


def along_z(array, hop):
    return lax.ppermute(array, Z, [(i, i ^ hop) for i in range(lax.axis_size(Z))])


def swap_cores(array):
    return lax.ppermute(array, CORE, [(0, 1), (1, 0)])


def per_device(
    hidden_in,
    queries,
    key_cache,
    value_cache,
    lengths,
    cache_slot,
    out_weight,
    ffn_gain,
    gate_weight,
    up_weight,
    down_weight,
):
    z_count = lax.axis_size(Z)
    core_count = lax.axis_size(CORE)
    attn_count = z_count * core_count
    ffn_count = lax.axis_size("x") * lax.axis_size("y")
    f_index = lax.axis_index(FFN).astype(jnp.int32)[None]
    z_index = lax.axis_index(Z).astype(jnp.int32)[None]
    core_index = lax.axis_index(CORE).astype(jnp.int32)[None]
    micro, total_rows, col_share = hidden_in.shape
    head_dim = key_cache.shape[2]
    model_width = col_share * attn_count
    hidden_share = gate_weight.shape[1]
    rows_chunk = attn_count * micro
    rows_all = ffn_count * rows_chunk
    rows_block = rows_all // attn_count

    order = (z_count, core_count, ffn_count, micro)
    payload = attend(
        queries.reshape(micro, -1), key_cache, value_cache, cache_slot.T, lengths.T, z_count, ffn_count
    )
    tile_rows = payload.shape[3]
    payload, f_index, z_index, core_index = lax.optimization_barrier((payload, f_index, z_index, core_index))
    payload = payload.reshape(z_count * ffn_count, micro * tile_rows, LANES)
    incoming = lax.all_to_all(payload, (Z,) + FFN, split_axis=0, concat_axis=0, tiled=True)
    own_rows = to_rows(incoming.reshape(z_count * ffn_count * micro, tile_rows, LANES), head_dim // LANES)
    own_rows, ffn_gain = lax.optimization_barrier((own_rows, ffn_gain))
    other_rows = swap_cores(own_rows)
    gain = ffn_gain[None, :]
    own_mixed = product_of(core_index, own_rows, out_weight, order)
    own_mixed, other_rows, gain = lax.optimization_barrier((own_mixed, other_rows, gain))
    mixed = mix(core_index, own_mixed, other_rows, out_weight, order)

    parts = lax.all_to_all(
        mixed.reshape(ffn_count, rows_chunk, col_share), FFN, split_axis=0, concat_axis=0, tiled=True
    )
    stream, send, copies = make_stream(f_index, core_index, parts, hidden_in.reshape(rows_all, col_share), order)
    stream_all = lax.all_to_all(copies, FFN, split_axis=0, concat_axis=0, tiled=True)
    stream_all = stream_all.reshape(rows_all, col_share)

    up_args = (z_index, core_index, stream_all, gain, gate_weight, up_weight)
    own3, own1, other3, other1 = up_part(order, (3, 1), *up_args)
    own0, own2, other0, other2 = up_part(order, (0, 2), *up_args)
    own3, send = lax.optimization_barrier((own3, send))
    received3, received1, own0, received = lax.optimization_barrier(
        (swap_cores(other3), swap_cores(other1), own0, swap_cores(send))
    )
    relayed3 = add(own3, received3)
    near1 = add(own1, received1)
    relayed3, other0, other2 = lax.optimization_barrier((relayed3, other0, other2))
    crossing = along_z(relayed3, 1)
    relayed = add(own2, swap_cores(other2), crossing)
    from_far = along_z(relayed, 2)
    from_near = along_z(near1, 1)
    down_weight, near1 = lax.optimization_barrier((down_weight, near1))
    down_own, down_other = fetch(down_weight, swap_cores(down_weight))
    from_far, down_own, down_other = lax.optimization_barrier((from_far, down_own, down_other))
    activated = activate((own0, swap_cores(other0), from_near, from_far), rows_block, hidden_share, model_width)

    far = along_z(activated, 2)
    near = along_z(activated, 1)
    most = down_most(z_index, (activated, near, far), down_own, down_other, order)
    lowered = down(z_index, most, along_z(far, 1), down_own, down_other, order)
    lowered_parts = lax.all_to_all(
        lowered.reshape(ffn_count, rows_chunk, col_share), FFN, split_axis=0, concat_axis=0, tiled=True
    )
    shares = finish(z_index, core_index, lowered_parts, stream, received, order)
    pieces = [shares[0]] + [along_z(shares[hop], hop) for hop in range(1, z_count)]
    return place(z_index, core_index, pieces, micro).reshape(micro, 1, model_width)


def solution(mesh):
    sizes = dict(mesh.shape)
    attn_count, ffn_count, rep_count = sizes["attn"], sizes["ffn"], sizes["rep"]
    side = int(round(ffn_count**0.5))
    fine = Mesh(
        mesh.devices.reshape(attn_count // 2, 2, side, ffn_count // side, rep_count),
        (Z, CORE, "x", "y", REP),
    )
    owners = (REP, Z, CORE, "x", "y")
    return jax.shard_map(
        per_device,
        mesh=fine,
        in_specs=(
            P(None, REP, ATTN),
            P(None, owners, None),
            P(owners, None, None),
            P(owners, None, None),
            P(None, owners),
            P(None, owners),
            P(FFN, ATTN),
            P(ATTN),
            P(ATTN, FFN),
            P(ATTN, FFN),
            P(FFN, ATTN),
        ),
        out_specs=P(None, owners, None),
        check_vma=False,
    )
```

```python
import functools

import jax
import jax.numpy as jnp
from jax import lax
from jax.experimental import pallas as pl
from jax.experimental.pallas import tpu as pltpu
from jax.sharding import Mesh, PartitionSpec as P

EPSILON = 1e-06
MASKED = -1e30
Z = "z"
CORE = "core"
ATTN = (Z, CORE)
FFN = ("x", "y")
REP = "rep"
LANES = 128
SQ_ROWS = 16
FEW = 16
BF16 = jnp.bfloat16
F32 = jnp.float32
HEAVY = pl.CostEstimate(flops=10**10, bytes_accessed=10**7, transcendentals=0)


def whole():
    return pl.BlockSpec(memory_space=pltpu.VMEM)


def scalars():
    return pl.BlockSpec(memory_space=pltpu.SMEM)


def in_hbm():
    return pl.BlockSpec(memory_space=pltpu.HBM)


def params(mib):
    return pltpu.CompilerParams(vmem_limit_bytes=mib * 1024 * 1024)


def one_hot(shape, source_of_row):
    rows = lax.broadcasted_iota(jnp.int32, (shape[0], 1), 0)
    cols = lax.broadcasted_iota(jnp.int32, shape, 1)
    return jnp.where(cols == source_of_row(rows), 1.0, 0.0)


def attention_kernel(
    slot_hbm,
    length_hbm,
    query_hbm,
    key_hbm,
    value_hbm,
    out_ref,
    slots,
    lengths,
    queries,
    keys,
    values,
    wide,
    small_sem,
    key_sem,
    value_sem,
):
    slot_count, pos, head_dim = keys.shape
    micro, width = queries.shape
    heads = width // head_dim
    copies, blocks, _, tile_rows, _ = out_ref.shape
    small = [
        pltpu.make_async_copy(source, target, small_sem.at[i])
        for i, (source, target) in enumerate(((query_hbm, queries), (slot_hbm, slots), (length_hbm, lengths)))
    ]
    key_copies = [pltpu.make_async_copy(key_hbm.at[s], keys.at[s], key_sem.at[s]) for s in range(slot_count)]
    value_copies = [pltpu.make_async_copy(value_hbm.at[s], values.at[s], value_sem.at[s]) for s in range(slot_count)]
    for copy in small + key_copies + value_copies:
        copy.start()
    for copy in small:
        copy.wait()
    for h in range(heads):
        wide[:, h, :] = queries[:, h * head_dim : (h + 1) * head_dim].astype(F32)
    pieces = head_dim // LANES
    group = heads // blocks
    positions = lax.broadcasted_iota(jnp.int32, (heads, pos), 1)
    requests = []
    scores = []
    for s in range(slot_count):
        request = micro - 1
        for m in range(micro - 1):
            request = jnp.where(slots[0, m] == s, m, request)
        requests.append(request)
        query = wide[request].astype(BF16)
        key_copies[s].wait()
        scores.append(lax.dot_general(query, keys[s], (((1,), (1,)), ((), ())), preferred_element_type=F32))
    softened = []
    totals = []
    for s in range(slot_count):
        in_cache = positions < lengths[0, requests[s]]
        masked = jnp.where(in_cache, scores[s] * head_dim ** (-0.5), MASKED)
        highest = jnp.max(masked, axis=1, keepdims=True)
        weights = jnp.where(in_cache, jnp.exp(masked - highest), 0.0)
        totals.append(jnp.sum(weights, axis=1, keepdims=True))
        softened.append(weights.astype(BF16))
    for copy in value_copies:
        copy.wait()
    for s in range(slot_count):
        weighted = jnp.dot(softened[s], values[s], preferred_element_type=F32)
        attended = weighted / totals[s]
        for piece in range(pieces):
            part = attended[:, piece * LANES : (piece + 1) * LANES].reshape(blocks, group, LANES).astype(BF16)
            for copy in range(copies):
                out_ref[copy, :, requests[s], piece * group : (piece + 1) * group, :] = part


def attend(queries, key_cache, value_cache, slots, lengths, z_count, ffn_count):
    slot_count, pos, head_dim = key_cache.shape
    micro, width = queries.shape
    tile_rows = width // ffn_count // LANES
    return pl.pallas_call(
        attention_kernel,
        in_specs=[in_hbm()] * 5,
        out_specs=whole(),
        out_shape=jax.ShapeDtypeStruct((z_count, ffn_count, micro, tile_rows, LANES), BF16),
        scratch_shapes=[
            pltpu.SMEM(slots.shape, jnp.int32),
            pltpu.SMEM(lengths.shape, jnp.int32),
            pltpu.VMEM(queries.shape, BF16),
            pltpu.VMEM((slot_count, pos, head_dim), BF16),
            pltpu.VMEM((slot_count, pos, head_dim), BF16),
            pltpu.VMEM((micro, width // head_dim, head_dim), F32),
            pltpu.SemaphoreType.DMA((3,)),
            pltpu.SemaphoreType.DMA((slot_count,)),
            pltpu.SemaphoreType.DMA((slot_count,)),
        ],
        compiler_params=params(60),
        name="attention",
    )(slots, lengths, queries, key_cache, value_cache)


def rows_kernel(pieces, in_ref, out_ref, wide):
    rows, tile_rows, lanes = in_ref.shape
    wide[...] = in_ref[...].astype(F32).reshape(rows * tile_rows, lanes)
    group = tile_rows // pieces
    for j in range(tile_rows):
        at = (j % pieces) * group + j // pieces
        out_ref[:, j * lanes : (j + 1) * lanes] = wide[pl.ds(at, rows, stride=tile_rows), :].astype(BF16)


def to_rows(tiles, pieces):
    rows, tile_rows, lanes = tiles.shape
    return pl.pallas_call(
        functools.partial(rows_kernel, pieces),
        out_shape=jax.ShapeDtypeStruct((rows, tile_rows * lanes), BF16),
        in_specs=[whole()],
        out_specs=whole(),
        scratch_shapes=[pltpu.VMEM((rows * tile_rows, lanes), F32)],
        compiler_params=params(8),
        name="to_rows",
    )(tiles)


def mixed_rows(order, core, rows_ref, weight_ref):
    z_count, core_count, ffn_count, micro = order
    product = jnp.dot(rows_ref[...], weight_ref[...], preferred_element_type=F32).astype(BF16)

    def source(r):
        m = r % micro
        c = (r // micro) % core_count
        z = (r // (micro * core_count)) % z_count
        f = r // (micro * core_count * z_count)
        return jnp.where(c == core, (z * ffn_count + f) * micro + m, -1)

    spread = one_hot((core_count * product.shape[0], product.shape[0]), source).astype(BF16)
    return jnp.dot(spread, product, preferred_element_type=F32)


def product_kernel(order, core_ref, rows_ref, weight_ref, out_ref):
    out_ref[...] = mixed_rows(order, core_ref[0], rows_ref, weight_ref).astype(BF16)


def product_of(core, rows, weight, order):
    return pl.pallas_call(
        functools.partial(product_kernel, order),
        out_shape=jax.ShapeDtypeStruct((2 * rows.shape[0], weight.shape[1]), BF16),
        in_specs=[scalars(), whole(), whole()],
        out_specs=whole(),
        compiler_params=params(12),
        cost_estimate=HEAVY,
        name="product",
    )(core, rows, weight)


def mix_kernel(order, core_ref, own_ref, rows_ref, weight_ref, out_ref):
    other = mixed_rows(order, 1 - core_ref[0], rows_ref, weight_ref)
    out_ref[...] = (own_ref[...].astype(F32) + other).astype(BF16)


def mix(core, own, rows, weight, order):
    return pl.pallas_call(
        functools.partial(mix_kernel, order),
        out_shape=jax.ShapeDtypeStruct(own.shape, BF16),
        in_specs=[scalars(), whole(), whole(), whole()],
        out_specs=whole(),
        compiler_params=params(12),
        name="mix",
    )(core, own, rows, weight)


def placed_rows(order, me, hops, rows, own_ref, other_ref):
    z_count, _, ffn_count, micro = order
    count = rows.shape[0]
    shares = [
        jnp.dot(rows, ref[...], preferred_element_type=F32).astype(BF16) for ref in (own_ref, other_ref)
    ]

    def source(r):
        m = r % micro
        hop = ((r // micro) % z_count) ^ me
        share = (r // (micro * z_count)) % 2
        f = r // (micro * z_count * 2)
        at = share * count + ((hop - hops[0]) * ffn_count + f) * micro + m
        return jnp.where(jnp.logical_and(hop >= hops[0], hop <= hops[-1]), at, -1)

    spread = one_hot((2 * z_count * ffn_count * micro, 2 * count), source).astype(BF16)
    return jnp.dot(spread, jnp.concatenate(shares, axis=0), preferred_element_type=F32)


def down_most_kernel(order, z_ref, *refs):
    *piece_refs, own_ref, other_ref, out_ref = refs
    rows = jnp.concatenate([ref[...] for ref in piece_refs], axis=0)
    hops = range(len(piece_refs))
    out_ref[...] = placed_rows(order, z_ref[0], hops, rows, own_ref, other_ref).astype(BF16)


def down_most(z, pieces, own_weight, other_weight, order):
    z_count, _, ffn_count, micro = order
    return pl.pallas_call(
        functools.partial(down_most_kernel, order),
        out_shape=jax.ShapeDtypeStruct((2 * z_count * ffn_count * micro, own_weight.shape[1]), BF16),
        in_specs=[scalars()] + [whole()] * (len(pieces) + 2),
        out_specs=whole(),
        compiler_params=params(16),
        cost_estimate=HEAVY,
        name="down_most",
    )(z, *pieces, own_weight, other_weight)


def down_kernel(order, z_ref, most_ref, rows_ref, own_ref, other_ref, out_ref):
    last = placed_rows(order, z_ref[0], (order[0] - 1,), rows_ref[...], own_ref, other_ref)
    out_ref[...] = (most_ref[...].astype(F32) + last).astype(BF16)


def down(z, most, last, own_weight, other_weight, order):
    return pl.pallas_call(
        functools.partial(down_kernel, order),
        out_shape=jax.ShapeDtypeStruct(most.shape, BF16),
        in_specs=[scalars()] + [whole()] * 4,
        out_specs=whole(),
        compiler_params=params(16),
        name="down",
    )(z, most, last, own_weight, other_weight)


def fetch_kernel(cuts, *refs):
    count = (len(refs) - 1) // 2
    sources, targets, sems = refs[:count], refs[count : 2 * count], refs[2 * count]
    copies = []
    for i in range(count):
        rows = sources[i].shape[0] // cuts
        for j in range(cuts):
            part = pl.ds(j * rows, rows)
            copies.append(pltpu.make_async_copy(sources[i].at[part], targets[i].at[part], sems.at[i * cuts + j]))
    for copy in copies:
        copy.start()
    for copy in copies:
        copy.wait()


def fetch(*arrays):
    cuts = 4
    return pl.pallas_call(
        functools.partial(fetch_kernel, cuts),
        out_shape=[jax.ShapeDtypeStruct(array.shape, array.dtype) for array in arrays],
        in_specs=[in_hbm()] * len(arrays),
        out_specs=[whole()] * len(arrays),
        scratch_shapes=[pltpu.SemaphoreType.DMA((len(arrays) * cuts,))],
        compiler_params=params(16),
        cost_estimate=HEAVY,
        name="fetch",
    )(*arrays)


def sum_parts(parts_ref):
    total = parts_ref[0].astype(F32)
    for j in range(1, parts_ref.shape[0]):
        total = total + parts_ref[j].astype(F32)
    return total


def stream_kernel(order, f_ref, core_ref, parts_ref, hidden_ref, stream_ref, send_ref, copies_ref):
    z_count, core_count, ffn_count, micro = order
    rows = stream_ref.shape[0]
    f = f_ref[0]

    def source(r):
        return ((r % micro) * z_count * core_count + r // micro) * ffn_count + f

    spread = one_hot((rows, hidden_ref.shape[0]), source).astype(BF16)
    hidden = jnp.dot(spread, hidden_ref[...], preferred_element_type=F32)
    stream = (hidden + sum_parts(parts_ref)).astype(BF16)
    stream_ref[...] = stream
    for j in range(copies_ref.shape[0]):
        copies_ref[j] = stream

    def other(r):
        row = ((r // micro) * core_count + 1 - core_ref[0]) * micro + r % micro
        return jnp.where(r < z_count * micro, row, -1)

    pick = one_hot((FEW, rows), other).astype(BF16)
    send_ref[...] = jnp.dot(pick, stream, preferred_element_type=F32).astype(BF16)


def make_stream(f, core, parts, hidden, order):
    _, rows, width = parts.shape
    return pl.pallas_call(
        functools.partial(stream_kernel, order),
        out_shape=(
            jax.ShapeDtypeStruct((rows, width), BF16),
            jax.ShapeDtypeStruct((FEW, width), BF16),
            jax.ShapeDtypeStruct(parts.shape, BF16),
        ),
        in_specs=[scalars()] * 2 + [whole()] * 2,
        out_specs=(whole(), whole(), whole()),
        compiler_params=params(8),
        name="make_stream",
    )(f, core, parts, hidden)


def squares_rows(row_values, width):
    high = row_values.astype(BF16).astype(F32)
    low = row_values - high
    index = lax.broadcasted_iota(jnp.int32, (SQ_ROWS, width), 0)
    return jnp.where(index == 0, high, jnp.where(index == 1, low, 0.0)).astype(BF16)


def up_kernel(order, hops, z_ref, core_ref, stream_ref, gain_ref, gate_ref, up_ref, *out_refs):
    z_count, core_count, ffn_count, micro = order
    tiles = gate_ref.shape[1] // LANES
    rows = ffn_count * micro
    me = z_ref[0]
    core = core_ref[0]

    def source(r):
        m = r % micro
        f = (r // micro) % ffn_count
        block = r // rows
        side = block // len(hops)
        hop = hops[0] + (hops[1] - hops[0]) * (block % len(hops))
        return ((f * z_count + (me ^ hop)) * core_count + (core ^ side)) * micro + m

    spread = one_hot((len(out_refs) * rows, stream_ref.shape[0]), source).astype(BF16)
    stream = jnp.dot(spread, stream_ref[...], preferred_element_type=F32)
    scaled = (stream * gain_ref[...].astype(F32)).astype(BF16)
    squares = jnp.sum(stream * stream, axis=1, keepdims=True)
    lane = one_hot((rows, LANES), lambda r: r)
    for i, out_ref in enumerate(out_refs):
        sums = jnp.sum(lane * squares[i * rows : (i + 1) * rows], axis=0, keepdims=True)
        out_ref[2 * tiles * rows :, :] = squares_rows(sums, LANES)
    for half, weight_ref in enumerate((gate_ref, up_ref)):
        product = jnp.dot(scaled, weight_ref[...], preferred_element_type=F32).astype(BF16)
        for i, out_ref in enumerate(out_refs):
            for j in range(tiles):
                at = (half * tiles + j) * rows
                out_ref[at : at + rows, :] = product[i * rows : (i + 1) * rows, j * LANES : (j + 1) * LANES]


def up_part(order, hops, z, core, stream_all, gain, gate_weight, up_weight):
    _, _, ffn_count, micro = order
    out_rows = 2 * gate_weight.shape[1] // LANES * ffn_count * micro + SQ_ROWS
    shape = jax.ShapeDtypeStruct((out_rows, LANES), BF16)
    return pl.pallas_call(
        functools.partial(up_kernel, order, hops),
        out_shape=[shape] * (2 * len(hops)),
        in_specs=[scalars(), scalars(), whole(), whole(), whole(), whole()],
        out_specs=[whole()] * (2 * len(hops)),
        compiler_params=params(16),
        cost_estimate=HEAVY,
        name="up_part",
    )(z, core, stream_all, gain, gate_weight, up_weight)


def sum_blocks(refs, start, stop):
    total = refs[0][start:stop, :].astype(F32)
    for ref in refs[1:]:
        total = total + ref[start:stop, :].astype(F32)
    return total


def add_kernel(*refs):
    *block_refs, out_ref = refs
    out_rows, lanes = out_ref.shape
    body = out_rows - SQ_ROWS
    out_ref[:body, :] = sum_blocks(block_refs, 0, body).astype(BF16)
    tail = sum_blocks(block_refs, body, out_rows)
    out_ref[body:, :] = squares_rows(tail[0:1] + tail[1:2], lanes)


def add(*blocks):
    return pl.pallas_call(
        add_kernel,
        out_shape=jax.ShapeDtypeStruct(blocks[0].shape, BF16),
        in_specs=[whole()] * len(blocks),
        out_specs=whole(),
        compiler_params=params(8),
        name="add",
    )(*blocks)


def activate_kernel(model_width, *refs):
    *block_refs, out_ref = refs
    out_rows, lanes = block_refs[0].shape
    rows, hidden = out_ref.shape
    tiles = hidden // lanes
    tail = sum_blocks(block_refs, out_rows - SQ_ROWS, out_rows)
    lane_sums = tail[0:1] + tail[1:2]
    spread = one_hot((rows, lanes), lambda r: r)
    squares = jnp.sum(spread * lane_sums, axis=1, keepdims=True)
    scale = lax.rsqrt(squares / model_width + EPSILON)
    for j in range(tiles):
        gate = sum_blocks(block_refs, j * rows, (j + 1) * rows) * scale
        upward = sum_blocks(block_refs, (tiles + j) * rows, (tiles + j + 1) * rows) * scale
        out_ref[:, j * lanes : (j + 1) * lanes] = (gate / (1.0 + jnp.exp(-gate)) * upward).astype(BF16)


def activate(blocks, rows, hidden, model_width):
    return pl.pallas_call(
        functools.partial(activate_kernel, model_width),
        out_shape=jax.ShapeDtypeStruct((rows, hidden), BF16),
        in_specs=[whole()] * len(blocks),
        out_specs=whole(),
        compiler_params=params(8),
        name="activate",
    )(*blocks)


def finish_kernel(order, z_ref, core_ref, parts_ref, stream_ref, received_ref, *out_refs):
    z_count, core_count, _, micro = order
    rows = stream_ref.shape[0]
    half = rows // 2

    def own(r):
        return jnp.where(r < half, ((r // micro) * core_count + core_ref[0]) * micro + r % micro, -1)

    first = one_hot((rows, rows), own).astype(BF16)
    second = one_hot((rows, FEW), lambda r: r - half).astype(BF16)
    stream = jnp.dot(first, stream_ref[...], preferred_element_type=F32)
    stream = stream + jnp.dot(second, received_ref[...], preferred_element_type=F32)
    finished = (stream + sum_parts(parts_ref)).astype(BF16)
    slots = out_refs[0].shape[0]
    me = z_ref[0]

    def source(r):
        q = r % slots
        at = (q // micro) * half + ((r // slots) ^ me) * micro + q % micro
        return jnp.where(q < 2 * micro, at, -1)

    spread = one_hot((len(out_refs) * slots, rows), source).astype(BF16)
    blocks = jnp.dot(spread, finished, preferred_element_type=F32)
    for k, out_ref in enumerate(out_refs):
        out_ref[...] = blocks[k * slots : (k + 1) * slots].astype(BF16)


def finish(z, core, parts, stream, received, order):
    z_count, _, _, micro = order
    slots = -(-2 * micro // 8) * 8
    return pl.pallas_call(
        functools.partial(finish_kernel, order),
        out_shape=[jax.ShapeDtypeStruct((slots, stream.shape[1]), BF16)] * z_count,
        in_specs=[scalars()] * 2 + [whole()] * 3,
        out_specs=[whole()] * z_count,
        compiler_params=params(8),
        name="finish",
    )(z, core, parts, stream, received)


def place_kernel(z_ref, core_ref, *refs):
    *piece_refs, out_ref, gathered = refs
    width = piece_refs[0].shape[1]
    micro = out_ref.shape[0]
    for k, ref in enumerate(piece_refs):
        block = ref[...].astype(F32)
        for side in range(2):
            share = 2 * (z_ref[0] ^ k) + (core_ref[0] ^ side)
            at = pl.multiple_of(share * width, LANES)
            gathered[:micro, pl.ds(at, width)] = block[side * micro : (side + 1) * micro]
    out_ref[...] = gathered[:micro, :].astype(BF16)


def place(z, core, pieces, micro):
    width = pieces[0].shape[1]
    return pl.pallas_call(
        place_kernel,
        out_shape=jax.ShapeDtypeStruct((micro, 2 * len(pieces) * width), BF16),
        in_specs=[scalars(), scalars()] + [whole()] * len(pieces),
        out_specs=whole(),
        scratch_shapes=[pltpu.VMEM((8, 2 * len(pieces) * width), F32)],
        compiler_params=params(8),
        name="place",
    )(z, core, *pieces)


def along_z(array, hop):
    return lax.ppermute(array, Z, [(i, i ^ hop) for i in range(lax.axis_size(Z))])


def swap_cores(array):
    return lax.ppermute(array, CORE, [(0, 1), (1, 0)])


def per_device(
    hidden_in,
    queries,
    key_cache,
    value_cache,
    lengths,
    cache_slot,
    out_weight,
    ffn_gain,
    gate_weight,
    up_weight,
    down_weight,
):
    z_count = lax.axis_size(Z)
    core_count = lax.axis_size(CORE)
    attn_count = z_count * core_count
    ffn_count = lax.axis_size("x") * lax.axis_size("y")
    f_index = lax.axis_index(FFN).astype(jnp.int32)[None]
    z_index = lax.axis_index(Z).astype(jnp.int32)[None]
    core_index = lax.axis_index(CORE).astype(jnp.int32)[None]
    micro, total_rows, col_share = hidden_in.shape
    head_dim = key_cache.shape[2]
    model_width = col_share * attn_count
    hidden_share = gate_weight.shape[1]
    rows_chunk = attn_count * micro
    rows_all = ffn_count * rows_chunk
    rows_block = rows_all // attn_count

    order = (z_count, core_count, ffn_count, micro)
    payload = attend(
        queries.reshape(micro, -1), key_cache, value_cache, cache_slot.T, lengths.T, z_count, ffn_count
    )
    tile_rows = payload.shape[3]
    payload, f_index, z_index, core_index = lax.optimization_barrier((payload, f_index, z_index, core_index))
    payload = payload.reshape(z_count * ffn_count, micro * tile_rows, LANES)
    incoming = lax.all_to_all(payload, (Z,) + FFN, split_axis=0, concat_axis=0, tiled=True)
    own_rows = to_rows(incoming.reshape(z_count * ffn_count * micro, tile_rows, LANES), head_dim // LANES)
    own_rows, ffn_gain = lax.optimization_barrier((own_rows, ffn_gain))
    other_rows = swap_cores(own_rows)
    gain = ffn_gain[None, :]
    own_mixed = product_of(core_index, own_rows, out_weight, order)
    own_mixed, other_rows, gain = lax.optimization_barrier((own_mixed, other_rows, gain))
    mixed = mix(core_index, own_mixed, other_rows, out_weight, order)

    parts = lax.all_to_all(
        mixed.reshape(ffn_count, rows_chunk, col_share), FFN, split_axis=0, concat_axis=0, tiled=True
    )
    stream, send, copies = make_stream(f_index, core_index, parts, hidden_in.reshape(rows_all, col_share), order)
    stream_all = lax.all_to_all(copies, FFN, split_axis=0, concat_axis=0, tiled=True)
    stream_all = stream_all.reshape(rows_all, col_share)

    up_args = (z_index, core_index, stream_all, gain, gate_weight, up_weight)
    own3, own1, other3, other1 = up_part(order, (3, 1), *up_args)
    own0, own2, other0, other2 = up_part(order, (0, 2), *up_args)
    received3, received1, own0 = lax.optimization_barrier((swap_cores(other3), swap_cores(other1), own0))
    relayed3 = add(own3, received3)
    near1 = add(own1, received1)
    relayed3, other0, other2 = lax.optimization_barrier((relayed3, other0, other2))
    crossing = along_z(relayed3, 1)
    relayed = add(own2, swap_cores(other2), crossing)
    relayed, send = lax.optimization_barrier((relayed, send))
    from_far = along_z(relayed, 2)
    from_near = along_z(near1, 1)
    down_weight, near1 = lax.optimization_barrier((down_weight, near1))
    down_own, down_other = fetch(down_weight, swap_cores(down_weight))
    from_far, down_own, down_other = lax.optimization_barrier((from_far, down_own, down_other))
    activated = activate((own0, swap_cores(other0), from_near, from_far), rows_block, hidden_share, model_width)

    far = along_z(activated, 2)
    near = along_z(activated, 1)
    far, received = lax.optimization_barrier((far, swap_cores(send)))
    most = down_most(z_index, (activated, near, far), down_own, down_other, order)
    lowered = down(z_index, most, along_z(far, 1), down_own, down_other, order)
    lowered_parts = lax.all_to_all(
        lowered.reshape(ffn_count, rows_chunk, col_share), FFN, split_axis=0, concat_axis=0, tiled=True
    )
    shares = finish(z_index, core_index, lowered_parts, stream, received, order)
    pieces = [shares[0]] + [along_z(shares[hop], hop) for hop in range(1, z_count)]
    return place(z_index, core_index, pieces, micro).reshape(micro, 1, model_width)


def solution(mesh):
    sizes = dict(mesh.shape)
    attn_count, ffn_count, rep_count = sizes["attn"], sizes["ffn"], sizes["rep"]
    side = int(round(ffn_count**0.5))
    fine = Mesh(
        mesh.devices.reshape(attn_count // 2, 2, side, ffn_count // side, rep_count),
        (Z, CORE, "x", "y", REP),
    )
    owners = (REP, Z, CORE, "x", "y")
    return jax.shard_map(
        per_device,
        mesh=fine,
        in_specs=(
            P(None, REP, ATTN),
            P(None, owners, None),
            P(owners, None, None),
            P(owners, None, None),
            P(None, owners),
            P(None, owners),
            P(FFN, ATTN),
            P(ATTN),
            P(ATTN, FFN),
            P(ATTN, FFN),
            P(FFN, ATTN),
        ),
        out_specs=P(None, owners, None),
        check_vma=False,
    )
```
